32 devices in a mesh: fsdp: 8 (over z, x), tensor: 4 (over y, core).
Axes of the slice: x: 2, y: 2, z: 4, core: 2. Of those that a mesh axis runs over, the one named last changes fastest.
Arguments:
- layer_input: bfloat16 [7168, 1024], P(('fsdp', 'tensor')), may hold values from -6 to 6, as said below
- encoder_states: bfloat16 [16, 1500, 1024], P('fsdp'), may hold values from -6 to 6, as said below
- out_grad: bfloat16 [7168, 1024], P(('fsdp', 'tensor')), may hold values from -6 to 6
- self_qkv: bfloat16 [3, 1024, 1024], P(None, 'fsdp', 'tensor'), may hold values from -0.25 to 0.25
- self_bias: bfloat16 [2, 16, 64], P(None, 'tensor', 'fsdp'), may hold values from -3 to 3
- self_out: bfloat16 [1024, 1024], P('tensor', 'fsdp'), may hold values from -0.75 to 0.75
- cross_qkv: bfloat16 [3, 1024, 1024], P(None, 'fsdp', 'tensor'), may hold values from -0.25 to 0.25
- cross_bias: bfloat16 [2, 16, 64], P(None, 'tensor', 'fsdp'), may hold values from -3 to 3
- cross_out: bfloat16 [1024, 1024], P('tensor', 'fsdp'), may hold values from -0.75 to 0.75
- ff_in: bfloat16 [1024, 4096], P('fsdp', 'tensor'), may hold values from -0.1875 to 0.1875
- ff_bias: bfloat16 [64, 64], P('tensor', 'fsdp'), may hold values from -3 to 3
- ff_out: bfloat16 [4096, 1024], P('tensor', 'fsdp'), may hold values from -0.125 to 0.125
- norm_gains: bfloat16 [3, 1024], P(None, 'fsdp'), may hold values from 0.5 to 1.5
- shifts: bfloat16 [6, 1024], P(None, 'fsdp'), may hold values from -2 to 2
Outputs:
- layer_output: float32 [7168, 1024], P(('fsdp', 'tensor'))
- input_grad: float32 [7168, 1024], P(('fsdp', 'tensor'))
- encoder_grad: float32 [16, 1500, 1024], P('fsdp', None, 'tensor')
- self_qkv_grad: float32 [3, 1024, 1024], P(None, 'fsdp', 'tensor')
- self_bias_grad: float32 [2, 16, 64], P(None, 'tensor', 'fsdp')
- self_out_grad: float32 [1024, 1024], P('tensor', 'fsdp')
- cross_qkv_grad: float32 [3, 1024, 1024], P(None, 'fsdp', 'tensor')
- cross_bias_grad: float32 [2, 16, 64], P(None, 'tensor', 'fsdp')
- cross_out_grad: float32 [1024, 1024], P('tensor', 'fsdp')
- ff_in_grad: float32 [1024, 4096], P('fsdp', 'tensor')
- ff_bias_grad: float32 [64, 64], P('tensor', 'fsdp')
- ff_out_grad: float32 [4096, 1024], P('tensor', 'fsdp')
- norm_gains_grad: float32 [3, 1024], P(None, ('fsdp', 'tensor'))
- shifts_grad: float32 [6, 1024], P(None, ('fsdp', 'tensor'))
The draws below stay inside these ranges and needn't reach their ends.
Inputs may be any that keep to these rules, and one draw needn't show every extreme that they name: `layer_input`: entries independent, of mean 0 and variance about 1. `encoder_states`: entries independent, of mean 0 and variance about 1.
All inputs are finite; a program needn't handle non-finite values.
Results may differ from the reference program's by a relative error of at most 0.02.
Values may be sent and summed in bfloat16 or wider, within the bound.
No kernel may reach another device: no remote copies, remote signals or barrier semaphores. Data moves between devices by JAX's collectives and lax.ppermute only.
A program may use at most 192 MiB of HBM per device.

```python
import jax
import jax.numpy as jnp
from jax import lax

D = 1024
HEADS = 16
HD = 64
FF = 4096
LEN = 448
FRAMES = 1500
SEQS = 16
TOKENS = 7168


def drawn_entries(key, shape):
    values = jax.random.truncated_normal(key, -6.0, 6.0, shape, jnp.float32)
    return values


def draw_layer_input(key, part):
    key = jax.random.fold_in(key, 11)
    return drawn_entries(key, (TOKENS, D)).astype(jnp.bfloat16)


def draw_encoder_states(key, part):
    key = jax.random.fold_in(key, 23)
    return drawn_entries(key, (SEQS, FRAMES, D)).astype(jnp.bfloat16)


def raised(entries, stream_key, source, target, blocks, factor):
    def block_of(position):
        return (jnp.arange(entries.shape[position]) // (entries.shape[position] // blocks)).reshape((-1,) + (1,) * (entries.ndim - 1 - position))

    one_side = jax.random.permutation(stream_key, blocks)[block_of(target)]
    other_side = (block_of(target) + blocks // 2) % blocks
    return jnp.where((block_of(source) == one_side) | (block_of(source) == other_side), factor * entries, entries)


def steps_of(key, shape, split, low, largest):
    def one(position, blocks):
        heights = jax.random.uniform(jax.random.fold_in(jax.random.fold_in(key, 6), position), (blocks,), jnp.float32, low / len(split), largest / len(split))
        return jnp.repeat(jnp.exp(heights), shape[position] // blocks).reshape((-1,) + (1,) * (len(shape) - position - 1))

    gain = one(*split[0])
    for cut in split[1:]:
        gain = gain * one(*cut)
    return gain


def centred(key, shape, deviation, limit, pieces=(), held_as=jnp.bfloat16):
    gain = steps_of(key, shape, pieces, -0.22, 0.18) if pieces else 1.0
    entries = jax.random.normal(key, shape, jnp.float32) * deviation * gain
    return jnp.minimum(jnp.maximum(entries, -limit), limit).astype(held_as)


def gaussian_with(stream_key, extent, spread, bound, cuts, heavy, kind=jnp.bfloat16):
    values = spread * jax.random.normal(stream_key, extent, jnp.float32)
    if cuts:
        values = values * steps_of(stream_key, extent, cuts, -0.22, 0.18)
    return jnp.clip(raised(values, jax.random.fold_in(stream_key, 3), *heavy), -bound, bound).astype(kind)


def setup_inputs(seed: int = 0) -> dict:
    streams_of = jax.random.split(jax.random.key(seed), 15)
    return {
        "layer_input": draw_layer_input(jax.random.fold_in(streams_of[14], 71), 0),
        "encoder_states": draw_encoder_states(jax.random.fold_in(streams_of[14], 71), 0),
        "out_grad": gaussian_with(streams_of[2], (TOKENS, D), 1.0, 6.0, ((0, 32),), (0, 1, 32, 2.75)),
        "self_qkv": centred(streams_of[3], (3, D, D), (D // 2) ** -0.5, 0.25, ((1, 8), (2, 4))),
        "self_bias": centred(streams_of[4], (2, HEADS, HD), 0.5, 3.0, ((1, 4), (2, 8))),
        "self_out": centred(streams_of[5], (D, D), (D // 16) ** -0.5, 0.75, ((0, 4), (1, 8))),
        "cross_qkv": centred(streams_of[6], (3, D, D), (D // 2) ** -0.5, 0.25, ((1, 8), (2, 4))),
        "cross_bias": centred(streams_of[7], (2, HEADS, HD), 0.5, 3.0, ((1, 4), (2, 8))),
        "cross_out": centred(streams_of[8], (D, D), (D // 16) ** -0.5, 0.75, ((0, 4), (1, 8))),
        "ff_in": centred(streams_of[9], (D, FF), D ** -0.5, 0.1875, ((0, 8), (1, 4))),
        "ff_bias": centred(streams_of[10], (FF // HD, HD), 0.5, 3.0, ((0, 4), (1, 8))),
        "ff_out": centred(streams_of[11], (FF, D), (FF // 2) ** -0.5, 0.125, ((0, 4), (1, 8))),
        "norm_gains": jnp.clip(1.0 + 0.1 * jax.random.normal(streams_of[12], (3, D), jnp.float32), 0.5, 1.5).astype(jnp.bfloat16),
        "shifts": centred(streams_of[13], (6, D), 0.3, 2.0, ((1, 8),)),
    }


HIGHEST = lax.Precision.HIGHEST

@jax.custom_vjp
def low(v):
    return lax.optimization_barrier(v.astype(jnp.bfloat16)).astype(jnp.float32)

@jax.custom_vjp
def low_back(v):
    return v

def low_keep(v):
    return (low(v), None)

def low_pass(kept, grad):
    return (grad,)

def back_keep(v):
    return (v, None)

def back_low(kept, grad):
    return (low(grad),)
low.defvjp(low_keep, low_pass)
low_back.defvjp(back_keep, back_low)

def product(left, right):
    return jnp.dot(left, right, precision=HIGHEST)

def layer_norm(row_block, gain_row, shift_row):
    center = row_block - lax.optimization_barrier(jnp.mean(row_block, axis=-1, keepdims=True))
    inverse = lax.rsqrt(lax.optimization_barrier(jnp.mean(center * center, axis=-1, keepdims=True)) + 1e-05)
    return center * inverse * gain_row + shift_row

def attend(queries, key_rows, values, causal):
    scaling = HD ** (-0.5)
    q_heads = queries.reshape(queries.shape[0], HEADS, HD)
    k_heads = key_rows.reshape(key_rows.shape[0], HEADS, HD)
    v_heads = values.reshape(values.shape[0], HEADS, HD)
    scores = low_back(jnp.einsum('qhd,khd->hqk', q_heads, k_heads, precision=HIGHEST) * scaling)
    if causal:
        length = queries.shape[0]
        allowed = lax.broadcasted_iota(jnp.int32, (length, length), 0) >= lax.broadcasted_iota(jnp.int32, (length, length), 1)
        scores = jnp.where(allowed, scores, -1e+30)
    highest = lax.optimization_barrier(jnp.max(scores, axis=-1, keepdims=True))
    log_total = highest + jnp.log(lax.optimization_barrier(jnp.sum(jnp.exp(scores - highest), axis=-1, keepdims=True)))
    probability = low(jnp.exp(scores - log_total))
    attended = jnp.einsum('hqk,khd->qhd', probability, v_heads, precision=HIGHEST)
    return attended.reshape(queries.shape[0], D)

def layer(params, inputs, frames):
    self_w, self_b, self_o, cross_w, cross_b, cross_o, ff_w_in, ff_b_in, ff_w_out, gain_rows, shift_rows = params
    input_one = low(layer_norm(inputs, gain_rows[0], shift_rows[0]))
    query_one = low(low_back(product(input_one, self_w[0]) + self_b[0].reshape(D)))
    key_one = low(low_back(product(input_one, self_w[1])))
    value_one = low(low_back(product(input_one, self_w[2]) + self_b[1].reshape(D)))
    context_one = low(low_back(attend(query_one, key_one, value_one, True)))
    hidden_one = inputs + low_back(product(context_one, self_o)) + shift_rows[1]
    input_two = low(layer_norm(hidden_one, gain_rows[1], shift_rows[2]))
    query_two = low(low_back(product(input_two, cross_w[0]) + cross_b[0].reshape(D)))
    key_two = low(low_back(product(frames, cross_w[1])))
    value_two = low(low_back(product(frames, cross_w[2]) + cross_b[1].reshape(D)))
    context_two = low(low_back(attend(query_two, key_two, value_two, False)))
    hidden_two = hidden_one + low_back(product(context_two, cross_o)) + shift_rows[3]
    input_three = low(layer_norm(hidden_two, gain_rows[2], shift_rows[4]))
    up_rows = low_back(product(input_three, ff_w_in) + ff_b_in.reshape(FF))
    activated = low(jax.nn.gelu(up_rows, approximate=False))
    return hidden_two + low_back(product(activated, ff_w_out)) + shift_rows[5]

def reference(layer_input, encoder_states, out_grad, self_qkv, self_bias, self_out, cross_qkv, cross_bias, cross_out, ff_in, ff_bias, ff_out, norm_gains, shifts):
    params = tuple((item.astype(jnp.float32) for item in (self_qkv, self_bias, self_out, cross_qkv, cross_bias, cross_out, ff_in, ff_bias, ff_out, norm_gains, shifts)))
    inputs = layer_input.astype(jnp.float32).reshape(SEQS, LEN, D)
    frames = encoder_states.astype(jnp.float32)
    cotangent = out_grad.astype(jnp.float32).reshape(SEQS, LEN, D)

    def one_sequence(totals, item):
        seq_input, seq_frames, seq_cotangent = item
        result, pullback = jax.vjp(layer, params, seq_input, seq_frames)
        param_grads, input_grads, frame_grads = pullback(seq_cotangent)
        totals = jax.tree.map(lambda first, second: first + second, totals, param_grads)
        return (totals, (result, input_grads, frame_grads))
    zeros = jax.tree.map(jnp.zeros_like, params)
    grads, (results, input_grads, frame_grads) = lax.scan(one_sequence, zeros, (inputs, frames, cotangent))
    return (results.reshape(TOKENS, D), input_grads.reshape(TOKENS, D), frame_grads, grads[0], grads[1], grads[2], grads[3], grads[4], grads[5], grads[6], grads[7], grads[8], grads[9], grads[10])
```

```python
import functools
import math

import jax
import jax.numpy as jnp
from jax import lax
from jax.experimental import pallas as pl
from jax.experimental.pallas import tpu as pltpu
from jax.sharding import PartitionSpec as P

D = 1024
HD = 64
f32 = jnp.float32
bf16 = jnp.bfloat16
NN = (((1,), (0,)), ((), ()))
NT = (((1,), (1,)), ((), ()))
TN = (((0,), (0,)), ((), ()))
MIB = 2**20


def dot(left, right, dims=NN):
    return lax.dot_general(left, right, dims, preferred_element_type=f32)


def struct(shape, dtype):
    return jax.ShapeDtypeStruct(shape, dtype)


class Line:
    def __init__(self, index):
        self.index = index

    def wait(self, *values):
        self.index, _ = lax.optimization_barrier((self.index, values))


def call(body, name, outs, line, *args, scratch=(), flops=0, vmem=44):
    moved = sum(math.prod(a.shape) * a.dtype.itemsize for a in (*args, *outs))
    vm = pl.BlockSpec(memory_space=pltpu.VMEM)
    got = pl.pallas_call(
        body,
        name=name,
        out_shape=outs,
        in_specs=[pl.BlockSpec(memory_space=pltpu.SMEM)] + [vm] * len(args),
        out_specs=tuple(vm for _ in outs),
        scratch_shapes=scratch,
        compiler_params=pltpu.CompilerParams(vmem_limit_bytes=vmem * MIB),
        cost_estimate=pl.CostEstimate(flops=int(flops), bytes_accessed=moved, transcendentals=0),
    )(line.index, *args)
    line.wait(got[-1])
    return got


def rows_at(half, count):
    return pl.ds(pl.multiple_of(half * count, 32), count)


def place(target, mine, other, half):
    count = mine.shape[0]
    target[rows_at(half, count), :] = mine[...]
    target[rows_at(1 - half, count), :] = other[...]


def pick(pair, seq, chip):
    near, far = pair
    return jnp.where(chip == seq, near[...].astype(f32), far[...].astype(f32)).astype(near.dtype)


def place_of(target, rows, seq, half, chip):
    count = rows[0].shape[0]
    target[rows_at(half, count), :] = pick(rows[:2], seq, chip)
    target[rows_at(1 - half, count), :] = pick(rows[2:], seq, chip)


def normalize(v):
    center = v - jnp.mean(v, axis=-1, keepdims=True)
    inverse = lax.rsqrt(jnp.mean(center * center, axis=-1, keepdims=True) + 1e-05)
    return center * inverse, inverse


def join_pairs(first, second, pieces, rels, me, lanes):
    for piece, pair in zip(pieces, rels):
        for spot, rel in enumerate(pair):
            at = pl.ds(pl.multiple_of((me ^ rel) * 128, 128), 128)
            for place, (target, lane) in enumerate(zip((first, second), lanes)):
                block = piece[spot, place]
                if lane is None:
                    target[:128, at] = block[:, :128]
                    target[128:, at] = block[:, 128:]
                else:
                    target[at, lane : lane + block.shape[1]] = block


def head_masks(width):
    lane = lax.broadcasted_iota(jnp.int32, (1, width), 1) // HD
    return [lane == h for h in range(width // HD)]


def causal_mask(length):
    return lax.broadcasted_iota(jnp.int32, (length, length), 0) >= lax.broadcasted_iota(
        jnp.int32, (length, length), 1
    )


def attention(q, k, v, lse_ref, causal):
    total = jnp.zeros(q.shape, f32)
    q = (q.astype(f32) * HD**-0.5).astype(bf16)
    allowed = causal_mask(q.shape[0]) if causal else None
    for h, mask in enumerate(head_masks(q.shape[1])):
        scores = dot(jnp.where(mask, q, 0), k, NT)
        if causal:
            scores = jnp.where(allowed, scores, -1e30)
        highest = jnp.max(scores, axis=1, keepdims=True)
        weight = jnp.exp(scores - highest)
        norm = jnp.sum(weight, axis=1, keepdims=True)
        total += dot(weight.astype(bf16), jnp.where(mask, v, 0)) * (1.0 / norm)
        lse_ref[:, h : h + 1] = highest + jnp.log(norm)
    return total.astype(bf16)


def attention_back(q, k, v, lse_ref, upstream, causal):
    dq = jnp.zeros(q.shape, f32)
    dk = jnp.zeros(k.shape, f32)
    dv = jnp.zeros(k.shape, f32)
    q = (q.astype(f32) * HD**-0.5).astype(bf16)
    allowed = causal_mask(q.shape[0]) if causal else None
    for h, mask in enumerate(head_masks(q.shape[1])):
        query, above = jnp.where(mask, q, 0), jnp.where(mask, upstream, 0)
        scores = dot(query, k, NT)
        if causal:
            scores = jnp.where(allowed, scores, -1e30)
        prob = jnp.exp(scores - lse_ref[:, h : h + 1])
        dprob = dot(above, v, NT)
        delta = jnp.sum(prob * dprob, axis=1, keepdims=True)
        dscore = (prob * (dprob - delta)).astype(bf16)
        dv += dot(prob.astype(bf16), above, TN)
        dk += dot(dscore, query, TN)
        dq += dot(dscore, jnp.where(mask, k, 0))
    return (dq * HD**-0.5).astype(bf16), dk.astype(bf16), dv.astype(bf16)


def halves(rows_ref, weight, dims, keep, send, half):
    count = keep.shape[0]
    send[...] = dot(rows_ref[rows_at(1 - half, count), :], weight, dims).astype(bf16)
    keep[...] = dot(rows_ref[rows_at(half, count), :], weight, dims)


def self_forward_body(rels, seq, index, x0, x1, x2, x3, vec, bias, *refs):
    if rels is None:
        w, wo, a_ref, qkv, o_ref, lse, keep, send, xs = refs
    else:
        pieces, (a_ref, qkv, o_ref, lse, keep, send, w, wo, xs) = refs[:8], refs[8:]
        join_pairs(w, w, pieces[:4], rels[0], index[0], (0, wo.shape[0]))
        join_pairs(w, wo, pieces[4:], rels[1], index[0], (2 * wo.shape[0], None))
    half = index[1]
    width = wo.shape[0]
    place_of(xs, (x0, x1, x2, x3), seq, half, index[2])
    normal, _ = normalize(xs[...].astype(f32))
    a = (normal * vec[0:1, :] + vec[3:4, :]).astype(bf16)
    a_ref[...] = a
    qkv[:, :width] = (dot(a, w[:, :width]) + bias[0:1, :]).astype(bf16)
    qkv[:, width : 2 * width] = dot(a, w[:, width : 2 * width]).astype(bf16)
    qkv[:, 2 * width :] = (dot(a, w[:, 2 * width :]) + bias[1:2, :]).astype(bf16)
    o_ref[...] = attention(
        qkv[:, :width], qkv[:, width : 2 * width], qkv[:, 2 * width :], lse, True
    )
    halves(o_ref, wo[...], NN, keep, send, half)


def frames_body(rels, index, e, bias, *refs):
    if rels is None:
        w, k, v = refs
        width = k.shape[1]
    else:
        pieces, (k, v, w) = refs[:4], refs[4:]
        width = k.shape[1]
        join_pairs(w, w, pieces, rels, index[0], (0, width))
    k[...] = dot(e[...], w[:, :width]).astype(bf16)
    v[...] = (dot(e[...], w[:, width:]) + bias[3:4, :]).astype(bf16)


def cross_forward_body(rels, index, am, ao, bias, k, v, *refs):
    if rels is None:
        w, wo, a_ref, q_ref, o_ref, lse, keep, send = refs
    else:
        pieces, (a_ref, q_ref, o_ref, lse, keep, send, w, wo) = refs[:4], refs[4:]
        join_pairs(w, wo, pieces, rels, index[0], (0, None))
    half = index[1]
    place(a_ref, am, ao, half)
    q_ref[...] = (dot(a_ref[...], w[...]) + bias[2:3, :]).astype(bf16)
    o_ref[...] = attention(q_ref[...], k[...], v[...], lse, False)
    halves(o_ref, wo[...], NN, keep, send, half)


def norm_body(rows, seq, index, *refs):
    shift, gain, bias = rows
    if seq is None:
        base, keep, recv, far, vec, h_ref, a_ref = refs
        start = base[...]
    else:
        near, across, keep, recv, far, vec, h_ref, a_ref = refs
        start = pick((near, across), seq, index[2])
    h = (
        start.astype(f32)
        + keep[...]
        + recv[...].astype(f32)
        + far[...].astype(f32)
        + vec[shift : shift + 1, :]
    )
    h_ref[...] = h
    normal, _ = normalize(h)
    a_ref[...] = (normal * vec[gain : gain + 1, :] + vec[bias : bias + 1, :]).astype(bf16)


def norm_back_body(gain, index, base, keep, recv, far, h, vec, dh_ref, low_ref, sums):
    incoming = keep[...] + recv[...].astype(f32) + far[...].astype(f32)
    normal, inverse = normalize(h[...].astype(f32))
    sums[...] = jnp.zeros(sums.shape, f32)
    sums[0:1, :] = jnp.sum(incoming * normal, axis=0, keepdims=True)
    sums[1:2, :] = jnp.sum(incoming, axis=0, keepdims=True)
    scaled = incoming * vec[gain : gain + 1, :]
    centered = (
        scaled
        - jnp.mean(scaled, axis=-1, keepdims=True)
        - normal * jnp.mean(scaled * normal, axis=-1, keepdims=True)
    )
    count = keep.shape[0]
    above = (base[...] if base.shape[0] == count else base[rows_at(index[1], count), :]).astype(f32)
    dh = above + inverse * centered
    dh_ref[...] = dh
    if low_ref is not None:
        low_ref[...] = dh.astype(bf16)
        sums[2:3, :] = jnp.sum(dh, axis=0, keepdims=True)
        sums[3:4, :] = jnp.sum(above, axis=0, keepdims=True)


def feed_body(rels, seq, index, am, ao, y0, y1, y2, y3, bias, *refs):
    if rels is None:
        w_in, w_out, a_ref, g_full, g_ref, du_ref, sums, keep, send = refs
    else:
        pieces, (a_ref, g_full, g_ref, du_ref, sums, keep, send, w_in, w_out) = refs[:8], refs[8:]
        for piece, pair in zip(pieces[:4], rels[0]):
            for spot, rel in enumerate(pair):
                at = pl.ds(pl.multiple_of((index[0] ^ rel) * 128, 128), 128)
                w_in[at, :] = piece[spot]
        for piece, pair in zip(pieces[4:], rels[1]):
            for spot, rel in enumerate(pair):
                at = pl.ds(pl.multiple_of((index[0] ^ rel) * 128, 128), 128)
                w_out[:, at] = piece[spot]
    half = index[1]
    place(a_ref, am, ao, half)
    place_of(g_full, (y0, y1, y2, y3), seq, half, index[2])
    hidden = w_in.shape[1]
    step = min(512, hidden)
    for at in range(0, hidden, step):
        to = at + step
        u = dot(a_ref[...], w_in[:, at:to]) + bias[:, at:to]
        dg = dot(g_full[...], w_out[at:to, :], NT)
        cdf = 0.5 * (1.0 + lax.erf(u * 0.7071067811865476))
        g_ref[:, at:to] = (u * cdf).astype(bf16)
        slope = cdf + u * (jnp.exp(-0.5 * u * u) * 0.3989422804014327)
        du = (dg * slope).astype(bf16)
        du_ref[:, at:to] = du
        sums[:, at:to] = jnp.sum(du.astype(f32), axis=0, keepdims=True)
    halves(du_ref, w_in[...], NT, keep, send, half)


def feed_out_body(index, g0, g1, w_out, keep, send):
    half = index[1]
    halves(g0, w_out[...], NN, keep.at[0], send.at[0], half)
    halves(g1, w_out[...], NN, keep.at[1], send.at[1], half)


def cross_back_body(index, hm, ho, q, k, v, lse, w, wo, h_full, dq_ref, dkv, sums, keep, send):
    half = index[1]
    width = q.shape[1]
    place(h_full, hm, ho, half)
    upstream = dot(h_full[...], wo[...], NT).astype(bf16)
    dq, dk, dv = attention_back(q[...], k[...], v[...], lse, upstream, False)
    dq_ref[...] = dq
    dkv[:, :width] = dk
    dkv[:, width:] = dv
    sums[0:1, :] = jnp.sum(dq.astype(f32), axis=0, keepdims=True)
    sums[1:2, :] = jnp.sum(dv.astype(f32), axis=0, keepdims=True)
    halves(dq_ref, w[...], NT, keep, send, half)


def self_back_body(
    seq, index, hm, ho, qkv, lse, w, wo, x0, x1, x2, x3, h_full, dqkv, sums, vsums, keep, send
):
    half = index[1]
    width = wo.shape[0]
    place(h_full, hm, ho, half)
    upstream = dot(h_full[...], wo[...], NT).astype(bf16)
    dq, dk, dv = attention_back(
        qkv[:, :width], qkv[:, width : 2 * width], qkv[:, 2 * width :], lse, upstream, True
    )
    dqkv[:, :width] = dq
    dqkv[:, width : 2 * width] = dk
    dqkv[:, 2 * width :] = dv
    sums[0:1, :] = jnp.sum(dq.astype(f32), axis=0, keepdims=True)
    sums[1:2, :] = jnp.sum(dv.astype(f32), axis=0, keepdims=True)
    count = keep.shape[0]
    other = dot(dqkv[rows_at(1 - half, count), :], w[...], NT)
    send[...] = other.astype(bf16)
    mine = dot(dqkv[rows_at(half, count), :], w[...], NT)
    keep[...] = mine
    normal_m, _ = normalize(pick((x0, x1), seq, index[2]).astype(f32))
    normal_o, _ = normalize(pick((x2, x3), seq, index[2]).astype(f32))
    vsums[0:1, :] = jnp.sum(mine * normal_m, axis=0, keepdims=True) + jnp.sum(
        other * normal_o, axis=0, keepdims=True
    )
    vsums[1:2, :] = jnp.sum(mine, axis=0, keepdims=True) + jnp.sum(other, axis=0, keepdims=True)


def input_grad_body(index, base, keep, recv, far, x, vec, out):
    norm_back_body(0, index, base, keep, recv, far, x, vec, out, None, _Nowhere())


class _Nowhere:
    shape = (8, D)

    def __setitem__(self, at, value):
        pass


def frame_grad_body(index, dkv, w, keep, across, send):
    half, chip = index[1], index[2]
    width = D // 4
    frames = dkv.shape[0]
    for spot in range(2):
        chip_of = (chip + spot) % 2
        at = pl.ds(pl.multiple_of((chip_of * 2 + 1 - half) * width, width), width)
        send[spot, frames // 8 * 8 :, :] = jnp.zeros((send.shape[1] - frames // 8 * 8, width), bf16)
        send[spot, :frames, :] = dot(dkv[...], w[at, :], NT).astype(bf16)
        at = pl.ds(pl.multiple_of((chip_of * 2 + half) * width, width), width)
        (across if spot else keep)[...] = dot(dkv[...], w[at, :], NT)


def frame_sum_body(index, keep0, near0, far0, keep1, near1, far1, out):
    frames, width = keep0.shape
    tiles = width // 128
    for s, (keep, near, far) in enumerate(((keep0, near0, far0), (keep1, near1, far1))):
        total = keep[...] + near[0, :frames, :].astype(f32) + far[...].astype(f32)
        for tile in range(tiles):
            out[pl.ds(2 * tile + s, frames, stride=2 * tiles), :] = total[:, tile * 128 : tile * 128 + 128]


def position_rel(order, position):
    return sum(bit for i, bit in enumerate(order) if position >> (len(order) - 1 - i) & 1)


def weight_grad_body(order, lanes, index, *refs):
    terms = [refs[4 * i : 4 * i + 4] for i in range(len(lanes))]
    keep, send, scratch = refs[4 * len(lanes) :]
    me = index[0]
    spots = {position_rel(order, p): p for p in range(8)}
    for rel in (0, 2, 4, 6):
        at = pl.ds(pl.multiple_of(((me ^ rel) // 2) * 256, 256), 256)
        lane = 0
        for (low, high), (left0, right0, left1, right1) in zip(lanes, terms):
            to = lane + high - low
            total = dot(left0[:, at], right0[:, low:high], TN) + dot(
                left1[:, at], right1[:, low:high], TN
            )
            scratch[0, :, lane:to] = total[:128]
            scratch[1, :, lane:to] = total[128:]
            lane = to
        for low in range(2):
            spot = spots[rel + low]
            target = send if spot >= 4 else keep
            target[spot % 4] = scratch[(me % 2) ^ low].astype(bf16)


def halve_body(count, index, *refs):
    for i in range(count):
        keep, recv = refs[2 * i : 2 * i + 2]
        stay, go = refs[2 * count + 2 * i : 2 * count + 2 * i + 2]
        size = stay.shape[0]
        stay[...] = keep[:size].astype(f32) + recv[:size].astype(f32)
        go[...] = (keep[size:].astype(f32) + recv[size:].astype(f32)).astype(bf16)


def ff_end_body(index, keep0, recv0, keep1, recv1, grad_in, grad_out):
    grad_in[...] = keep0[0] + recv0[0].astype(f32)
    grad_out[...] = (keep1[0] + recv1[0].astype(f32)).T


def cross_end_body(index, keep, recv, qkv, out):
    width = qkv.shape[2]
    total = keep[0] + recv[0].astype(f32)
    for i, lane in enumerate((2, 0, 1)):
        qkv[i] = total[:, lane * width : (lane + 1) * width]
    out[...] = total[:, 3 * width :].T


def self_end_body(index, keep0, recv0, keep1, recv1, qkv, out):
    width = qkv.shape[2]
    total = keep0[0] + recv0[0].astype(f32)
    qkv[0] = total[:, :width]
    qkv[1] = total[:, width:]
    total = keep1[0] + recv1[0].astype(f32)
    qkv[2] = total[:, :width]
    out[...] = total[:, width:].T


def untangle_body(index, tangled, first, second):
    frames = first.shape[0]
    row = lax.broadcasted_iota(jnp.int32, (256, 256), 0)
    column = lax.broadcasted_iota(jnp.int32, (256, 256), 1)
    group = row // 16
    source = (row % 16) * 16 + 2 * (group % 8) + group // 8
    moves = jnp.where(source == column, 1.0, 0.0).astype(bf16)
    for frame in range(0, frames, 16):
        n = min(16, frames - frame)
        block = dot(moves[:, : 16 * n], tangled[16 * frame : 16 * (frame + n), :]).astype(bf16)
        for seq, target in enumerate((first, second)):
            for tile in range(8):
                at = (seq * 8 + tile) * 16
                target[frame : frame + n, tile * 128 : tile * 128 + 128] = block[at : at + n]


def permute_by(value, axis, bit):
    size = lax.axis_size(axis)
    return lax.ppermute(value, axis, [(i, i ^ bit) for i in range(size)])


class Gather:
    def __init__(self, shard, order):
        self.shard, self.order = shard, order

    def step(self, number, *after):
        bit = self.order[number - 1]
        if number == 1:
            if after:
                self.shard, _ = lax.optimization_barrier((self.shard, after))
            self.got = permute_by(self.shard, "fsdp", bit)
        elif number == 2:
            self.near = jnp.stack([self.shard, self.got])
            self.got = self.far = permute_by(self.near, "fsdp", bit)
        else:
            self.pieces = (
                self.near,
                self.far,
                permute_by(self.near, "fsdp", bit),
                permute_by(self.far, "fsdp", bit),
            )
        return self


class Sum:
    def __init__(self, line, *parts):
        self.line = line
        self.keeps = [keep for keep, _, _ in parts]
        self.orders = [order for _, _, order in parts]
        self.number = 0
        self.send([send for _, send, _ in parts])

    def send(self, sends):
        self.recvs = [
            permute_by(send, "fsdp", order[self.number]) for send, order in zip(sends, self.orders)
        ]
        self.number += 1

    def step(self):
        outs, args = [], []
        for keep, recv in zip(self.keeps, self.recvs):
            half = (keep.shape[0] // 2, *keep.shape[1:])
            outs += [struct(half, f32), struct(half, bf16)]
            args += [keep, recv]
        got = call(
            functools.partial(halve_body, len(self.keeps)), "halve", tuple(outs), self.line, *args, vmem=24
        )
        self.keeps = got[::2]
        self.send(got[1::2])

    def end(self, body, name, outs):
        args = [a for pair in zip(self.keeps, self.recvs) for a in pair]
        return call(body, name, outs, self.line, *args, vmem=24)


def rels_of(order):
    b1, b2, b3 = order
    return ((0, b1), (b2, b2 ^ b1), (b3, b3 ^ b1), (b3 ^ b2, b3 ^ b2 ^ b1))


GATHER_A, GATHER_B = (4, 2, 1), (4, 1, 2)
SUM_A, SUM_B = (1, 2, 4), (2, 1, 4)


def shards(
    fast,
    layer_input,
    encoder_states,
    out_grad,
    self_qkv,
    self_bias,
    self_out,
    cross_qkv,
    cross_bias,
    cross_out,
    ff_in,
    ff_bias,
    ff_out,
    norm_gains,
    shifts,
):
    tensor = lax.axis_size("tensor")
    fsdp_size = lax.axis_size("fsdp")
    t = lax.axis_index("tensor")
    me = lax.axis_index("fsdp")
    local_rows = layer_input.shape[0]
    seqs, frames, _ = encoder_states.shape
    length = local_rows * tensor // seqs
    count = length // 2
    width = self_qkv.shape[2]
    heads = width // HD
    hidden = ff_in.shape[1]
    step = tensor // 4
    half = (t // step) % 2
    chip = t // (tensor // 2)
    line = Line(jnp.stack([me, half, chip]).astype(jnp.int32))
    group = [[i for i in range(tensor) if (i // step) % 2 == side] for side in range(2)]

    def partner(value):
        return permute_by(value, "tensor", step)

    def rows_of_all(own):
        if fast:
            across = permute_by(own, "tensor", 2)
            return own, across, partner(own), partner(across)
        whole = lax.all_gather(own, "tensor", axis=0, tiled=True).reshape(seqs, 2, count, D)
        return tuple(
            lax.dynamic_index_in_dim(
                lax.dynamic_index_in_dim(whole, seq, 0, False), side, 0, False
            )
            for side in (half, 1 - half)
            for seq in (chip, 1 - chip)
        )

    def summed(keep, send):
        recv = partner(send)
        if fast:
            going = (keep + recv.astype(f32)).astype(bf16)
            line.wait(going)
            return keep, recv, permute_by(going, "tensor", 2)
        total = lax.psum(keep + recv.astype(f32), "tensor", axis_index_groups=group)
        return total, jnp.zeros_like(recv), jnp.zeros_like(recv)

    def own_of(first, second):
        return jnp.where(chip == 0, first, second)

    def own_rows(first, second):
        return lax.dynamic_slice_in_dim(
            own_of(first, second), (t % step) * local_rows, local_rows, 0
        )

    def summed_own(keeps, sends):
        if not fast:
            terms = [summed(k, s) for k, s in zip(keeps, sends)]
            return tuple(own_rows(a, b) for a, b in zip(*terms))
        recvs = [partner(s) for s in sends]
        going = own_of(keeps[1] + recvs[1].astype(f32), keeps[0] + recvs[0].astype(f32))
        far = permute_by(going.astype(bf16), "tensor", 2)
        return own_of(keeps[0], keeps[1]), own_of(recvs[0], recvs[1]), far

    def with_out(weight, out):
        return jnp.stack([weight, jnp.concatenate([out[:128], out[128:]], 1)])

    rels_a, rels_b = rels_of(GATHER_A), rels_of(GATHER_B)
    packed_rows = jnp.concatenate([norm_gains, shifts], 0)
    packed_bias = jnp.concatenate(
        [self_bias.reshape(-1, HD // fsdp_size), cross_bias.reshape(-1, HD // fsdp_size), ff_bias],
        0,
    )
    if fast:
        self_a = Gather(self_qkv[:2], GATHER_A).step(1)
        self_b = Gather(with_out(self_qkv[2], self_out), GATHER_B).step(1)
        x_rows = rows_of_all(layer_input)
        e_seq = call(
            untangle_body,
            "untangle",
            (struct((frames, D), bf16),) * 2,
            line,
            encoder_states.reshape(2, frames, 8, 128).transpose(1, 2, 0, 3).reshape(-1, 128),
        )
        bias_rows = packed_bias.shape[0] * packed_bias.shape[1] // 128
        small = jnp.concatenate(
            [packed_rows, packed_bias.reshape(bias_rows, 128), jnp.zeros((5, 128), bf16)], 0
        )
        for bit in (1, 2, 4):
            pair = permute_by(small, "fsdp", bit)
            up = (me // bit) % 2 == 1
            small = jnp.concatenate(
                [jnp.where(up, pair, small), jnp.where(up, small, pair)], 0
            )
        small = small.reshape(8, -1, 128)
        vec = small[:, :9].transpose(1, 0, 2).reshape(9, D).astype(f32)
        biases = (
            small[:, 9 : 9 + bias_rows]
            .reshape(8, -1, HD // fsdp_size)
            .transpose(1, 0, 2)
            .reshape(-1, HD)
            .astype(f32)
        )
        self_a.step(2)
        self_b.step(2)
        cross_a = Gather(cross_qkv[1:], GATHER_A).step(1, self_a.near, self_b.near)
        cross_b = Gather(with_out(cross_qkv[0], cross_out), GATHER_B).step(1, self_a.near, self_b.near)
        self_a.step(3)
        self_b.step(3)
        cross_a.step(2)
        cross_b.step(2)
        out_grad, _ = lax.optimization_barrier((out_grad, (x_rows, self_a.far)))
    else:
        x_rows = rows_of_all(layer_input)
        e_seq = [encoder_states[s] for s in range(2)]
        vec = lax.all_gather(packed_rows, "fsdp", axis=1, tiled=True).astype(f32)
        biases = lax.all_gather(packed_bias, "fsdp", axis=1, tiled=True).astype(f32)
        whole = lax.all_gather(self_qkv, "fsdp", axis=1, tiled=True)
        w_self = jnp.concatenate([whole[0], whole[1], whole[2]], 1)
        wo_self = lax.all_gather(self_out, "fsdp", axis=1, tiled=True)
        whole = lax.all_gather(cross_qkv, "fsdp", axis=1, tiled=True)
        w_cross, w_kv = whole[0], jnp.concatenate([whole[1], whole[2]], 1)
        wo_cross = lax.all_gather(cross_out, "fsdp", axis=1, tiled=True)
        w_in = lax.all_gather(ff_in, "fsdp", axis=0, tiled=True)
        w_out = lax.all_gather(ff_out, "fsdp", axis=1, tiled=True)
    bias = biases[: 4 * heads].reshape(4, width)
    ff_bias_row = biases[4 * heads :].reshape(1, hidden)

    attn_flops = 8 * length * width * 1024
    row_pair = (struct((count, D), f32), struct((count, D), bf16))

    def self_forward(s):
        nonlocal w_self, wo_self
        outs = (
            struct((length, D), bf16),
            struct((length, 3 * width), bf16),
            struct((length, width), bf16),
            struct((length, heads), f32),
            *row_pair,
        )
        kwargs = dict(scratch=(pltpu.VMEM((length, D), bf16),), flops=attn_flops)
        args = (*x_rows, vec, bias)
        if fast and s == 0:
            outs += (struct((D, 3 * width), bf16), struct((width, D), bf16))
            *got, w_self, wo_self = call(
                functools.partial(self_forward_body, (rels_a, rels_b), s),
                "self_forward", outs, line, *args, *self_a.pieces, *self_b.pieces, **kwargs,
            )
        else:
            got = call(
                functools.partial(self_forward_body, None, s),
                "self_forward", outs, line, *args, w_self, wo_self, **kwargs,
            )
        a1[s], qkv1[s], o1[s], lse1[s], *res = got
        sum1[s] = summed(*res)

    def frames_in(s):
        nonlocal w_kv
        outs = (struct((frames, width), bf16),) * 2
        flops = 4 * frames * D * width
        if fast and s == 0:
            k2[s], v2[s], w_kv = call(
                functools.partial(frames_body, rels_a),
                "frames_in", outs + (struct((D, 2 * width), bf16),), line, e_seq[s], bias,
                *cross_a.pieces, flops=flops,
            )
        else:
            k2[s], v2[s] = call(
                functools.partial(frames_body, None),
                "frames_in", outs, line, e_seq[s], bias, w_kv, flops=flops,
            )

    def norm_of(rows, seq, base, terms, name):
        return call(
            functools.partial(norm_body, rows, seq),
            name, (struct((count, D), f32), struct((count, D), bf16)), line, *base, *terms, vec, vmem=16,
        )

    def norm_two(s):
        h1[s], mine = norm_of((4, 1, 5), s, x_rows[:2], sum1[s], "norm_two")
        a2_rows[s] = mine, partner(mine)

    def cross_forward(s):
        nonlocal w_cross, wo_cross
        outs = (
            struct((length, D), bf16),
            struct((length, width), bf16),
            struct((length, width), bf16),
            struct((length, heads), f32),
            *row_pair,
        )
        args = (*a2_rows[s], bias, k2[s], v2[s])
        if fast and s == 0:
            *got, w_cross, wo_cross = call(
                functools.partial(cross_forward_body, rels_b),
                "cross_forward", outs + (struct((D, width), bf16), struct((width, D), bf16)),
                line, *args, *cross_b.pieces, flops=2 * attn_flops,
            )
        else:
            got = call(
                functools.partial(cross_forward_body, None),
                "cross_forward", outs, line, *args, w_cross, wo_cross, flops=2 * attn_flops,
            )
        a2[s], q2[s], o2[s], lse2[s], *res = got
        sum2[s] = summed(*res)

    def norm_three(s):
        h2[s], mine = norm_of((6, 2, 7), None, (h1[s],), sum2[s], "norm_three")
        a3_rows[s] = mine, partner(mine)

    def feed(s):
        nonlocal w_in, w_out
        outs = (
            struct((length, D), bf16),
            struct((length, D), bf16),
            struct((length, hidden), bf16),
            struct((length, hidden), bf16),
            struct((1, hidden), f32),
            *row_pair,
        )
        args = (*a3_rows[s], *g_rows, ff_bias_row)
        flops = 6 * length * D * hidden
        if fast and s == 0:
            *got, w_in, w_out = call(
                functools.partial(feed_body, (rels_a, rels_b), s),
                "feed", outs + (struct((D, hidden), bf16), struct((hidden, D), bf16)), line,
                *args, *ff_a.pieces, *ff_b.pieces, flops=flops,
            )
        else:
            got = call(
                functools.partial(feed_body, None, s),
                "feed", outs, line, *args, w_in, w_out, flops=flops,
            )
        a3[s], g_full[s], act[s], du[s], ff_sums[s], *res = got
        sum3[s] = summed(*res)

    def feed_out():
        out_keep, out_send = call(
            feed_out_body, "feed_out",
            (struct((2, count, D), f32), struct((2, count, D), bf16)),
            line, act[0], act[1], w_out, flops=4 * length * D * hidden,
        )
        return summed_own((out_keep[0], out_keep[1]), (out_send[0], out_send[1]))

    def norm_back(gain, base, terms, h, name):
        return call(
            functools.partial(norm_back_body, gain),
            name,
            (struct((count, D), f32), struct((count, D), bf16), struct((8, D), f32)),
            line, base, *terms, h, vec, vmem=24,
        )

    def norm_three_back(s):
        dh2[s], low, sums3[s] = norm_back(2, g_full[s], sum3[s], h2[s], "norm_three_back")
        h2_rows[s] = low, partner(low)

    def cross_back(s):
        outs = (
            struct((length, D), bf16),
            struct((length, width), bf16),
            struct((frames, 2 * width), bf16),
            struct((2, width), f32),
            *row_pair,
        )
        h2_full[s], dq2[s], dkv2[s], cross_sums[s], *res = call(
            cross_back_body, "cross_back", outs, line,
            *h2_rows[s], q2[s], k2[s], v2[s], lse2[s], w_cross, wo_cross, flops=4 * attn_flops,
        )
        sum4[s] = summed(*res)

    def norm_two_back(s):
        dh1[s], low, sums2[s] = norm_back(1, dh2[s], sum4[s], h1[s], "norm_two_back")
        h1_rows[s] = low, partner(low)

    def self_back(s):
        outs = (
            struct((length, D), bf16),
            struct((length, 3 * width), bf16),
            struct((2, width), f32),
            struct((2, D), f32),
            *row_pair,
        )
        h1_full[s], dqkv1[s], self_sums[s], vec_sums[s], *res5[s] = call(
            functools.partial(self_back_body, s), "self_back", outs, line,
            *h1_rows[s], qkv1[s], lse1[s], w_self, wo_self, *x_rows, flops=2 * attn_flops,
        )

    def weight_grad(terms, order, name):
        lanes = [span if span else (0, right[0].shape[1]) for _, right, span in terms]
        n = sum(high - low for low, high in lanes)
        flat = [x for left, right, _ in terms for x in (left[0], right[0], left[1], right[1])]
        got = call(
            functools.partial(weight_grad_body, order, lanes),
            name,
            (struct((4, 128, n), bf16), struct((4, 128, n), bf16)),
            line,
            *flat,
            scratch=(pltpu.VMEM((2, 128, n), f32),),
            flops=sum(4 * math.prod(term[0][0].shape) for term in terms) * n / len(terms),
        )
        return (*got, order)

    def plain_grad(lefts, rights):
        return sum(dot(a, b, TN) for a, b in zip(lefts, rights))

    def frame_grad(s):
        padded = -(-frames // 16) * 16
        keep, across, send = call(
            frame_grad_body, "frame_grad",
            (
                struct((frames, D // 4), f32),
                struct((frames, D // 4), f32),
                struct((2, padded, D // 4), bf16),
            ),
            line, dkv2[s], w_kv, flops=4 * frames * D * width,
        )
        near = partner(send)
        far = (across + near[1, :frames].astype(f32)).astype(bf16)
        return keep, near, permute_by(far, "tensor", 2)

    (
        a1, qkv1, o1, lse1, sum1, h1, k2, v2, a2_rows, a2, q2, o2, lse2, sum2, h2, a3_rows, a3, g_full,
        act, du, ff_sums, sum3, dh2, sums3, h2_rows, h2_full, dq2, dkv2, cross_sums, sum4, dh1, sums2,
        h1_rows, h1_full, dqkv1, self_sums, vec_sums, res5,
    ) = ([None] * 2 for _ in range(38))
    if not fast:
        g_rows = rows_of_all(out_grad)
        for stage in (
            self_forward, frames_in, norm_two, cross_forward, norm_three, feed, norm_three_back,
            cross_back, norm_two_back, self_back,
        ):
            for s in range(2):
                stage(s)
        out_terms = feed_out()
    else:
        w_self = wo_self = w_kv = w_cross = wo_cross = w_in = w_out = None
        self_forward(0)
        cross_a.step(3)
        cross_b.step(3)
        ff_a = Gather(ff_in, GATHER_A).step(1, cross_a.far, cross_b.far)
        ff_b = Gather(ff_out, GATHER_B).step(1, cross_a.far, cross_b.far)
        self_forward(1)
        g_rows = rows_of_all(out_grad)
        frames_in(0)
        norm_two(0)
        ff_a.step(2)
        ff_b.step(2)
        cross_forward(0)
        frames_in(1)
        norm_two(1)
        ff_a.step(3)
        ff_b.step(3)
        cross_forward(1)
        norm_three(0)
        feed(0)
        norm_three(1)
        feed(1)
        out_terms = feed_out()
        ff_sum = [weight_grad([(a3, du, None)], SUM_A, "ff_in_grad")]
        norm_three_back(0)
        cross_back(0)
        ff_sum = Sum(line, *ff_sum, weight_grad([(g_full, act, None)], SUM_B, "ff_out_grad"))
        norm_three_back(1)
        cross_back(1)
        norm_two_back(0)
        ff_sum.step()
        cross_sum = Sum(
            line,
            weight_grad([(e_seq, dkv2, None), (a2, dq2, None), (h2_full, o2, None)], SUM_A, "cross_grad"),
        )
        self_back(0)
        ff_sum.step()
        norm_two_back(1)
        frame_terms = frame_grad(0)
        self_back(1)
    terms = summed_own((res5[0][0], res5[1][0]), (res5[0][1], res5[1][1]))

    counts = (t % step) == 0

    def vector(sums, row):
        mine = own_of(sums[0][row], sums[1][row])
        return jnp.where(counts, mine, 0.0)

    vectors = jnp.stack(
        [
            vec_sums[0][0] + vec_sums[1][0],
            vector(sums2, 0),
            vector(sums3, 0),
            vec_sums[0][1] + vec_sums[1][1],
            vector(sums2, 2),
            vector(sums2, 1),
            vector(sums3, 2),
            vector(sums3, 1),
            vector(sums3, 3),
        ]
    )
    bias_sums = jnp.concatenate(
        [
            self_sums[0] + self_sums[1],
            cross_sums[0] + cross_sums[1],
            (ff_sums[0] + ff_sums[1]).reshape(-1, width),
        ],
        0,
    ).reshape(-1, HD)
    if fast:
        self_sum = Sum(
            line,
            weight_grad([(a1, dqkv1, (0, 2 * width))], SUM_A, "self_grad"),
            weight_grad([(a1, dqkv1, (2 * width, 3 * width)), (h1_full, o1, None)], SUM_B, "self_grad_b"),
        )
        cross_sum.step()
        frame_terms = (*frame_terms, *frame_grad(1))
        ff_in_grad, ff_out_grad = ff_sum.end(
            ff_end_body, "ff_end", (struct((128, hidden), f32), struct((hidden, 128), f32))
        )
        self_sum.step()
        cross_sum.step()
        self_sum.step()
    layer_output = (
        own_rows(h2[0], h2[1]) + sum(term.astype(f32) for term in out_terms) + vec[8][None, :]
    )
    (input_grad,) = call(
        input_grad_body, "input_grad", (struct((local_rows, D), f32),),
        line, own_rows(dh1[0], dh1[1]), *terms, layer_input, vec, vmem=16,
    )
    if fast:
        cross_qkv_grad, cross_out_grad = cross_sum.end(
            cross_end_body, "cross_end", (struct((3, 128, width), f32), struct((width, 128), f32))
        )
        tiles = D // 4 // 128
        (rows,) = call(
            frame_sum_body, "frame_sum", (struct((frames * 2 * tiles, 128), f32),), line, *frame_terms,
        )
        encoder_grad = (
            rows.reshape(frames, tiles, 2, 128).transpose(2, 0, 1, 3).reshape(2, frames, D // 4)
        )
        self_qkv_grad, self_out_grad = self_sum.end(
            self_end_body, "self_end", (struct((3, 128, width), f32), struct((width, 128), f32))
        )
        rows = bias_sums.size // D
        small = jnp.concatenate([vectors, bias_sums.reshape(rows, D)], 0)
        for bit in (1, 2, 4):
            small = small + permute_by(small, "fsdp", bit)
        vectors = lax.dynamic_slice_in_dim(small[:9], me * 128, 128, 1)
        for bit in (1, 2):
            vectors = vectors + permute_by(vectors, "tensor", bit)
        vectors = lax.dynamic_slice_in_dim(vectors, t * 32, 32, 1)
        bias_sums = lax.dynamic_slice_in_dim(small[9:].reshape(-1, HD), me * 8, 8, 1)
    else:
        part = jnp.stack([dot(dkv2[s], w_kv, NT) for s in range(2)])
        encoder_grad = lax.psum_scatter(part, "tensor", scatter_dimension=2, tiled=True)

        def scattered(part, dimension):
            return lax.psum_scatter(part, "fsdp", scatter_dimension=dimension, tiled=True)

        vectors = scattered(vectors, 1)
        vectors = lax.psum_scatter(vectors, "tensor", scatter_dimension=1, tiled=True)
        bias_sums = scattered(bias_sums, 1)
        ff_in_grad = scattered(plain_grad(a3, du), 0)
        ff_out_grad = scattered(plain_grad(act, g_full), 1)
        cross_out_grad = scattered(plain_grad(o2, h2_full), 1)
        kv_grad = plain_grad(e_seq, dkv2)
        cross_qkv_grad = scattered(
            jnp.stack([plain_grad(a2, dq2), kv_grad[:, :width], kv_grad[:, width:]]), 1
        )
        self_out_grad = scattered(plain_grad(o1, h1_full), 1)
        qkv_grad = scattered(plain_grad(a1, dqkv1), 0)
        self_qkv_grad = jnp.stack([qkv_grad[:, i * width : (i + 1) * width] for i in range(3)])
    piece = HD // fsdp_size
    self_bias_grad = bias_sums[: 2 * heads].reshape(2, heads, piece)
    cross_bias_grad = bias_sums[2 * heads : 4 * heads].reshape(2, heads, piece)
    ff_bias_grad = bias_sums[4 * heads :]
    return (
        layer_output,
        input_grad,
        encoder_grad,
        self_qkv_grad,
        self_bias_grad,
        self_out_grad,
        cross_qkv_grad,
        cross_bias_grad,
        cross_out_grad,
        ff_in_grad,
        ff_bias_grad,
        ff_out_grad,
        vectors[:3],
        vectors[3:],
    )


def solution(mesh):
    fast = mesh.shape["fsdp"] == 8 and mesh.shape["tensor"] == 4
    return jax.shard_map(
        functools.partial(shards, fast),
        mesh=mesh,
        in_specs=(
            P(("fsdp", "tensor"), None),
            P("fsdp", None, None),
            P(("fsdp", "tensor"), None),
            P(None, "fsdp", "tensor"),
            P(None, "tensor", "fsdp"),
            P("tensor", "fsdp"),
            P(None, "fsdp", "tensor"),
            P(None, "tensor", "fsdp"),
            P("tensor", "fsdp"),
            P("fsdp", "tensor"),
            P("tensor", "fsdp"),
            P("tensor", "fsdp"),
            P(None, "fsdp"),
            P(None, "fsdp"),
        ),
        out_specs=(
            P(("fsdp", "tensor"), None),
            P(("fsdp", "tensor"), None),
            P("fsdp", None, "tensor"),
            P(None, "fsdp", "tensor"),
            P(None, "tensor", "fsdp"),
            P("tensor", "fsdp"),
            P(None, "fsdp", "tensor"),
            P(None, "tensor", "fsdp"),
            P("tensor", "fsdp"),
            P("fsdp", "tensor"),
            P("tensor", "fsdp"),
            P("tensor", "fsdp"),
            P(None, ("fsdp", "tensor")),
            P(None, ("fsdp", "tensor")),
        ),
        check_vma=False,
    )
```

```python
import functools
import math

import jax
import jax.numpy as jnp
from jax import lax
from jax.experimental import pallas as pl
from jax.experimental.pallas import tpu as pltpu
from jax.sharding import PartitionSpec as P

D = 1024
HD = 64
f32 = jnp.float32
bf16 = jnp.bfloat16
NN = (((1,), (0,)), ((), ()))
NT = (((1,), (1,)), ((), ()))
TN = (((0,), (0,)), ((), ()))
MIB = 2**20


def dot(left, right, dims=NN):
    return lax.dot_general(left, right, dims, preferred_element_type=f32)


def struct(shape, dtype):
    return jax.ShapeDtypeStruct(shape, dtype)


class Line:
    def __init__(self, index):
        self.index = index
        self.kept = {}

    def wait(self, *values):
        self.index, _ = lax.optimization_barrier((self.index, values))

    def away(self, *values):
        for value in values:
            self.kept[id(value)] = value


KERNELS = {
    "untangle": (16, 0.3),
    "self_forward": (14, 0.3),
    "frames_in": (12, 0.3),
    "norm_two": (8, 4),
    "norm_three": (8, 4),
    "cross_forward": (20, 0.3),
    "feed": (22, 0.3),
    "feed_out": (12, 0.3),
    "ff_grad": (20, 0.3),
    "norm_three_back": (10, 4),
    "norm_two_back": (10, 4),
    "cross_back": (24, 0.3),
    "self_back": (16, 0.3),
    "cross_grad": (18, 0.3),
    "cross_grad_b": (16, 0.3),
    "self_grad": (10, 0.3),
    "self_grad_b": (10, 0.3),
    "frame_grad": (16, 0.3),
    "frame_sum": (20, 0.3),
    "halve": (12, 0.3),
    "input_grad": (8, 0.3),
    "ff_end": (8, 0.3),
    "cross_end": (8, 0.3),
    "self_end": (8, 0.3),
    "own": (8, 0.3),
    "output": (8, 0.3),
    "biases": (8, 0.3),
    "vectors": (8, 0.3),
    "frame_across": (12, 0.3),
    "small": (8, 0.3),
}


def call(body, name, outs, line, *args, far=(), scratch=()):
    grant, time = KERNELS[name]
    vm = pl.BlockSpec(memory_space=pltpu.VMEM)
    args = [
        pltpu.with_memory_space_constraint(a, pltpu.HBM) if id(a) in line.kept else a for a in args
    ]
    got = pl.pallas_call(
        body,
        name=name,
        out_shape=tuple(
            (pltpu.HBM if i in far else pltpu.VMEM)(out.shape, out.dtype)
            for i, out in enumerate(outs)
        ),
        in_specs=[pl.BlockSpec(memory_space=pltpu.SMEM)] + [vm] * len(args),
        out_specs=tuple(vm for _ in outs),
        scratch_shapes=scratch,
        compiler_params=pltpu.CompilerParams(vmem_limit_bytes=grant * MIB),
        cost_estimate=pl.CostEstimate(
            flops=int(time * 1.15e9), bytes_accessed=int(time * 3.69e6), transcendentals=0
        ),
    )(line.index, *args)
    line.away(*(got[i] for i in far))
    line.wait(got[-1])
    return got


def rows_at(half, count):
    return pl.ds(pl.multiple_of(half * count, 32), count)


def place(target, mine, other, half):
    count = mine.shape[0]
    target[rows_at(half, count), :] = mine[...]
    target[rows_at(1 - half, count), :] = other[...]


def pick(pair, seq, chip):
    near, far = pair
    return jnp.where(chip == seq, near[...].astype(f32), far[...].astype(f32)).astype(near.dtype)


def place_of(target, rows, seq, half, chip):
    count = rows[0].shape[0]
    target[rows_at(half, count), :] = pick(rows[:2], seq, chip)
    target[rows_at(1 - half, count), :] = pick(rows[2:], seq, chip)


def normalize(v):
    center = v - jnp.mean(v, axis=-1, keepdims=True)
    inverse = lax.rsqrt(jnp.mean(center * center, axis=-1, keepdims=True) + 1e-05)
    return center * inverse, inverse


def spots(pieces, rels, me):
    for piece, group in zip(pieces, rels):
        for spot, rel in enumerate(group):
            yield piece.at[spot], me ^ rel, pl.ds(pl.multiple_of((me ^ rel) * 128, 128), 128)


def head_masks(width):
    lane = lax.broadcasted_iota(jnp.int32, (1, width), 1) // HD
    return [lane == h for h in range(width // HD)]


def causal_mask(length):
    return lax.broadcasted_iota(jnp.int32, (length, length), 0) >= lax.broadcasted_iota(
        jnp.int32, (length, length), 1
    )


def attention(q, k, v, lse_ref, causal):
    total = jnp.zeros(q.shape, f32)
    q = (q.astype(f32) * HD**-0.5).astype(bf16)
    allowed = causal_mask(q.shape[0]) if causal else None
    for h, mask in enumerate(head_masks(q.shape[1])):
        scores = dot(jnp.where(mask, q, 0), k, NT)
        if causal:
            scores = jnp.where(allowed, scores, -1e30)
        highest = jnp.max(scores, axis=1, keepdims=True)
        weight = jnp.exp(scores - highest)
        norm = jnp.sum(weight, axis=1, keepdims=True)
        total += dot(weight.astype(bf16), jnp.where(mask, v, 0)) * (1.0 / norm)
        lse_ref[:, h : h + 1] = highest + jnp.log(norm)
    return total.astype(bf16)


def attention_back(q, k, v, lse_ref, upstream, causal):
    dq = jnp.zeros(q.shape, f32)
    dk = jnp.zeros(k.shape, f32)
    dv = jnp.zeros(k.shape, f32)
    q = (q.astype(f32) * HD**-0.5).astype(bf16)
    allowed = causal_mask(q.shape[0]) if causal else None
    for h, mask in enumerate(head_masks(q.shape[1])):
        query, above = jnp.where(mask, q, 0), jnp.where(mask, upstream, 0)
        scores = dot(query, k, NT)
        if causal:
            scores = jnp.where(allowed, scores, -1e30)
        prob = jnp.exp(scores - lse_ref[:, h : h + 1])
        dprob = dot(above, v, NT)
        delta = jnp.sum(prob * dprob, axis=1, keepdims=True)
        dscore = (prob * (dprob - delta)).astype(bf16)
        dv += dot(prob.astype(bf16), above, TN)
        dk += dot(dscore, query, TN)
        dq += dot(dscore, jnp.where(mask, k, 0))
    return (dq * HD**-0.5).astype(bf16), dk.astype(bf16), dv.astype(bf16)


def halves(rows_ref, weight, dims, keep, send, half):
    count = keep.shape[0]
    send[...] = dot(rows_ref[rows_at(1 - half, count), :], weight, dims).astype(bf16)
    keep[...] = dot(rows_ref[rows_at(half, count), :], weight, dims)


def join_out(wo, piece, at):
    wo[:128, at] = piece[128:256, :128]
    wo[128:, at] = piece[128:256, 128:]


def join_small(vec, bias, pieces, rels, me):
    lane = lax.broadcasted_iota(jnp.int32, (128, D), 1)
    spot_of = lax.broadcasted_iota(jnp.int32, (128, D), 0)
    total = jnp.zeros((32, D), f32)
    for piece, owner, at in spots(pieces, rels, me):
        vec[:, at] = piece[256:272, :128].astype(f32)
        moves = jnp.where(((lane & 63) == owner * 8 + spot_of) & (spot_of < 8), 1.0, 0.0)
        total += dot(piece[256:288, 128:], moves.astype(bf16))
    row = lax.broadcasted_iota(jnp.int32, (32, D), 0)
    head = lax.broadcasted_iota(jnp.int32, (32, D), 1) >> 6
    total = jnp.where(head == jnp.where(row < 16, row & 3, row - 16), total, 0.0).astype(bf16)
    kind = lax.broadcasted_iota(jnp.int32, (8, 32), 0)
    row = lax.broadcasted_iota(jnp.int32, (8, 32), 1)
    moves = jnp.where(kind == jnp.where(row < 16, row >> 2, 4), 1.0, 0.0).astype(bf16)
    bias[...] = dot(moves, total)


def self_forward_body(rels, seq, index, x0, x1, x2, x3, *refs):
    if rels is None:
        vec, bias, w, wo, a_ref, qkv, o_ref, lse, keep, send, xs = refs
    else:
        pieces, (a_ref, qkv, o_ref, lse, keep, send, w, wo, vec, bias, xs) = refs[:6], refs[6:]
        me, wide = index[0], wo.shape[0]
        for piece, _, at in spots(pieces[:3], rels[0], me):
            w[at, :wide] = piece[:128, :]
            w[at, wide : 2 * wide] = piece[128:, :]
        for piece, _, at in spots(pieces[3:], rels[1], me):
            w[at, 2 * wide :] = piece[:128, :]
            join_out(wo, piece, at)
        join_small(vec, bias, pieces[3:], rels[1], me)
    half = index[1]
    width = wo.shape[0]
    place_of(xs, (x0, x1, x2, x3), seq, half, index[2])
    normal, _ = normalize(xs[...].astype(f32))
    a = (normal * vec[0:1, :] + vec[3:4, :]).astype(bf16)
    a_ref[...] = a
    qkv[:, :width] = (dot(a, w[:, :width]) + bias[0:1, :width]).astype(bf16)
    qkv[:, width : 2 * width] = dot(a, w[:, width : 2 * width]).astype(bf16)
    qkv[:, 2 * width :] = (dot(a, w[:, 2 * width :]) + bias[1:2, :width]).astype(bf16)
    o_ref[...] = attention(
        qkv[:, :width], qkv[:, width : 2 * width], qkv[:, 2 * width :], lse, True
    )
    halves(o_ref, wo[...], NN, keep, send, half)


def frames_body(rels, index, e, bias, *refs):
    if rels is None:
        w, k, v = refs
        width = k.shape[1]
    else:
        pieces, (k, v, w) = refs[:3], refs[3:]
        width = k.shape[1]
        for piece, _, at in spots(pieces, rels, index[0]):
            w[at, :width] = piece[:128, :]
            w[at, width:] = piece[128:, :]
    k[...] = dot(e[...], w[:, :width]).astype(bf16)
    v[...] = (dot(e[...], w[:, width:]) + bias[3:4, :width]).astype(bf16)


def cross_forward_body(rels, index, am, ao, bias, k, v, *refs):
    if rels is None:
        w, wo, a_ref, q_ref, o_ref, lse, keep, send = refs
    else:
        pieces, (a_ref, q_ref, o_ref, lse, keep, send, w, wo) = refs[:3], refs[3:]
        for piece, _, at in spots(pieces, rels, index[0]):
            w[at, :] = piece[:128, :]
            join_out(wo, piece, at)
    half = index[1]
    place(a_ref, am, ao, half)
    q_ref[...] = (dot(a_ref[...], w[...]) + bias[2:3, : w.shape[1]]).astype(bf16)
    o_ref[...] = attention(q_ref[...], k[...], v[...], lse, False)
    halves(o_ref, wo[...], NN, keep, send, half)


def norm_body(rows, seq, index, *refs):
    shift, gain, bias = rows
    if seq is None:
        base, keep, recv, far, vec, h_ref, a_ref = refs
        start = base[...]
    else:
        near, across, keep, recv, far, vec, h_ref, a_ref = refs
        start = pick((near, across), seq, index[2])
    h = (
        start.astype(f32)
        + keep[...]
        + recv[...].astype(f32)
        + far[...].astype(f32)
        + vec[shift : shift + 1, :]
    )
    h_ref[...] = h
    normal, _ = normalize(h)
    a_ref[...] = (normal * vec[gain : gain + 1, :] + vec[bias : bias + 1, :]).astype(bf16)


def norm_back_body(gain, index, base, keep, recv, far, h, vec, dh_ref, low_ref, sums):
    incoming = keep[...] + recv[...].astype(f32) + far[...].astype(f32)
    normal, inverse = normalize(h[...].astype(f32))
    sums[...] = jnp.zeros(sums.shape, f32)
    sums[0:1, :] = jnp.sum(incoming * normal, axis=0, keepdims=True)
    sums[1:2, :] = jnp.sum(incoming, axis=0, keepdims=True)
    scaled = incoming * vec[gain : gain + 1, :]
    centered = (
        scaled
        - jnp.mean(scaled, axis=-1, keepdims=True)
        - normal * jnp.mean(scaled * normal, axis=-1, keepdims=True)
    )
    count = keep.shape[0]
    above = (base[...] if base.shape[0] == count else base[rows_at(index[1], count), :]).astype(f32)
    dh = above + inverse * centered
    dh_ref[...] = dh
    low_ref[...] = dh.astype(bf16)
    sums[2:3, :] = jnp.sum(dh, axis=0, keepdims=True)
    sums[3:4, :] = jnp.sum(above, axis=0, keepdims=True)


def feed_body(rels, seq, index, am, ao, y0, y1, y2, y3, bias, *refs):
    if rels is None:
        w_in, w_out, a_ref, g_full, g_ref, du_ref, sums, keep, send = refs
    else:
        pieces, (a_ref, g_full, g_ref, du_ref, sums, keep, send, w_in, w_out) = refs[:6], refs[6:]
        for piece, _, at in spots(pieces[:3], rels[0], index[0]):
            for tile in range(w_in.shape[1] // 128):
                w_in[at, tile * 128 : tile * 128 + 128] = piece[tile]
        for piece, _, at in spots(pieces[3:], rels[1], index[0]):
            for tile in range(w_in.shape[1] // 128):
                w_out[tile * 128 : tile * 128 + 128, at] = piece[tile]
    half = index[1]
    place(a_ref, am, ao, half)
    place_of(g_full, (y0, y1, y2, y3), seq, half, index[2])
    hidden = w_in.shape[1]
    step = min(512, hidden)
    for at in range(0, hidden, step):
        to = at + step
        u = dot(a_ref[...], w_in[:, at:to]) + bias[4:5, at:to]
        dg = dot(g_full[...], w_out[at:to, :], NT)
        cdf = 0.5 * (1.0 + lax.erf(u * 0.7071067811865476))
        g_ref[:, at:to] = (u * cdf).astype(bf16)
        slope = cdf + u * (jnp.exp(-0.5 * u * u) * 0.3989422804014327)
        du = (dg * slope).astype(bf16)
        du_ref[:, at:to] = du
        sums[:, at:to] = jnp.sum(du.astype(f32), axis=0, keepdims=True)
    halves(du_ref, w_in[...], NT, keep, send, half)


def feed_out_body(index, g0, g1, w_out, keep0, keep1, send0, send1):
    half = index[1]
    halves(g0, w_out[...], NN, keep0, send0, half)
    halves(g1, w_out[...], NN, keep1, send1, half)


def cross_back_body(index, hm, ho, q, k, v, lse, w, wo, h_full, dq_ref, dkv, sums, keep, send):
    half = index[1]
    width = q.shape[1]
    place(h_full, hm, ho, half)
    upstream = dot(h_full[...], wo[...], NT).astype(bf16)
    dq, dk, dv = attention_back(q[...], k[...], v[...], lse, upstream, False)
    dq_ref[...] = dq
    dkv[:, :width] = dk
    dkv[:, width:] = dv
    sums[0:1, :] = jnp.sum(dq.astype(f32), axis=0, keepdims=True)
    sums[1:2, :] = jnp.sum(dv.astype(f32), axis=0, keepdims=True)
    halves(dq_ref, w[...], NT, keep, send, half)


def self_back_body(
    seq, index, hm, ho, qkv, lse, w, wo, x0, x1, x2, x3, h_full, dqkv, sums, vsums, keep, send
):
    half = index[1]
    width = wo.shape[0]
    place(h_full, hm, ho, half)
    upstream = dot(h_full[...], wo[...], NT).astype(bf16)
    dq, dk, dv = attention_back(
        qkv[:, :width], qkv[:, width : 2 * width], qkv[:, 2 * width :], lse, upstream, True
    )
    dqkv[:, :width] = dq
    dqkv[:, width : 2 * width] = dk
    dqkv[:, 2 * width :] = dv
    sums[0:1, :] = jnp.sum(dq.astype(f32), axis=0, keepdims=True)
    sums[1:2, :] = jnp.sum(dv.astype(f32), axis=0, keepdims=True)
    count = keep.shape[0]
    other = dot(dqkv[rows_at(1 - half, count), :], w[...], NT)
    send[...] = other.astype(bf16)
    mine = dot(dqkv[rows_at(half, count), :], w[...], NT)
    keep[...] = mine
    normal_m, _ = normalize(pick((x0, x1), seq, index[2]).astype(f32))
    normal_o, _ = normalize(pick((x2, x3), seq, index[2]).astype(f32))
    vsums[0:1, :] = jnp.sum(mine * normal_m, axis=0, keepdims=True) + jnp.sum(
        other * normal_o, axis=0, keepdims=True
    )
    vsums[1:2, :] = jnp.sum(mine, axis=0, keepdims=True) + jnp.sum(other, axis=0, keepdims=True)


def own_body(index, keep0, keep1, recv0, recv1, going, stay):
    own = index[2] == 0
    first = keep0[...] + recv0[...].astype(f32)
    second = keep1[...] + recv1[...].astype(f32)
    going[...] = jnp.where(own, second, first).astype(bf16)
    stay[...] = jnp.where(own, first, second)


def output_body(index, h0, h1, stay, far, vec, out):
    out[...] = (
        jnp.where(index[2] == 0, h0[...], h1[...])
        + stay[...]
        + far[...].astype(f32)
        + vec[8:9, :]
    )


def input_grad_body(index, base0, base1, stay, far, x, vec, out):
    incoming = stay[...] + far[...].astype(f32)
    normal, inverse = normalize(x[...].astype(f32))
    scaled = incoming * vec[0:1, :]
    centered = (
        scaled
        - jnp.mean(scaled, axis=-1, keepdims=True)
        - normal * jnp.mean(scaled * normal, axis=-1, keepdims=True)
    )
    out[...] = jnp.where(index[2] == 0, base0[...], base1[...]) + inverse * centered


def frame_grad_body(index, dkv0, dkv1, w, keep, across, send):
    half, chip = index[1], index[2]
    width = D // 4
    frames = dkv0.shape[0]
    for seq, dkv in enumerate((dkv0, dkv1)):
        for spot in range(2):
            chip_of = (chip + spot) % 2
            row = (seq * 2 + spot) * send.shape[0] // 4
            at = pl.ds(pl.multiple_of((chip_of * 2 + 1 - half) * width, width), width)
            send[row : row + frames, :] = dot(dkv[...], w[at, :], NT).astype(bf16)
            at = pl.ds(pl.multiple_of((chip_of * 2 + half) * width, width), width)
            row = seq * keep.shape[0] // 2
            (across if spot else keep)[row : row + frames, :] = dot(dkv[...], w[at, :], NT).astype(
                keep.dtype
            )


def frame_across_body(index, across, near, going):
    size = across.shape[0] // 2
    for seq in range(2):
        at, other = seq * size, (seq * 2 + 1) * size
        going[at : at + size, :] = (
            across[at : at + size, :].astype(f32) + near[other : other + size, :].astype(f32)
        ).astype(bf16)


def frame_sum_body(index, keep, near, far, out):
    size, width = keep.shape[0] // 2, keep.shape[1]
    tiles = width // 128
    frames = out.shape[0] // 2 // tiles
    for seq in range(2):
        at, other = seq * size, seq * 2 * size
        total = (
            keep[at : at + frames, :].astype(f32)
            + near[other : other + frames, :].astype(f32)
            + far[at : at + frames, :].astype(f32)
        )
        for tile in range(tiles):
            out[pl.ds(2 * tile + seq, frames, stride=2 * tiles), :] = total[:, tile * 128 : tile * 128 + 128]


def position_rel(order, position):
    return sum(bit for i, bit in enumerate(order) if position >> (len(order) - 1 - i) & 1)


def weight_grad_body(order, terms, index, *refs):
    keep, send, scratch = refs[-3:]
    me, half = index[0], index[1]
    places = {position_rel(order, p): p for p in range(8)}
    for rel in (0, 2, 4, 6):
        at = pl.ds(pl.multiple_of(((me ^ rel) // 2) * 256, 256), 256)
        lane = 0
        for low, high, products in terms:
            to = lane + high - low
            total = None
            for left, right, side in products:
                left, right = refs[left], refs[right]
                if side is None:
                    rows = right[:, low:high]
                else:
                    rows = right[rows_at(half if side == 0 else 1 - half, left.shape[0]), low:high]
                part = dot(left[:, at], rows, TN)
                total = part if total is None else total + part
            scratch[0, :, lane:to] = total[:128]
            scratch[1, :, lane:to] = total[128:]
            lane = to
        for low in range(2):
            spot = places[rel + low]
            target = send if spot >= 4 else keep
            target[spot % 4] = scratch[(me % 2) ^ low].astype(bf16)


def halve_body(count, index, *refs):
    for i in range(count):
        keep, recv = refs[2 * i : 2 * i + 2]
        stay, go = refs[2 * count + 2 * i : 2 * count + 2 * i + 2]
        size = stay.shape[0]
        stay[...] = keep[:size].astype(f32) + recv[:size].astype(f32)
        go[...] = (keep[size:].astype(f32) + recv[size:].astype(f32)).astype(bf16)


def cross_end_body(index, keep0, recv0, keep1, recv1, qkv, out, self_out):
    width = qkv.shape[2]
    total = keep0[0] + recv0[0].astype(f32)
    qkv[1] = total[:, :width]
    qkv[2] = total[:, width:]
    total = keep1[0] + recv1[0].astype(f32)
    qkv[0] = total[:, :width]
    out[...] = total[:, width : 2 * width].T
    self_out[...] = total[:, 2 * width :].T


def self_end_body(index, keep0, recv0, keep1, recv1, qkv):
    width = qkv.shape[2]
    total = jnp.concatenate(
        [keep0[0] + recv0[0].astype(f32), keep1[0] + recv1[0].astype(f32)], axis=1
    )
    for i in range(3):
        qkv[i] = total[:, i * width : (i + 1) * width]


def small_body(index, vecs0, vecs1, two0, two1, three0, three1, self0, self1, cross0, cross1, ff0, ff1, out):
    own = index[2] == 0
    two = jnp.where(own, two0[...], two1[...])
    three = jnp.where(own, three0[...], three1[...])
    vecs = vecs0[...] + vecs1[...]
    rows = (
        vecs[0:1], two[0:1], three[0:1],
        vecs[1:2], two[2:3], two[1:2], three[2:3], three[1:2], three[3:4],
    )
    for i, row in enumerate(rows):
        out[i : i + 1, :] = row
    width = self0.shape[1]
    for i, (first, second) in enumerate(((self0, self1), (cross0, cross1))):
        total = first[...] + second[...]
        for j in range(2):
            at = (2 * i + j) * width
            out[9:10, at : at + width] = total[j : j + 1]
    out[10:11, :] = ff0[...] + ff1[...]
    out[11:16, :] = jnp.zeros((5, D), f32)


def biases_body(index, small, vectors, self_bias, cross_bias, ff_bias):
    me = index[0]
    vectors[...] = small[:, pl.ds(pl.multiple_of(me * 128, 128), 128)]
    lane = lax.broadcasted_iota(jnp.int32, (16, D), 1)
    row = lax.broadcasted_iota(jnp.int32, (16, D), 0)
    moves = jnp.where(
        (lax.broadcasted_iota(jnp.int32, (D, 8), 0) & 63)
        == me * 8 + lax.broadcasted_iota(jnp.int32, (D, 8), 1),
        1.0,
        0.0,
    )
    for source, targets in ((9, (self_bias, cross_bias)), (10, (ff_bias,))):
        heads = jnp.where((lane >> 6) == row, small[source : source + 1, :], 0.0)
        got = lax.dot_general(
            heads, moves, NN, precision=lax.Precision.HIGHEST, preferred_element_type=f32
        )
        if len(targets) == 1:
            targets[0][...] = got
        else:
            for i, target in enumerate(targets):
                for j in range(2):
                    target[j] = got[8 * i + 4 * j : 8 * i + 4 * j + 4]


def vectors_body(index, vectors, gains, shifts):
    part = jnp.zeros((16, 32), f32)
    for t in range(4):
        part = jnp.where(index[3] == t, vectors[:, 32 * t : 32 * t + 32], part)
    gains[...] = part[:3]
    shifts[...] = part[3:9]


def ff_grad_body(index, a0, a1, du0, du1, g0, g1, act0, act1, out):
    hidden = du0.shape[1]
    for at in range(0, D, 256):
        to = at + 256
        out[at:to, :hidden] = (
            dot(a0[:, at:to], du0[...], TN) + dot(a1[:, at:to], du1[...], TN)
        ).astype(bf16)
        out[at:to, hidden:] = (
            dot(g0[:, at:to], act0[...], TN) + dot(g1[:, at:to], act1[...], TN)
        ).astype(bf16)


def ff_end_body(index, total, grad_in, grad_out):
    hidden = grad_in.shape[1]
    grad_in[...] = total[:, :hidden].astype(f32)
    grad_out[...] = total[:, hidden:].astype(f32).T


def untangle_body(index, tangled, first, second):
    frames = first.shape[0]
    row = lax.broadcasted_iota(jnp.int32, (256, 256), 0)
    column = lax.broadcasted_iota(jnp.int32, (256, 256), 1)
    group = row // 16
    source = (row % 16) * 16 + 2 * (group % 8) + group // 8
    moves = jnp.where(source == column, 1.0, 0.0).astype(bf16)
    for frame in range(0, frames, 16):
        n = min(16, frames - frame)
        block = dot(moves[:, : 16 * n], tangled[16 * frame : 16 * (frame + n), :]).astype(bf16)
        for seq, target in enumerate((first, second)):
            for tile in range(8):
                at = (seq * 8 + tile) * 16
                target[frame : frame + n, tile * 128 : tile * 128 + 128] = block[at : at + n]


def permute_by(value, axis, bit):
    size = lax.axis_size(axis)
    return lax.ppermute(value, axis, [(i, i ^ bit) for i in range(size)])


class Gather:
    def __init__(self, line, shard, split, *after):
        self.line, self.split = line, split
        self.shard = self.pinned(shard, after)
        self.got = permute_by(self.shard, "fsdp", GATHER_A[0])

    @staticmethod
    def pinned(value, after):
        return lax.optimization_barrier((value, after))[0] if after else value

    def second(self, *after):
        got = self.pinned(self.got, after)
        cuts = slice(0, self.split), slice(self.split, None)
        self.near = [jnp.stack([self.shard[cut], got[cut]]) for cut in cuts]
        self.far = [
            permute_by(near, "fsdp", order[1]) for near, order in zip(self.near, (GATHER_A, GATHER_B))
        ]

    def third(self, *after):
        far = self.pinned(self.far, after)
        self.pieces = []
        for near, part, order in zip(self.near, far, (GATHER_A, GATHER_B)):
            self.pieces += [near, part, permute_by(jnp.concatenate([near, part]), "fsdp", order[2])]
        self.line.away(*self.pieces)


class Sum:
    def __init__(self, line, *parts):
        self.line = line
        self.keeps = [keep for keep, _, _ in parts]
        self.orders = [order for _, _, order in parts]
        self.number = 0
        self.send([send for _, send, _ in parts])

    def send(self, sends):
        self.recvs = [
            permute_by(send, "fsdp", order[self.number]) for send, order in zip(sends, self.orders)
        ]
        self.line.away(*self.recvs)
        self.number += 1

    def step(self):
        outs, args = [], []
        for keep, recv in zip(self.keeps, self.recvs):
            half = (keep.shape[0] // 2, *keep.shape[1:])
            outs += [struct(half, f32), struct(half, bf16)]
            args += [keep, recv]
        got = call(
            functools.partial(halve_body, len(self.keeps)), "halve", tuple(outs), self.line, *args,
        )
        self.keeps = got[::2]
        self.send(got[1::2])

    def end(self, body, name, outs, *others):
        args = [
            a for one in (self, *others) for pair in zip(one.keeps, one.recvs) for a in pair
        ]
        return call(body, name, outs, self.line, *args, far=range(len(outs)))


def rels_of(order):
    b1, b2, b3 = order
    return ((0, b1), (b2, b2 ^ b1), (b3, b3 ^ b1, b3 ^ b2, b3 ^ b2 ^ b1))


GATHER_A, GATHER_B = (4, 2, 1), (4, 1, 2)
SUM_A, SUM_B = (1, 2, 4), (2, 1, 4)


def shards(
    fast,
    layer_input,
    encoder_states,
    out_grad,
    self_qkv,
    self_bias,
    self_out,
    cross_qkv,
    cross_bias,
    cross_out,
    ff_in,
    ff_bias,
    ff_out,
    norm_gains,
    shifts,
):
    tensor = lax.axis_size("tensor")
    fsdp_size = lax.axis_size("fsdp")
    t = lax.axis_index("tensor")
    me = lax.axis_index("fsdp")
    local_rows = layer_input.shape[0]
    seqs, frames, _ = encoder_states.shape
    length = local_rows * tensor // seqs
    count = length // 2
    width = self_qkv.shape[2]
    heads = width // HD
    hidden = ff_in.shape[1]
    step = tensor // 4
    half = (t // step) % 2
    chip = t // (tensor // 2)
    line = Line(jnp.stack([me, half, chip, t]).astype(jnp.int32))
    group = [[i for i in range(tensor) if (i // step) % 2 == side] for side in range(2)]

    def partner(value):
        return permute_by(value, "tensor", step)

    def rows_of_all(own):
        if fast:
            across = permute_by(own, "tensor", 2)
            return own, across, partner(own), partner(across)
        whole = lax.all_gather(own, "tensor", axis=0, tiled=True).reshape(seqs, 2, count, D)
        return tuple(
            lax.dynamic_index_in_dim(
                lax.dynamic_index_in_dim(whole, seq, 0, False), side, 0, False
            )
            for side in (half, 1 - half)
            for seq in (chip, 1 - chip)
        )

    class Exchange:
        def __init__(self, keep, send):
            self.keep, self.recv = keep, partner(send)

        def go(self):
            keep, recv = self.keep, self.recv
            if fast:
                going = (keep + recv.astype(f32)).astype(bf16)
                line.wait(going)
                self.terms = keep, recv, permute_by(going, "tensor", 2)
            else:
                total = lax.psum(keep + recv.astype(f32), "tensor", axis_index_groups=group)
                self.terms = total, jnp.zeros_like(recv), jnp.zeros_like(recv)
            return self.terms

    def own_of(first, second):
        return jnp.where(chip == 0, first, second)

    def own_rows(first, second):
        return lax.dynamic_slice_in_dim(
            own_of(first, second), (t % step) * local_rows, local_rows, 0
        )

    def own_sum(keep0, keep1, send0, send1):
        terms = [Exchange(k, s).go() for k, s in ((keep0, send0), (keep1, send1))]
        stay, near, far = (own_rows(a, b) for a, b in zip(*terms))
        return stay + near.astype(f32), far

    def own_terms(keep0, keep1, recv0, recv1):
        going, stay = call(
            own_body, "own", (struct(recv0.shape, bf16), struct(recv0.shape, f32)), line,
            keep0, keep1, recv0, recv1,
        )
        return stay, permute_by(going, "tensor", 2)

    rels_a, rels_b = rels_of(GATHER_A), rels_of(GATHER_B)
    packed_rows = jnp.concatenate([norm_gains, shifts], 0)
    packed_bias = jnp.concatenate(
        [self_bias.reshape(-1, HD // fsdp_size), cross_bias.reshape(-1, HD // fsdp_size), ff_bias],
        0,
    )
    if fast:
        extra = jnp.concatenate(
            [
                jnp.pad(packed_rows, ((0, 32 - packed_rows.shape[0]), (0, 0))),
                jnp.pad(packed_bias, ((0, 0), (0, 128 - packed_bias.shape[1]))),
            ],
            1,
        )

        def beside(out):
            return jnp.concatenate([out[:128], out[128:]], 1)

        packed = jnp.concatenate(
            [self_qkv.reshape(3 * 128, width), beside(self_out), extra], 0
        )
        self_w = Gather(line, packed, 256)
        (x_own, g_own), _ = lax.optimization_barrier(((layer_input, out_grad), self_w.got))
        packed = jnp.concatenate(
            [cross_qkv[1], cross_qkv[2], cross_qkv[0], beside(cross_out)], 0
        )
        tiles = hidden // 128
        packed_ff = jnp.concatenate(
            [
                ff_in.reshape(128, tiles, 128).transpose(1, 0, 2),
                ff_out.reshape(tiles, 128, 128),
            ],
            0,
        )
        self_w.second()
        x_rows = rows_of_all(x_own)
        cross_w = Gather(line, packed, 256, self_w.far)
        g_own, _ = lax.optimization_barrier((g_own, x_rows[2]))
        g_rows = rows_of_all(g_own)
        line.wait(self_w.far)
        tangled = encoder_states.reshape(2, frames, 8, 128).transpose(1, 2, 0, 3).reshape(-1, 128)
        line.away(tangled, *x_rows, *g_rows)
        e_seq = call(untangle_body, "untangle", (struct((frames, D), bf16),) * 2, line, tangled)
        self_w.third()
        cross_w.second(e_seq[0])
        ff_w = Gather(line, packed_ff, tiles, e_seq[0])
        line.wait(cross_w.near)
    else:
        x_rows = rows_of_all(layer_input)
        e_seq = [encoder_states[s] for s in range(2)]
        vec = lax.all_gather(packed_rows, "fsdp", axis=1, tiled=True).astype(f32)
        biases = lax.all_gather(packed_bias, "fsdp", axis=1, tiled=True).astype(f32)
        whole = lax.all_gather(self_qkv, "fsdp", axis=1, tiled=True)
        w_self = jnp.concatenate([whole[0], whole[1], whole[2]], 1)
        wo_self = lax.all_gather(self_out, "fsdp", axis=1, tiled=True)
        whole = lax.all_gather(cross_qkv, "fsdp", axis=1, tiled=True)
        w_cross, w_kv = whole[0], jnp.concatenate([whole[1], whole[2]], 1)
        wo_cross = lax.all_gather(cross_out, "fsdp", axis=1, tiled=True)
        w_in = lax.all_gather(ff_in, "fsdp", axis=0, tiled=True)
        w_out = lax.all_gather(ff_out, "fsdp", axis=1, tiled=True)
        bias = jnp.zeros((8, hidden), f32)
        bias = bias.at[:4, :width].set(biases[: 4 * heads].reshape(4, width))
        bias = bias.at[4].set(biases[4 * heads :].reshape(hidden))

    attn_flops = 8 * length * width * 1024
    row_pair = (struct((count, D), f32), struct((count, D), bf16))

    def self_forward(s):
        nonlocal w_self, wo_self, vec, bias
        outs = (
            struct((length, D), bf16),
            struct((length, 3 * width), bf16),
            struct((length, width), bf16),
            struct((length, heads), f32),
            *row_pair,
        )
        kwargs = dict(scratch=(pltpu.VMEM((length, D), bf16),),)
        if fast and s == 0:
            outs += (
                struct((D, 3 * width), bf16),
                struct((width, D), bf16),
                struct((16, D), f32),
                struct((8, D), f32),
            )
            *got, w_self, wo_self, vec, bias = call(
                functools.partial(self_forward_body, (rels_a, rels_b), s),
                "self_forward", outs, line, *x_rows, *self_w.pieces, **kwargs,
            )
        else:
            got = call(
                functools.partial(self_forward_body, None, s),
                "self_forward", outs, line, *x_rows, vec, bias, w_self, wo_self, **kwargs,
            )
        a1[s], qkv1[s], o1[s], lse1[s], *res = got
        sum1[s] = Exchange(*res)

    def frames_in(s):
        nonlocal w_kv
        outs = (struct((frames, width), bf16),) * 2
        flops = 4 * frames * D * width
        if fast and s == 0:
            k2[s], v2[s], w_kv = call(
                functools.partial(frames_body, rels_a),
                "frames_in", outs + (struct((D, 2 * width), bf16),), line, e_seq[s], bias,
                *cross_w.pieces[:3],
            )
        else:
            k2[s], v2[s] = call(
                functools.partial(frames_body, None),
                "frames_in", outs, line, e_seq[s], bias, w_kv,
            )

    def norm_of(rows, seq, base, terms, name):
        return call(
            functools.partial(norm_body, rows, seq),
            name, (struct((count, D), f32), struct((count, D), bf16)), line, *base, *terms, vec,
        )

    def norm_two(s):
        h1[s], mine = norm_of((4, 1, 5), s, x_rows[:2], sum1[s].terms, "norm_two")
        a2_rows[s] = mine, partner(mine)

    def cross_forward(s):
        nonlocal w_cross, wo_cross
        outs = (
            struct((length, D), bf16),
            struct((length, width), bf16),
            struct((length, width), bf16),
            struct((length, heads), f32),
            *row_pair,
        )
        args = (*a2_rows[s], bias, k2[s], v2[s])
        if fast and s == 0:
            *got, w_cross, wo_cross = call(
                functools.partial(cross_forward_body, rels_b), "cross_forward",
                outs + (struct((D, width), bf16), struct((width, D), bf16)),
                line, *args, *cross_w.pieces[3:],
            )
        else:
            got = call(
                functools.partial(cross_forward_body, None), "cross_forward",
                outs, line, *args, w_cross, wo_cross,
            )
        a2[s], q2[s], o2[s], lse2[s], *res = got
        sum2[s] = Exchange(*res)

    def norm_three(s):
        h2[s], mine = norm_of((6, 2, 7), None, (h1[s],), sum2[s].terms, "norm_three")
        a3_rows[s] = mine, partner(mine)

    def feed(s):
        nonlocal w_in, w_out
        outs = (
            struct((length, D), bf16),
            struct((length, D), bf16),
            struct((length, hidden), bf16),
            struct((length, hidden), bf16),
            struct((1, hidden), f32),
            *row_pair,
        )
        args = (*a3_rows[s], *g_rows, bias)
        flops = 6 * length * D * hidden
        if fast and s == 0:
            *got, w_in, w_out = call(
                functools.partial(feed_body, (rels_a, rels_b), s),
                "feed", outs + (struct((D, hidden), bf16), struct((hidden, D), bf16)), line,
                *args, *ff_w.pieces,
            )
        else:
            got = call(
                functools.partial(feed_body, None, s),
                "feed", outs, line, *args, w_in, w_out,
            )
        a3[s], g_full[s], act[s], du[s], ff_sums[s], *res = got
        sum3[s] = Exchange(*res)

    def feed_out():
        return call(
            feed_out_body, "feed_out",
            (*[row_pair[0]] * 2, *[row_pair[1]] * 2),
            line, act[0], act[1], w_out,
        )

    def norm_back(gain, base, terms, h, name):
        return call(
            functools.partial(norm_back_body, gain),
            name,
            (struct((count, D), f32), struct((count, D), bf16), struct((8, D), f32)),
            line, base, *terms, h, vec,
        )

    def norm_three_back(s):
        dh2[s], low, sums3[s] = norm_back(2, g_full[s], sum3[s].terms, h2[s], "norm_three_back")
        h2_rows[s] = low, partner(low)

    def cross_back(s):
        outs = (
            struct((length, D), bf16),
            struct((length, width), bf16),
            struct((frames, 2 * width), bf16),
            struct((2, width), f32),
            *row_pair,
        )
        h2_full[s], dq2[s], dkv2[s], cross_sums[s], *res = call(
            cross_back_body, "cross_back", outs, line,
            *h2_rows[s], q2[s], k2[s], v2[s], lse2[s], w_cross, wo_cross,
        )
        sum4[s] = Exchange(*res)

    def norm_two_back(s):
        dh1[s], low, sums2[s] = norm_back(1, dh2[s], sum4[s].terms, h1[s], "norm_two_back")
        h1_rows[s] = low, partner(low)

    def self_back(s):
        outs = (
            struct((length, D), bf16),
            struct((length, 3 * width), bf16),
            struct((2, width), f32),
            struct((2, D), f32),
            *row_pair,
        )
        h1_full[s], dqkv1[s], self_sums[s], vec_sums[s], *res5[s] = call(
            functools.partial(self_back_body, s), "self_back", outs, line,
            *h1_rows[s], qkv1[s], lse1[s], w_self, wo_self, *x_rows,
        )

    def weight_grad(terms, order, name):
        operands, table, n = [], [], 0
        for lefts, rights, span in terms:
            low, high = span or (0, rights[0].shape[1])
            products = []
            for left, right in zip(lefts, rights):
                sides = [(left, None)] if not isinstance(left, tuple) else list(zip(left, (0, 1)))
                for part, side in sides:
                    products.append((len(operands), len(operands) + 1, side))
                    operands += [part, right]
            table.append((low, high, products))
            n += high - low
        got = call(
            functools.partial(weight_grad_body, order, table),
            name,
            (struct((4, 128, n), bf16), struct((4, 128, n), bf16)),
            line,
            *operands,

            scratch=(pltpu.VMEM((2, 128, n), f32),),
        )
        return (*got, order)

    def plain_grad(lefts, rights):
        return sum(dot(a, b, TN) for a, b in zip(lefts, rights))

    def frame_grad():
        padded = -(-frames // 16) * 16
        keep, across, send = call(
            frame_grad_body, "frame_grad",
            (
                struct((2 * padded, D // 4), bf16),
                struct((2 * padded, D // 4), bf16),
                struct((4 * padded, D // 4), bf16),
            ),
            line, dkv2[0], dkv2[1], w_kv,
        )
        return keep, across, partner(send)

    def frame_go(keep, across, near):
        (going,) = call(
            frame_across_body, "frame_across", (struct(across.shape, bf16),), line, across, near
        )
        return keep, near, permute_by(going, "tensor", 2)

    (
        a1, qkv1, o1, lse1, sum1, h1, k2, v2, a2_rows, a2, q2, o2, lse2, sum2, h2, a3_rows, a3, g_full,
        act, du, ff_sums, sum3, dh2, sums3, h2_rows, h2_full, dq2, dkv2, cross_sums, sum4, dh1, sums2,
        h1_rows, h1_full, dqkv1, self_sums, vec_sums, res5,
    ) = ([None] * 2 for _ in range(38))
    rows_struct = (struct((local_rows, D), f32),)

    def output():
        pair = h2 if fast else [own_rows(*h2)] * 2
        return call(output_body, "output", rows_struct, line, *pair, *out_terms, vec, far=(0,))[0]

    def input_gradient():
        pair = dh1 if fast else [own_rows(*dh1)] * 2
        args = (*pair, *terms, layer_input, vec)
        return call(input_grad_body, "input_grad", rows_struct, line, *args, far=(0,))[0]

    if not fast:
        g_rows = rows_of_all(out_grad)
        for stage, sums in (
            (self_forward, sum1), (frames_in, None), (norm_two, None), (cross_forward, sum2), (norm_three, None),
            (feed, sum3), (norm_three_back, None), (cross_back, sum4), (norm_two_back, None), (self_back, None),
        ):
            for s in range(2):
                stage(s)
                if sums:
                    sums[s].go()
        out_terms = own_sum(*feed_out())
        terms = own_sum(res5[0][0], res5[1][0], res5[0][1], res5[1][1])
        layer_output, input_grad = output(), input_gradient()
    else:
        w_self = wo_self = w_kv = w_cross = wo_cross = w_in = w_out = vec = bias = None
        self_forward(0)
        cross_w.third(a1[0])
        self_forward(1)
        sum1[0].go()
        frames_in(0)
        sum1[1].go()
        ff_w.second(k2[0])
        norm_two(0)
        cross_forward(0)
        line.wait(ff_w.far)
        frames_in(1)
        norm_two(1)
        sum2[0].go()
        ff_w.third(k2[1])
        cross_forward(1)
        line.wait(ff_w.pieces)
        norm_three(0)
        sum2[1].go()
        feed(0)
        norm_three(1)
        sum3[0].go()
        feed(1)
        out_parts = feed_out()
        out_recv = partner(out_parts[2]), partner(out_parts[3])
        norm_three_back(0)
        sum3[1].go()
        (ff_parts,) = call(
            ff_grad_body, "ff_grad", (struct((D, 2 * hidden), bf16),), line,
            *a3, *du, *g_full, *act, far=(0,),
        )
        ff_total = lax.psum_scatter(ff_parts, "fsdp", scatter_dimension=0, tiled=True)
        out_terms = own_terms(*out_parts[:2], *out_recv)
        cross_back(0)
        line.wait(out_terms[1])
        norm_three_back(1)
        sum4[0].go()
        layer_output = output()
        cross_back(1)
        norm_two_back(0)
        sum4[1].go()
        frame_terms = frame_grad()
        kv_sum = Sum(line, weight_grad([(e_seq, dkv2, None)], SUM_A, "cross_grad"))
        frame_terms = frame_go(*frame_terms)
        self_back(0)
        end0 = partner(res5[0][1])
        norm_two_back(1)
        cross_sum = Sum(
            line,
            weight_grad(
                [(a2, dq2, None), (h2_full, o2, None), ((h1_full[0], h1_rows[1]), o1, None)],
                SUM_A,
                "cross_grad_b",
            ),
        )
        kv_sum.step()
        self_back(1)
        end1 = partner(res5[1][1])
        split = 3 * width // 2
        self_parts = (
            weight_grad([(a1, dqkv1, (0, split))], SUM_A, "self_grad"),
            weight_grad([(a1, dqkv1, (split, 3 * width))], SUM_B, "self_grad_b"),
        )
        self_sum = Sum(line, *self_parts)
        terms = own_terms(res5[0][0], res5[1][0], end0, end1)
        kv_sum.step()
        (small,) = call(
            small_body, "small", (struct((16, D), f32),), line,
            *vec_sums, *sums2, *sums3, *self_sums, *cross_sums, *ff_sums,
        )
        pair = permute_by(small, "fsdp", 1)
        cross_sum.step()
        tiles = D // 4 // 128
        (rows,) = call(
            frame_sum_body, "frame_sum", (struct((frames * 2 * tiles, 128), f32),), line, *frame_terms, far=(0,),
        )
        small = small + pair
        line.wait(small)
        pair = permute_by(small, "fsdp", 2)
        self_sum.step()
        input_grad = input_gradient()
        small = small + pair
        line.wait(small)
        pair = permute_by(small, "fsdp", 4)
        cross_sum.step()
        ff_in_grad, ff_out_grad = call(
            ff_end_body, "ff_end", (struct((128, hidden), f32), struct((hidden, 128), f32)), line,
            ff_total, far=(0, 1),
        )
        self_sum.step()
        small = small + pair
        vectors, self_bias_grad, cross_bias_grad, ff_bias_grad = call(
            biases_body, "biases",
            (
                struct((16, 128), f32),
                struct((2, heads, 8), f32),
                struct((2, heads, 8), f32),
                struct((hidden // HD, 8), f32),
            ),
            line, small, far=(1, 2, 3),
        )
        vectors = vectors + permute_by(vectors, "tensor", 1)
        vectors = vectors + permute_by(vectors, "tensor", 2)

    if fast:
        cross_qkv_grad, cross_out_grad, self_out_grad = kv_sum.end(
            cross_end_body,
            "cross_end",
            (
                struct((3, 128, width), f32),
                struct((width, 128), f32),
                struct((width, 128), f32),
            ),
            cross_sum,
        )
        encoder_grad = (
            rows.reshape(frames, tiles, 2, 128).transpose(2, 0, 1, 3).reshape(2, frames, D // 4)
        )
        (self_qkv_grad,) = self_sum.end(self_end_body, "self_end", (struct((3, 128, width), f32),))
        gains_grad, shifts_grad = call(
            vectors_body, "vectors", (struct((3, 32), f32), struct((6, 32), f32)), line, vectors,
            far=(0, 1),
        )
    else:
        part = jnp.stack([dot(dkv2[s], w_kv, NT) for s in range(2)])
        encoder_grad = lax.psum_scatter(part, "tensor", scatter_dimension=2, tiled=True)

        def scattered(part, dimension):
            return lax.psum_scatter(part, "fsdp", scatter_dimension=dimension, tiled=True)

        counts = (t % step) == 0

        def vector(sums, row):
            return jnp.where(counts, own_of(sums[0][row], sums[1][row]), 0.0)

        vectors = jnp.stack(
            [
                vec_sums[0][0] + vec_sums[1][0],
                vector(sums2, 0),
                vector(sums3, 0),
                vec_sums[0][1] + vec_sums[1][1],
                vector(sums2, 2),
                vector(sums2, 1),
                vector(sums3, 2),
                vector(sums3, 1),
                vector(sums3, 3),
            ]
        )
        bias_sums = jnp.concatenate(
            [
                self_sums[0] + self_sums[1],
                cross_sums[0] + cross_sums[1],
                (ff_sums[0] + ff_sums[1]).reshape(-1, width),
            ],
            0,
        ).reshape(-1, HD)
        vectors = scattered(vectors, 1)
        vectors = lax.psum_scatter(vectors, "tensor", scatter_dimension=1, tiled=True)
        bias_sums = scattered(bias_sums, 1)
        ff_in_grad = scattered(plain_grad(a3, du), 0)
        ff_out_grad = scattered(plain_grad(act, g_full), 1)
        cross_out_grad = scattered(plain_grad(o2, h2_full), 1)
        kv_grad = plain_grad(e_seq, dkv2)
        cross_qkv_grad = scattered(
            jnp.stack([plain_grad(a2, dq2), kv_grad[:, :width], kv_grad[:, width:]]), 1
        )
        self_out_grad = scattered(plain_grad(o1, h1_full), 1)
        qkv_grad = scattered(plain_grad(a1, dqkv1), 0)
        self_qkv_grad = jnp.stack([qkv_grad[:, i * width : (i + 1) * width] for i in range(3)])
        piece = HD // fsdp_size
        self_bias_grad = bias_sums[: 2 * heads].reshape(2, heads, piece)
        cross_bias_grad = bias_sums[2 * heads : 4 * heads].reshape(2, heads, piece)
        ff_bias_grad = bias_sums[4 * heads :]
        gains_grad, shifts_grad = vectors[:3], vectors[3:]
    return (
        layer_output,
        input_grad,
        encoder_grad,
        self_qkv_grad,
        self_bias_grad,
        self_out_grad,
        cross_qkv_grad,
        cross_bias_grad,
        cross_out_grad,
        ff_in_grad,
        ff_bias_grad,
        ff_out_grad,
        gains_grad,
        shifts_grad,
    )


def solution(mesh):
    fast = mesh.shape["fsdp"] == 8 and mesh.shape["tensor"] == 4
    return jax.shard_map(
        functools.partial(shards, fast),
        mesh=mesh,
        in_specs=(
            P(("fsdp", "tensor"), None),
            P("fsdp", None, None),
            P(("fsdp", "tensor"), None),
            P(None, "fsdp", "tensor"),
            P(None, "tensor", "fsdp"),
            P("tensor", "fsdp"),
            P(None, "fsdp", "tensor"),
            P(None, "tensor", "fsdp"),
            P("tensor", "fsdp"),
            P("fsdp", "tensor"),
            P("tensor", "fsdp"),
            P("tensor", "fsdp"),
            P(None, "fsdp"),
            P(None, "fsdp"),
        ),
        out_specs=(
            P(("fsdp", "tensor"), None),
            P(("fsdp", "tensor"), None),
            P("fsdp", None, "tensor"),
            P(None, "fsdp", "tensor"),
            P(None, "tensor", "fsdp"),
            P("tensor", "fsdp"),
            P(None, "fsdp", "tensor"),
            P(None, "tensor", "fsdp"),
            P("tensor", "fsdp"),
            P("fsdp", "tensor"),
            P("tensor", "fsdp"),
            P("tensor", "fsdp"),
            P(None, ("fsdp", "tensor")),
            P(None, ("fsdp", "tensor")),
        ),
        check_vma=False,
    )
```

```python
import functools
import math

import jax
import jax.numpy as jnp
from jax import lax
from jax.experimental import pallas as pl
from jax.experimental.pallas import tpu as pltpu
from jax.sharding import PartitionSpec as P

D = 1024
HD = 64
f32 = jnp.float32
bf16 = jnp.bfloat16
NN = (((1,), (0,)), ((), ()))
NT = (((1,), (1,)), ((), ()))
TN = (((0,), (0,)), ((), ()))
MIB = 2**20


def dot(left, right, dims=NN):
    return lax.dot_general(left, right, dims, preferred_element_type=f32)


def struct(shape, dtype):
    return jax.ShapeDtypeStruct(shape, dtype)


class Line:
    def __init__(self, index):
        self.index = index
        self.kept = {}

    def wait(self, *values):
        self.index, _ = lax.optimization_barrier((self.index, values))

    def away(self, *values):
        for value in values:
            self.kept[id(value)] = value


KERNELS = {
    "untangle": (16, 0.3),
    "self_forward": (14, 0.3),
    "frames_in": (12, 0.3),
    "norm_two": (8, 4),
    "norm_three": (8, 4),
    "cross_forward": (20, 0.3),
    "feed": (22, 0.3),
    "feed_out": (12, 0.3),
    "ff_grad": (20, 0.3),
    "norm_three_back": (10, 4),
    "norm_two_back": (10, 4),
    "cross_back": (24, 0.3),
    "self_back": (16, 0.3),
    "cross_grad": (18, 0.3),
    "cross_grad_b": (18, 0.3),
    "self_grad": (10, 0.3),
    "self_grad_b": (12, 0.3),
    "frame_grad": (16, 0.3),
    "frame_sum": (20, 0.3),
    "halve": (12, 0.3),
    "input_grad": (8, 0.3),
    "ff_end": (8, 0.3),
    "cross_end": (8, 0.3),
    "self_end": (8, 0.3),
    "own": (8, 0.3),
    "output": (8, 0.3),
    "vectors": (8, 0.3),
    "frame_across": (12, 0.3),
    "small": (8, 0.3),
}


def call(body, name, outs, line, *args, far=(), scratch=()):
    grant, time = KERNELS[name]
    vm = pl.BlockSpec(memory_space=pltpu.VMEM)
    args = [
        pltpu.with_memory_space_constraint(a, pltpu.HBM) if id(a) in line.kept else a for a in args
    ]
    got = pl.pallas_call(
        body,
        name=name,
        out_shape=tuple(
            (pltpu.HBM if i in far else pltpu.VMEM)(out.shape, out.dtype)
            for i, out in enumerate(outs)
        ),
        in_specs=[pl.BlockSpec(memory_space=pltpu.SMEM)] + [vm] * len(args),
        out_specs=tuple(vm for _ in outs),
        scratch_shapes=scratch,
        compiler_params=pltpu.CompilerParams(vmem_limit_bytes=grant * MIB),
        cost_estimate=pl.CostEstimate(
            flops=int(time * 1.15e9), bytes_accessed=int(time * 3.69e6), transcendentals=0
        ),
    )(line.index, *args)
    line.away(*(got[i] for i in far))
    line.wait(got[-1])
    return got


def rows_at(half, count):
    return pl.ds(pl.multiple_of(half * count, 32), count)


def place(target, mine, other, half):
    count = mine.shape[0]
    target[rows_at(half, count), :] = mine[...]
    target[rows_at(1 - half, count), :] = other[...]


def pick(pair, seq, chip):
    near, far = pair
    return jnp.where(chip == seq, near[...].astype(f32), far[...].astype(f32)).astype(near.dtype)


def place_of(target, rows, seq, half, chip):
    count = rows[0].shape[0]
    target[rows_at(half, count), :] = pick(rows[:2], seq, chip)
    target[rows_at(1 - half, count), :] = pick(rows[2:], seq, chip)


def normalize(v):
    center = v - jnp.mean(v, axis=-1, keepdims=True)
    inverse = lax.rsqrt(jnp.mean(center * center, axis=-1, keepdims=True) + 1e-05)
    return center * inverse, inverse


def spots(pieces, rels, me):
    for piece, group in zip(pieces, rels):
        for spot, rel in enumerate(group):
            yield piece.at[spot], me ^ rel, pl.ds(pl.multiple_of((me ^ rel) * 128, 128), 128)


def head_masks(width):
    lane = lax.broadcasted_iota(jnp.int32, (1, width), 1) // HD
    return [lane == h for h in range(width // HD)]


def causal_mask(length):
    return lax.broadcasted_iota(jnp.int32, (length, length), 0) >= lax.broadcasted_iota(
        jnp.int32, (length, length), 1
    )


def attention(q, k, v, lse_ref, causal):
    total = jnp.zeros(q.shape, f32)
    q = (q.astype(f32) * HD**-0.5).astype(bf16)
    allowed = causal_mask(q.shape[0]) if causal else None
    for h, mask in enumerate(head_masks(q.shape[1])):
        scores = dot(jnp.where(mask, q, 0), k, NT)
        if causal:
            scores = jnp.where(allowed, scores, -1e30)
        highest = jnp.max(scores, axis=1, keepdims=True)
        weight = jnp.exp(scores - highest)
        norm = jnp.sum(weight, axis=1, keepdims=True)
        total += dot(weight.astype(bf16), jnp.where(mask, v, 0)) * (1.0 / norm)
        lse_ref[:, h : h + 1] = highest + jnp.log(norm)
    return total.astype(bf16)


def attention_back(q, k, v, lse_ref, upstream, causal):
    dq = jnp.zeros(q.shape, f32)
    dk = jnp.zeros(k.shape, f32)
    dv = jnp.zeros(k.shape, f32)
    q = (q.astype(f32) * HD**-0.5).astype(bf16)
    allowed = causal_mask(q.shape[0]) if causal else None
    for h, mask in enumerate(head_masks(q.shape[1])):
        query, above = jnp.where(mask, q, 0), jnp.where(mask, upstream, 0)
        scores = dot(query, k, NT)
        if causal:
            scores = jnp.where(allowed, scores, -1e30)
        prob = jnp.exp(scores - lse_ref[:, h : h + 1])
        dprob = dot(above, v, NT)
        delta = jnp.sum(prob * dprob, axis=1, keepdims=True)
        dscore = (prob * (dprob - delta)).astype(bf16)
        dv += dot(prob.astype(bf16), above, TN)
        dk += dot(dscore, query, TN)
        dq += dot(dscore, jnp.where(mask, k, 0))
    return (dq * HD**-0.5).astype(bf16), dk.astype(bf16), dv.astype(bf16)


def halves(rows_ref, weight, dims, keep, send, half):
    count = keep.shape[0]
    send[...] = dot(rows_ref[rows_at(1 - half, count), :], weight, dims).astype(bf16)
    keep[...] = dot(rows_ref[rows_at(half, count), :], weight, dims)


def join_out(wo, piece, at):
    wo[:128, at] = piece[128:256, :128]
    wo[128:, at] = piece[128:256, 128:]


def join_small(vec, bias, pieces, rels, me):
    lane = lax.broadcasted_iota(jnp.int32, (128, D), 1)
    spot_of = lax.broadcasted_iota(jnp.int32, (128, D), 0)
    total = jnp.zeros((32, D), f32)
    for piece, owner, at in spots(pieces, rels, me):
        vec[:, at] = piece[256:272, :128].astype(f32)
        moves = jnp.where(((lane & 63) == owner * 8 + spot_of) & (spot_of < 8), 1.0, 0.0)
        total += dot(piece[256:288, 128:], moves.astype(bf16))
    row = lax.broadcasted_iota(jnp.int32, (32, D), 0)
    head = lax.broadcasted_iota(jnp.int32, (32, D), 1) >> 6
    total = jnp.where(head == jnp.where(row < 16, row & 3, row - 16), total, 0.0).astype(bf16)
    kind = lax.broadcasted_iota(jnp.int32, (8, 32), 0)
    row = lax.broadcasted_iota(jnp.int32, (8, 32), 1)
    moves = jnp.where(kind == jnp.where(row < 16, row >> 2, 4), 1.0, 0.0).astype(bf16)
    bias[...] = dot(moves, total)


def self_forward_body(rels, seq, index, x0, x1, x2, x3, *refs):
    if rels is None:
        vec, bias, w, wo, a_ref, qkv, o_ref, lse, keep, send, xs = refs
    else:
        pieces, (a_ref, qkv, o_ref, lse, keep, send, w, wo, vec, bias, xs) = refs[:6], refs[6:]
        me, wide = index[0], wo.shape[0]
        for piece, _, at in spots(pieces[:3], rels[0], me):
            w[at, :wide] = piece[:128, :]
            w[at, wide : 2 * wide] = piece[128:, :]
        for piece, _, at in spots(pieces[3:], rels[1], me):
            w[at, 2 * wide :] = piece[:128, :]
            join_out(wo, piece, at)
        join_small(vec, bias, pieces[3:], rels[1], me)
    half = index[1]
    width = wo.shape[0]
    place_of(xs, (x0, x1, x2, x3), seq, half, index[2])
    normal, _ = normalize(xs[...].astype(f32))
    a = (normal * vec[0:1, :] + vec[3:4, :]).astype(bf16)
    a_ref[...] = a
    qkv[:, :width] = (dot(a, w[:, :width]) + bias[0:1, :width]).astype(bf16)
    qkv[:, width : 2 * width] = dot(a, w[:, width : 2 * width]).astype(bf16)
    qkv[:, 2 * width :] = (dot(a, w[:, 2 * width :]) + bias[1:2, :width]).astype(bf16)
    o_ref[...] = attention(
        qkv[:, :width], qkv[:, width : 2 * width], qkv[:, 2 * width :], lse, True
    )
    halves(o_ref, wo[...], NN, keep, send, half)


def frames_body(rels, index, e, bias, *refs):
    if rels is None:
        w, k, v = refs
        width = k.shape[1]
    else:
        pieces, (k, v, w) = refs[:3], refs[3:]
        width = k.shape[1]
        for piece, _, at in spots(pieces, rels, index[0]):
            w[at, :width] = piece[:128, :]
            w[at, width:] = piece[128:, :]
    k[...] = dot(e[...], w[:, :width]).astype(bf16)
    v[...] = (dot(e[...], w[:, width:]) + bias[3:4, :width]).astype(bf16)


def cross_forward_body(rels, index, am, ao, bias, k, v, *refs):
    if rels is None:
        w, wo, a_ref, q_ref, o_ref, lse, keep, send = refs
    else:
        pieces, (a_ref, q_ref, o_ref, lse, keep, send, w, wo) = refs[:3], refs[3:]
        for piece, _, at in spots(pieces, rels, index[0]):
            w[at, :] = piece[:128, :]
            join_out(wo, piece, at)
    half = index[1]
    place(a_ref, am, ao, half)
    q_ref[...] = (dot(a_ref[...], w[...]) + bias[2:3, : w.shape[1]]).astype(bf16)
    o_ref[...] = attention(q_ref[...], k[...], v[...], lse, False)
    halves(o_ref, wo[...], NN, keep, send, half)


def norm_body(rows, seq, index, *refs):
    shift, gain, bias = rows
    if seq is None:
        base, keep, recv, far, vec, h_ref, a_ref = refs
        start = base[...]
    else:
        near, across, keep, recv, far, vec, h_ref, a_ref = refs
        start = pick((near, across), seq, index[2])
    h = (
        start.astype(f32)
        + keep[...]
        + recv[...].astype(f32)
        + far[...].astype(f32)
        + vec[shift : shift + 1, :]
    )
    h_ref[...] = h
    normal, _ = normalize(h)
    a_ref[...] = (normal * vec[gain : gain + 1, :] + vec[bias : bias + 1, :]).astype(bf16)


def norm_back_body(gain, index, base, keep, recv, far, h, vec, dh_ref, low_ref, sums):
    incoming = keep[...] + recv[...].astype(f32) + far[...].astype(f32)
    normal, inverse = normalize(h[...].astype(f32))
    sums[...] = jnp.zeros(sums.shape, f32)
    sums[0:1, :] = jnp.sum(incoming * normal, axis=0, keepdims=True)
    sums[1:2, :] = jnp.sum(incoming, axis=0, keepdims=True)
    scaled = incoming * vec[gain : gain + 1, :]
    centered = (
        scaled
        - jnp.mean(scaled, axis=-1, keepdims=True)
        - normal * jnp.mean(scaled * normal, axis=-1, keepdims=True)
    )
    count = keep.shape[0]
    above = (base[...] if base.shape[0] == count else base[rows_at(index[1], count), :]).astype(f32)
    dh = above + inverse * centered
    dh_ref[...] = dh
    low_ref[...] = dh.astype(bf16)
    sums[2:3, :] = jnp.sum(dh, axis=0, keepdims=True)
    sums[3:4, :] = jnp.sum(above, axis=0, keepdims=True)


def feed_body(rels, seq, index, am, ao, y0, y1, y2, y3, bias, *refs):
    if rels is None:
        w_in, w_out, a_ref, g_full, g_ref, du_ref, sums, keep, send = refs
    else:
        pieces, (a_ref, g_full, g_ref, du_ref, sums, keep, send, w_in, w_out) = refs[:6], refs[6:]
        for piece, _, at in spots(pieces[:3], rels[0], index[0]):
            for tile in range(w_in.shape[1] // 128):
                w_in[at, tile * 128 : tile * 128 + 128] = piece[tile]
        for piece, _, at in spots(pieces[3:], rels[1], index[0]):
            for tile in range(w_in.shape[1] // 128):
                w_out[tile * 128 : tile * 128 + 128, at] = piece[tile]
    half = index[1]
    place(a_ref, am, ao, half)
    place_of(g_full, (y0, y1, y2, y3), seq, half, index[2])
    hidden = w_in.shape[1]
    step = min(512, hidden)
    for at in range(0, hidden, step):
        to = at + step
        u = dot(a_ref[...], w_in[:, at:to]) + bias[4:5, at:to]
        dg = dot(g_full[...], w_out[at:to, :], NT)
        cdf = 0.5 * (1.0 + lax.erf(u * 0.7071067811865476))
        g_ref[:, at:to] = (u * cdf).astype(bf16)
        slope = cdf + u * (jnp.exp(-0.5 * u * u) * 0.3989422804014327)
        du = (dg * slope).astype(bf16)
        du_ref[:, at:to] = du
        sums[:, at:to] = jnp.sum(du.astype(f32), axis=0, keepdims=True)
    halves(du_ref, w_in[...], NT, keep, send, half)


def feed_out_body(index, g0, g1, w_out, keep0, keep1, send0, send1):
    half = index[1]
    halves(g0, w_out[...], NN, keep0, send0, half)
    halves(g1, w_out[...], NN, keep1, send1, half)


def cross_back_body(index, hm, ho, q, k, v, lse, w, wo, h_full, dq_ref, dkv, sums, keep, send):
    half = index[1]
    width = q.shape[1]
    place(h_full, hm, ho, half)
    upstream = dot(h_full[...], wo[...], NT).astype(bf16)
    dq, dk, dv = attention_back(q[...], k[...], v[...], lse, upstream, False)
    dq_ref[...] = dq
    dkv[:, :width] = dk
    dkv[:, width:] = dv
    sums[0:1, :] = jnp.sum(dq.astype(f32), axis=0, keepdims=True)
    sums[1:2, :] = jnp.sum(dv.astype(f32), axis=0, keepdims=True)
    halves(dq_ref, w[...], NT, keep, send, half)


def self_back_body(
    seq, index, hm, ho, qkv, lse, w, wo, x0, x1, x2, x3, h_full, dqkv, sums, vsums, keep, send
):
    half = index[1]
    width = wo.shape[0]
    place(h_full, hm, ho, half)
    upstream = dot(h_full[...], wo[...], NT).astype(bf16)
    dq, dk, dv = attention_back(
        qkv[:, :width], qkv[:, width : 2 * width], qkv[:, 2 * width :], lse, upstream, True
    )
    dqkv[:, :width] = dq
    dqkv[:, width : 2 * width] = dk
    dqkv[:, 2 * width :] = dv
    sums[0:1, :] = jnp.sum(dq.astype(f32), axis=0, keepdims=True)
    sums[1:2, :] = jnp.sum(dv.astype(f32), axis=0, keepdims=True)
    count = keep.shape[0]
    other = dot(dqkv[rows_at(1 - half, count), :], w[...], NT)
    send[...] = other.astype(bf16)
    mine = dot(dqkv[rows_at(half, count), :], w[...], NT)
    keep[...] = mine
    normal_m, _ = normalize(pick((x0, x1), seq, index[2]).astype(f32))
    normal_o, _ = normalize(pick((x2, x3), seq, index[2]).astype(f32))
    vsums[0:1, :] = jnp.sum(mine * normal_m, axis=0, keepdims=True) + jnp.sum(
        other * normal_o, axis=0, keepdims=True
    )
    vsums[1:2, :] = jnp.sum(mine, axis=0, keepdims=True) + jnp.sum(other, axis=0, keepdims=True)


def own_body(index, keep0, keep1, recv0, recv1, going, stay):
    own = index[2] == 0
    first = keep0[...] + recv0[...].astype(f32)
    second = keep1[...] + recv1[...].astype(f32)
    going[...] = jnp.where(own, second, first).astype(bf16)
    stay[...] = jnp.where(own, first, second)


def output_body(index, h0, h1, stay, far, vec, out):
    out[...] = (
        jnp.where(index[2] == 0, h0[...], h1[...])
        + stay[...]
        + far[...].astype(f32)
        + vec[8:9, :]
    )


def input_grad_body(index, base0, base1, stay, far, x, vec, out):
    incoming = stay[...] + far[...].astype(f32)
    normal, inverse = normalize(x[...].astype(f32))
    scaled = incoming * vec[0:1, :]
    centered = (
        scaled
        - jnp.mean(scaled, axis=-1, keepdims=True)
        - normal * jnp.mean(scaled * normal, axis=-1, keepdims=True)
    )
    out[...] = jnp.where(index[2] == 0, base0[...], base1[...]) + inverse * centered


def frame_grad_body(index, dkv0, dkv1, w, keep, across, send):
    half, chip = index[1], index[2]
    width = D // 4
    frames = dkv0.shape[0]
    for seq, dkv in enumerate((dkv0, dkv1)):
        for spot in range(2):
            chip_of = (chip + spot) % 2
            row = (seq * 2 + spot) * send.shape[0] // 4
            at = pl.ds(pl.multiple_of((chip_of * 2 + 1 - half) * width, width), width)
            send[row : row + frames, :] = dot(dkv[...], w[at, :], NT).astype(bf16)
            at = pl.ds(pl.multiple_of((chip_of * 2 + half) * width, width), width)
            row = seq * keep.shape[0] // 2
            (across if spot else keep)[row : row + frames, :] = dot(dkv[...], w[at, :], NT).astype(
                keep.dtype
            )


def frame_across_body(index, across, near, going):
    size = across.shape[0] // 2
    for seq in range(2):
        at, other = seq * size, (seq * 2 + 1) * size
        going[at : at + size, :] = (
            across[at : at + size, :].astype(f32) + near[other : other + size, :].astype(f32)
        ).astype(bf16)


def frame_sum_body(index, keep, near, far, out):
    size, width = keep.shape[0] // 2, keep.shape[1]
    tiles = width // 128
    frames = out.shape[0] // 2 // tiles
    for seq in range(2):
        at, other = seq * size, seq * 2 * size
        total = (
            keep[at : at + frames, :].astype(f32)
            + near[other : other + frames, :].astype(f32)
            + far[at : at + frames, :].astype(f32)
        )
        for tile in range(tiles):
            out[pl.ds(2 * tile + seq, frames, stride=2 * tiles), :] = total[:, tile * 128 : tile * 128 + 128]


def position_rel(order, position):
    return sum(bit for i, bit in enumerate(order) if position >> (len(order) - 1 - i) & 1)


def weight_grad_body(order, terms, rider, index, *refs):
    keep, send, scratch = refs[-3:]
    me, half = index[0], index[1]
    places = {position_rel(order, p): p for p in range(8)}
    for rel in (0, 2, 4, 6):
        at = pl.ds(pl.multiple_of(((me ^ rel) // 2) * 256, 256), 256)
        lane = 0
        for low, high, products in terms:
            to = lane + high - low
            total = None
            for left, right, side in products:
                left, right = refs[left], refs[right]
                if side is None:
                    rows = right[:, low:high]
                else:
                    rows = right[rows_at(half if side == 0 else 1 - half, left.shape[0]), low:high]
                part = dot(left[:, at], rows, TN)
                total = part if total is None else total + part
            scratch[0, :, lane:to] = total[:128]
            scratch[1, :, lane:to] = total[128:]
            lane = to
        for low in range(2):
            spot = places[rel + low]
            target = send if spot >= 4 else keep
            target[spot % 4, :128] = scratch[(me % 2) ^ low].astype(bf16)
            if rider is not None:
                target[spot % 4, 128:] = refs[rider][me ^ (rel + low)]


def halve_body(count, index, *refs):
    for i in range(count):
        keep, recv = refs[2 * i : 2 * i + 2]
        stay, go = refs[2 * count + 2 * i : 2 * count + 2 * i + 2]
        size = stay.shape[0]
        stay[...] = keep[:size].astype(f32) + recv[:size].astype(f32)
        go[...] = (keep[size:].astype(f32) + recv[size:].astype(f32)).astype(bf16)


def cross_end_body(index, keep0, recv0, keep1, recv1, qkv, out, self_out):
    width = qkv.shape[2]
    total = jnp.concatenate(
        [keep0[0] + recv0[0].astype(f32), keep1[0] + recv1[0].astype(f32)], axis=1
    )
    for i, lane in enumerate((2, 0, 1)):
        qkv[i] = total[:, lane * width : (lane + 1) * width]
    out[...] = total[:, 3 * width : 4 * width].T
    self_out[...] = total[:, 4 * width :].T


def self_end_body(index, keep0, recv0, keep1, recv1, vectors, qkv, self_bias, cross_bias, ff_bias):
    width = qkv.shape[2]
    second = keep1[0] + recv1[0].astype(f32)
    total = jnp.concatenate([keep0[0] + recv0[0].astype(f32), second[:128]], axis=1)
    for i in range(3):
        qkv[i] = total[:, i * width : (i + 1) * width]
    vectors[...] = second[128:144, :128]
    count = self_bias.shape[1]
    for i, target in enumerate((self_bias, cross_bias)):
        for j in range(2):
            row = 128 + (2 * i + j) * count
            target[j] = second[row : row + count, 128:136]
    ff_bias[...] = second[128 + 4 * count :, 128:136]


def small_body(index, vecs0, vecs1, two0, two1, three0, three1, self0, self1, cross0, cross1, ff0, ff1, out, rows):
    own = index[2] == 0
    two = jnp.where(own, two0[...], two1[...])
    three = jnp.where(own, three0[...], three1[...])
    vecs = vecs0[...] + vecs1[...]
    rows[...] = jnp.zeros(rows.shape, f32)
    for i, row in enumerate(
        (vecs[0:1], two[0:1], three[0:1], vecs[1:2], two[2:3], two[1:2], three[2:3], three[1:2], three[3:4])
    ):
        rows[i : i + 1, :] = row
    width = self0.shape[1]
    for i, (first, second) in enumerate(((self0, self1), (cross0, cross1))):
        total = first[...] + second[...]
        for j in range(2):
            at = (2 * i + j) * width
            rows[16:17, at : at + width] = total[j : j + 1]
    rows[17:18, :] = ff0[...] + ff1[...]
    row = lax.broadcasted_iota(jnp.int32, (32, D), 0)
    lane = lax.broadcasted_iota(jnp.int32, (32, D), 1)
    heads = jnp.where(row < 16, rows[16:17, :], rows[17:18, :])
    heads = jnp.where((lane >> 6) == (row & 15), heads, 0.0).astype(bf16)
    moves = jnp.where(
        (lax.broadcasted_iota(jnp.int32, (D, 64), 0) & 63) == lax.broadcasted_iota(jnp.int32, (D, 64), 1),
        1.0,
        0.0,
    ).astype(bf16)
    heads = dot(heads, moves).astype(bf16)
    spot = lax.broadcasted_iota(jnp.int32, (64, 128), 0)
    place = lax.broadcasted_iota(jnp.int32, (64, 128), 1)
    for owner in range(8):
        out[owner, :, :128] = rows[:32, owner * 128 : owner * 128 + 128].astype(bf16)
        moves = jnp.where((spot == owner * 8 + place) & (place < 8), 1.0, 0.0).astype(bf16)
        out[owner, :, 128:256] = dot(heads, moves).astype(bf16)
        out[owner, :, 256:] = jnp.zeros((32, out.shape[2] - 256), bf16)


def vectors_body(index, vectors, gains, shifts):
    part = jnp.zeros((16, 32), f32)
    for t in range(4):
        part = jnp.where(index[3] == t, vectors[:, 32 * t : 32 * t + 32], part)
    gains[...] = part[:3]
    shifts[...] = part[3:9]


def ff_grad_body(index, a0, a1, du0, du1, g0, g1, act0, act1, out):
    hidden = du0.shape[1]
    for at in range(0, D, 256):
        to = at + 256
        out[at:to, :hidden] = (
            dot(a0[:, at:to], du0[...], TN) + dot(a1[:, at:to], du1[...], TN)
        ).astype(bf16)
        out[at:to, hidden:] = (
            dot(g0[:, at:to], act0[...], TN) + dot(g1[:, at:to], act1[...], TN)
        ).astype(bf16)


def ff_end_body(index, total, grad_in, grad_out):
    hidden = grad_in.shape[1]
    grad_in[...] = total[:, :hidden].astype(f32)
    grad_out[...] = total[:, hidden:].astype(f32).T


def untangle_body(index, tangled, first, second):
    frames = first.shape[0]
    row = lax.broadcasted_iota(jnp.int32, (256, 256), 0)
    column = lax.broadcasted_iota(jnp.int32, (256, 256), 1)
    group = row // 16
    source = (row % 16) * 16 + 2 * (group % 8) + group // 8
    moves = jnp.where(source == column, 1.0, 0.0).astype(bf16)
    for frame in range(0, frames, 16):
        n = min(16, frames - frame)
        block = dot(moves[:, : 16 * n], tangled[16 * frame : 16 * (frame + n), :]).astype(bf16)
        for seq, target in enumerate((first, second)):
            for tile in range(8):
                at = (seq * 8 + tile) * 16
                target[frame : frame + n, tile * 128 : tile * 128 + 128] = block[at : at + n]


def permute_by(value, axis, bit):
    size = lax.axis_size(axis)
    return lax.ppermute(value, axis, [(i, i ^ bit) for i in range(size)])


class Gather:
    def __init__(self, line, shard, split, *after):
        self.line, self.split = line, split
        self.shard = self.pinned(shard, after)
        self.got = permute_by(self.shard, "fsdp", GATHER_A[0])

    @staticmethod
    def pinned(value, after):
        return lax.optimization_barrier((value, after))[0] if after else value

    def second(self, *after):
        got = self.pinned(self.got, after)
        cuts = slice(0, self.split), slice(self.split, None)
        self.near = [jnp.stack([self.shard[cut], got[cut]]) for cut in cuts]
        self.far = [
            permute_by(near, "fsdp", order[1]) for near, order in zip(self.near, (GATHER_A, GATHER_B))
        ]

    def third(self, *after):
        far = self.pinned(self.far, after)
        self.pieces = []
        for near, part, order in zip(self.near, far, (GATHER_A, GATHER_B)):
            self.pieces += [near, part, permute_by(jnp.concatenate([near, part]), "fsdp", order[2])]
        self.line.away(*self.pieces)


class Sum:
    def __init__(self, line, *parts):
        self.line = line
        self.keeps = [keep for keep, _, _ in parts]
        self.orders = [order for _, _, order in parts]
        self.number = 0
        self.send([send for _, send, _ in parts])

    def send(self, sends):
        self.recvs = [
            permute_by(send, "fsdp", order[self.number]) for send, order in zip(sends, self.orders)
        ]
        self.line.away(*self.recvs)
        self.number += 1

    def step(self):
        outs, args = [], []
        for keep, recv in zip(self.keeps, self.recvs):
            half = (keep.shape[0] // 2, *keep.shape[1:])
            outs += [struct(half, f32), struct(half, bf16)]
            args += [keep, recv]
        got = call(
            functools.partial(halve_body, len(self.keeps)), "halve", tuple(outs), self.line, *args,
        )
        self.keeps = got[::2]
        self.send(got[1::2])

    def end(self, body, name, outs):
        args = [a for pair in zip(self.keeps, self.recvs) for a in pair]
        return call(body, name, outs, self.line, *args, far=range(len(outs)))


def rels_of(order):
    b1, b2, b3 = order
    return ((0, b1), (b2, b2 ^ b1), (b3, b3 ^ b1, b3 ^ b2, b3 ^ b2 ^ b1))


GATHER_A, GATHER_B = (4, 2, 1), (4, 1, 2)
SUM_A, SUM_B = (1, 2, 4), (2, 1, 4)


def shards(
    fast,
    layer_input,
    encoder_states,
    out_grad,
    self_qkv,
    self_bias,
    self_out,
    cross_qkv,
    cross_bias,
    cross_out,
    ff_in,
    ff_bias,
    ff_out,
    norm_gains,
    shifts,
):
    tensor = lax.axis_size("tensor")
    fsdp_size = lax.axis_size("fsdp")
    t = lax.axis_index("tensor")
    me = lax.axis_index("fsdp")
    local_rows = layer_input.shape[0]
    seqs, frames, _ = encoder_states.shape
    length = local_rows * tensor // seqs
    count = length // 2
    width = self_qkv.shape[2]
    heads = width // HD
    hidden = ff_in.shape[1]
    step = tensor // 4
    half = (t // step) % 2
    chip = t // (tensor // 2)
    line = Line(jnp.stack([me, half, chip, t]).astype(jnp.int32))
    group = [[i for i in range(tensor) if (i // step) % 2 == side] for side in range(2)]

    def partner(value):
        return permute_by(value, "tensor", step)

    def rows_of_all(own):
        if fast:
            across = permute_by(own, "tensor", 2)
            return own, across, partner(own), partner(across)
        whole = lax.all_gather(own, "tensor", axis=0, tiled=True).reshape(seqs, 2, count, D)
        return tuple(
            lax.dynamic_index_in_dim(
                lax.dynamic_index_in_dim(whole, seq, 0, False), side, 0, False
            )
            for side in (half, 1 - half)
            for seq in (chip, 1 - chip)
        )

    class Exchange:
        def __init__(self, keep, send):
            self.keep, self.recv = keep, partner(send)

        def go(self):
            keep, recv = self.keep, self.recv
            if fast:
                going = (keep + recv.astype(f32)).astype(bf16)
                line.wait(going)
                self.terms = keep, recv, permute_by(going, "tensor", 2)
            else:
                total = lax.psum(keep + recv.astype(f32), "tensor", axis_index_groups=group)
                self.terms = total, jnp.zeros_like(recv), jnp.zeros_like(recv)
            return self.terms

    def own_of(first, second):
        return jnp.where(chip == 0, first, second)

    def own_rows(first, second):
        return lax.dynamic_slice_in_dim(
            own_of(first, second), (t % step) * local_rows, local_rows, 0
        )

    def own_sum(keep0, keep1, send0, send1):
        terms = [Exchange(k, s).go() for k, s in ((keep0, send0), (keep1, send1))]
        stay, near, far = (own_rows(a, b) for a, b in zip(*terms))
        return stay + near.astype(f32), far

    def own_terms(keep0, keep1, recv0, recv1):
        going, stay = call(
            own_body, "own", (struct(recv0.shape, bf16), struct(recv0.shape, f32)), line,
            keep0, keep1, recv0, recv1,
        )
        return stay, permute_by(going, "tensor", 2)

    rels_a, rels_b = rels_of(GATHER_A), rels_of(GATHER_B)
    packed_rows = jnp.concatenate([norm_gains, shifts], 0)
    packed_bias = jnp.concatenate(
        [self_bias.reshape(-1, HD // fsdp_size), cross_bias.reshape(-1, HD // fsdp_size), ff_bias],
        0,
    )
    if fast:
        extra = jnp.concatenate(
            [
                jnp.pad(packed_rows, ((0, 32 - packed_rows.shape[0]), (0, 0))),
                jnp.pad(packed_bias, ((0, 0), (0, 128 - packed_bias.shape[1]))),
            ],
            1,
        )

        def beside(out):
            return jnp.concatenate([out[:128], out[128:]], 1)

        packed = jnp.concatenate(
            [self_qkv.reshape(3 * 128, width), beside(self_out), extra], 0
        )
        self_w = Gather(line, packed, 256)
        (x_own, g_own), _ = lax.optimization_barrier(((layer_input, out_grad), self_w.got))
        packed = jnp.concatenate(
            [cross_qkv[1], cross_qkv[2], cross_qkv[0], beside(cross_out)], 0
        )
        tiles = hidden // 128
        packed_ff = jnp.concatenate(
            [
                ff_in.reshape(128, tiles, 128).transpose(1, 0, 2),
                ff_out.reshape(tiles, 128, 128),
            ],
            0,
        )
        self_w.second()
        x_rows = rows_of_all(x_own)
        cross_w = Gather(line, packed, 256, self_w.far)
        g_own, _ = lax.optimization_barrier((g_own, x_rows[2]))
        g_rows = rows_of_all(g_own)
        line.wait(self_w.far)
        tangled = encoder_states.reshape(2, frames, 8, 128).transpose(1, 2, 0, 3).reshape(-1, 128)
        line.away(tangled, *x_rows, *g_rows)
        e_seq = call(untangle_body, "untangle", (struct((frames, D), bf16),) * 2, line, tangled)
        self_w.third()
        cross_w.second(e_seq[0])
        ff_w = Gather(line, packed_ff, tiles, e_seq[0])
        line.wait(cross_w.near, g_rows)
    else:
        x_rows = rows_of_all(layer_input)
        e_seq = [encoder_states[s] for s in range(2)]
        vec = lax.all_gather(packed_rows, "fsdp", axis=1, tiled=True).astype(f32)
        biases = lax.all_gather(packed_bias, "fsdp", axis=1, tiled=True).astype(f32)
        whole = lax.all_gather(self_qkv, "fsdp", axis=1, tiled=True)
        w_self = jnp.concatenate([whole[0], whole[1], whole[2]], 1)
        wo_self = lax.all_gather(self_out, "fsdp", axis=1, tiled=True)
        whole = lax.all_gather(cross_qkv, "fsdp", axis=1, tiled=True)
        w_cross, w_kv = whole[0], jnp.concatenate([whole[1], whole[2]], 1)
        wo_cross = lax.all_gather(cross_out, "fsdp", axis=1, tiled=True)
        w_in = lax.all_gather(ff_in, "fsdp", axis=0, tiled=True)
        w_out = lax.all_gather(ff_out, "fsdp", axis=1, tiled=True)
        bias = jnp.zeros((8, hidden), f32)
        bias = bias.at[:4, :width].set(biases[: 4 * heads].reshape(4, width))
        bias = bias.at[4].set(biases[4 * heads :].reshape(hidden))

    attn_flops = 8 * length * width * 1024
    row_pair = (struct((count, D), f32), struct((count, D), bf16))

    def self_forward(s):
        nonlocal w_self, wo_self, vec, bias
        outs = (
            struct((length, D), bf16),
            struct((length, 3 * width), bf16),
            struct((length, width), bf16),
            struct((length, heads), f32),
            *row_pair,
        )
        kwargs = dict(scratch=(pltpu.VMEM((length, D), bf16),),)
        if fast and s == 0:
            outs += (
                struct((D, 3 * width), bf16),
                struct((width, D), bf16),
                struct((16, D), f32),
                struct((8, D), f32),
            )
            *got, w_self, wo_self, vec, bias = call(
                functools.partial(self_forward_body, (rels_a, rels_b), s),
                "self_forward", outs, line, *x_rows, *self_w.pieces, **kwargs,
            )
        else:
            got = call(
                functools.partial(self_forward_body, None, s),
                "self_forward", outs, line, *x_rows, vec, bias, w_self, wo_self, **kwargs,
            )
        a1[s], qkv1[s], o1[s], lse1[s], *res = got
        sum1[s] = Exchange(*res)

    def frames_in(s):
        nonlocal w_kv
        outs = (struct((frames, width), bf16),) * 2
        flops = 4 * frames * D * width
        if fast and s == 0:
            k2[s], v2[s], w_kv = call(
                functools.partial(frames_body, rels_a),
                "frames_in", outs + (struct((D, 2 * width), bf16),), line, e_seq[s], bias,
                *cross_w.pieces[:3],
            )
        else:
            k2[s], v2[s] = call(
                functools.partial(frames_body, None),
                "frames_in", outs, line, e_seq[s], bias, w_kv,
            )

    def norm_of(rows, seq, base, terms, name):
        return call(
            functools.partial(norm_body, rows, seq),
            name, (struct((count, D), f32), struct((count, D), bf16)), line, *base, *terms, vec,
        )

    def norm_two(s):
        h1[s], mine = norm_of((4, 1, 5), s, x_rows[:2], sum1[s].terms, "norm_two")
        a2_rows[s] = mine, partner(mine)

    def cross_forward(s):
        nonlocal w_cross, wo_cross
        outs = (
            struct((length, D), bf16),
            struct((length, width), bf16),
            struct((length, width), bf16),
            struct((length, heads), f32),
            *row_pair,
        )
        args = (*a2_rows[s], bias, k2[s], v2[s])
        if fast and s == 0:
            *got, w_cross, wo_cross = call(
                functools.partial(cross_forward_body, rels_b), "cross_forward",
                outs + (struct((D, width), bf16), struct((width, D), bf16)),
                line, *args, *cross_w.pieces[3:],
            )
        else:
            got = call(
                functools.partial(cross_forward_body, None), "cross_forward",
                outs, line, *args, w_cross, wo_cross,
            )
        a2[s], q2[s], o2[s], lse2[s], *res = got
        sum2[s] = Exchange(*res)

    def norm_three(s):
        h2[s], mine = norm_of((6, 2, 7), None, (h1[s],), sum2[s].terms, "norm_three")
        a3_rows[s] = mine, partner(mine)

    def feed(s):
        nonlocal w_in, w_out
        outs = (
            struct((length, D), bf16),
            struct((length, D), bf16),
            struct((length, hidden), bf16),
            struct((length, hidden), bf16),
            struct((1, hidden), f32),
            *row_pair,
        )
        args = (*a3_rows[s], *g_rows, bias)
        flops = 6 * length * D * hidden
        if fast and s == 0:
            *got, w_in, w_out = call(
                functools.partial(feed_body, (rels_a, rels_b), s),
                "feed", outs + (struct((D, hidden), bf16), struct((hidden, D), bf16)), line,
                *args, *ff_w.pieces,
            )
        else:
            got = call(
                functools.partial(feed_body, None, s),
                "feed", outs, line, *args, w_in, w_out,
            )
        a3[s], g_full[s], act[s], du[s], ff_sums[s], *res = got
        sum3[s] = Exchange(*res)

    def feed_out():
        return call(
            feed_out_body, "feed_out",
            (*[row_pair[0]] * 2, *[row_pair[1]] * 2),
            line, act[0], act[1], w_out,
        )

    def norm_back(gain, base, terms, h, name):
        return call(
            functools.partial(norm_back_body, gain),
            name,
            (struct((count, D), f32), struct((count, D), bf16), struct((8, D), f32)),
            line, base, *terms, h, vec,
        )

    def norm_three_back(s):
        dh2[s], low, sums3[s] = norm_back(2, g_full[s], sum3[s].terms, h2[s], "norm_three_back")
        h2_rows[s] = low, partner(low)

    def cross_back(s):
        outs = (
            struct((length, D), bf16),
            struct((length, width), bf16),
            struct((frames, 2 * width), bf16),
            struct((2, width), f32),
            *row_pair,
        )
        h2_full[s], dq2[s], dkv2[s], cross_sums[s], *res = call(
            cross_back_body, "cross_back", outs, line,
            *h2_rows[s], q2[s], k2[s], v2[s], lse2[s], w_cross, wo_cross,
        )
        sum4[s] = Exchange(*res)

    def norm_two_back(s):
        dh1[s], low, sums2[s] = norm_back(1, dh2[s], sum4[s].terms, h1[s], "norm_two_back")
        h1_rows[s] = low, partner(low)

    def self_back(s):
        outs = (
            struct((length, D), bf16),
            struct((length, 3 * width), bf16),
            struct((2, width), f32),
            struct((2, D), f32),
            *row_pair,
        )
        h1_full[s], dqkv1[s], self_sums[s], vec_sums[s], *res5[s] = call(
            functools.partial(self_back_body, s), "self_back", outs, line,
            *h1_rows[s], qkv1[s], lse1[s], w_self, wo_self, *x_rows,
        )

    def weight_grad(terms, order, name, rider=None):
        operands, table, n = [], [], 0
        for lefts, rights, span in terms:
            low, high = span or (0, rights[0].shape[1])
            products = []
            for left, right in zip(lefts, rights):
                sides = [(left, None)] if not isinstance(left, tuple) else list(zip(left, (0, 1)))
                for part, side in sides:
                    products.append((len(operands), len(operands) + 1, side))
                    operands += [part, right]
            table.append((low, high, products))
            n += high - low
        part = struct((4, 128 + (0 if rider is None else rider.shape[1]), n), bf16)
        at = None
        if rider is not None:
            at = len(operands)
            operands.append(rider)
        got = call(
            functools.partial(weight_grad_body, order, table, at),
            name,
            (part, part),
            line,
            *operands,

            scratch=(pltpu.VMEM((2, 128, n), f32),),
        )
        return (*got, order)

    def plain_grad(lefts, rights):
        return sum(dot(a, b, TN) for a, b in zip(lefts, rights))

    def frame_grad():
        padded = -(-frames // 16) * 16
        keep, across, send = call(
            frame_grad_body, "frame_grad",
            (
                struct((2 * padded, D // 4), bf16),
                struct((2 * padded, D // 4), bf16),
                struct((4 * padded, D // 4), bf16),
            ),
            line, dkv2[0], dkv2[1], w_kv,
        )
        return keep, across, partner(send)

    def frame_go(keep, across, near):
        (going,) = call(
            frame_across_body, "frame_across", (struct(across.shape, bf16),), line, across, near
        )
        return keep, near, permute_by(going, "tensor", 2)

    (
        a1, qkv1, o1, lse1, sum1, h1, k2, v2, a2_rows, a2, q2, o2, lse2, sum2, h2, a3_rows, a3, g_full,
        act, du, ff_sums, sum3, dh2, sums3, h2_rows, h2_full, dq2, dkv2, cross_sums, sum4, dh1, sums2,
        h1_rows, h1_full, dqkv1, self_sums, vec_sums, res5,
    ) = ([None] * 2 for _ in range(38))
    rows_struct = (struct((local_rows, D), f32),)

    def output():
        pair = h2 if fast else [own_rows(*h2)] * 2
        return call(output_body, "output", rows_struct, line, *pair, *out_terms, vec, far=(0,))[0]

    def input_gradient():
        pair = dh1 if fast else [own_rows(*dh1)] * 2
        args = (*pair, *terms, layer_input, vec)
        return call(input_grad_body, "input_grad", rows_struct, line, *args, far=(0,))[0]

    if not fast:
        g_rows = rows_of_all(out_grad)
        for stage, sums in (
            (self_forward, sum1), (frames_in, None), (norm_two, None), (cross_forward, sum2), (norm_three, None),
            (feed, sum3), (norm_three_back, None), (cross_back, sum4), (norm_two_back, None), (self_back, None),
        ):
            for s in range(2):
                stage(s)
                if sums:
                    sums[s].go()
        out_terms = own_sum(*feed_out())
        terms = own_sum(res5[0][0], res5[1][0], res5[0][1], res5[1][1])
        layer_output, input_grad = output(), input_gradient()
    else:
        w_self = wo_self = w_kv = w_cross = wo_cross = w_in = w_out = vec = bias = None
        self_forward(0)
        self_forward(1)
        cross_w.third(a1[1])
        sum1[0].go()
        frames_in(0)
        sum1[1].go()
        ff_w.second(k2[0])
        norm_two(0)
        cross_forward(0)
        line.wait(ff_w.far)
        frames_in(1)
        norm_two(1)
        sum2[0].go()
        ff_w.third(o2[0])
        cross_forward(1)
        line.wait(ff_w.pieces)
        norm_three(0)
        sum2[1].go()
        feed(0)
        norm_three(1)
        sum3[0].go()
        feed(1)
        out_parts = feed_out()
        out_recv = partner(out_parts[2]), partner(out_parts[3])
        norm_three_back(0)
        sum3[1].go()
        (ff_parts,) = call(
            ff_grad_body, "ff_grad", (struct((D, 2 * hidden), bf16),), line,
            *a3, *du, *g_full, *act, far=(0,),
        )
        ff_total = lax.psum_scatter(ff_parts, "fsdp", scatter_dimension=0, tiled=True)
        out_terms = own_terms(*out_parts[:2], *out_recv)
        cross_back(0)
        line.wait(out_terms[1])
        norm_three_back(1)
        sum4[0].go()
        layer_output = output()
        cross_back(1)
        norm_two_back(0)
        sum4[1].go()
        frame_terms = frame_grad()
        frame_terms = frame_go(*frame_terms)
        self_back(0)
        end0 = partner(res5[0][1])
        norm_two_back(1)
        cross_sum = Sum(
            line,
            weight_grad([(e_seq, dkv2, None), (a2, dq2, (0, width // 2))], SUM_A, "cross_grad"),
            weight_grad(
                [
                    (a2, dq2, (width // 2, width)),
                    (h2_full, o2, None),
                    ((h1_full[0], h1_rows[1]), o1, None),
                ],
                SUM_B,
                "cross_grad_b",
            ),
        )
        self_back(1)
        end1 = partner(res5[1][1])
        split = 3 * width // 2
        self_parts = weight_grad([(a1, dqkv1, (0, split))], SUM_A, "self_grad")
        (small,) = call(
            small_body, "small", (struct((8, 32, split), bf16),), line,
            *vec_sums, *sums2, *sums3, *self_sums, *cross_sums, *ff_sums,
            scratch=(pltpu.VMEM((32, D), f32),),
        )
        self_sum = Sum(
            line,
            self_parts,
            weight_grad([(a1, dqkv1, (split, 3 * width))], SUM_B, "self_grad_b", small),
        )
        cross_sum.step()
        terms = own_terms(res5[0][0], res5[1][0], end0, end1)
        self_sum.step()
        cross_sum.step()
        input_grad = input_gradient()
        self_sum.step()
        tiles = D // 4 // 128
        (rows,) = call(
            frame_sum_body, "frame_sum", (struct((frames * 2 * tiles, 128), f32),), line, *frame_terms, far=(0,),
        )
        ff_in_grad, ff_out_grad = call(
            ff_end_body, "ff_end", (struct((128, hidden), f32), struct((hidden, 128), f32)), line,
            ff_total, far=(0, 1),
        )
        vectors, self_qkv_grad, self_bias_grad, cross_bias_grad, ff_bias_grad = self_sum.end(
            self_end_body,
            "self_end",
            (
                struct((16, 128), f32),
                struct((3, 128, width), f32),
                struct((2, heads, 8), f32),
                struct((2, heads, 8), f32),
                struct((hidden // HD, 8), f32),
            ),
        )
        vectors = vectors + permute_by(vectors, "tensor", 1)
        vectors = vectors + permute_by(vectors, "tensor", 2)

    if fast:
        cross_qkv_grad, cross_out_grad, self_out_grad = cross_sum.end(
            cross_end_body,
            "cross_end",
            (
                struct((3, 128, width), f32),
                struct((width, 128), f32),
                struct((width, 128), f32),
            ),
        )
        encoder_grad = (
            rows.reshape(frames, tiles, 2, 128).transpose(2, 0, 1, 3).reshape(2, frames, D // 4)
        )
        gains_grad, shifts_grad = call(
            vectors_body, "vectors", (struct((3, 32), f32), struct((6, 32), f32)), line, vectors,
            far=(0, 1),
        )
    else:
        part = jnp.stack([dot(dkv2[s], w_kv, NT) for s in range(2)])
        encoder_grad = lax.psum_scatter(part, "tensor", scatter_dimension=2, tiled=True)

        def scattered(part, dimension):
            return lax.psum_scatter(part, "fsdp", scatter_dimension=dimension, tiled=True)

        counts = (t % step) == 0

        def vector(sums, row):
            return jnp.where(counts, own_of(sums[0][row], sums[1][row]), 0.0)

        vectors = jnp.stack(
            [
                vec_sums[0][0] + vec_sums[1][0],
                vector(sums2, 0),
                vector(sums3, 0),
                vec_sums[0][1] + vec_sums[1][1],
                vector(sums2, 2),
                vector(sums2, 1),
                vector(sums3, 2),
                vector(sums3, 1),
                vector(sums3, 3),
            ]
        )
        bias_sums = jnp.concatenate(
            [
                self_sums[0] + self_sums[1],
                cross_sums[0] + cross_sums[1],
                (ff_sums[0] + ff_sums[1]).reshape(-1, width),
            ],
            0,
        ).reshape(-1, HD)
        vectors = scattered(vectors, 1)
        vectors = lax.psum_scatter(vectors, "tensor", scatter_dimension=1, tiled=True)
        bias_sums = scattered(bias_sums, 1)
        ff_in_grad = scattered(plain_grad(a3, du), 0)
        ff_out_grad = scattered(plain_grad(act, g_full), 1)
        cross_out_grad = scattered(plain_grad(o2, h2_full), 1)
        kv_grad = plain_grad(e_seq, dkv2)
        cross_qkv_grad = scattered(
            jnp.stack([plain_grad(a2, dq2), kv_grad[:, :width], kv_grad[:, width:]]), 1
        )
        self_out_grad = scattered(plain_grad(o1, h1_full), 1)
        qkv_grad = scattered(plain_grad(a1, dqkv1), 0)
        self_qkv_grad = jnp.stack([qkv_grad[:, i * width : (i + 1) * width] for i in range(3)])
        piece = HD // fsdp_size
        self_bias_grad = bias_sums[: 2 * heads].reshape(2, heads, piece)
        cross_bias_grad = bias_sums[2 * heads : 4 * heads].reshape(2, heads, piece)
        ff_bias_grad = bias_sums[4 * heads :]
        gains_grad, shifts_grad = vectors[:3], vectors[3:]
    return (
        layer_output,
        input_grad,
        encoder_grad,
        self_qkv_grad,
        self_bias_grad,
        self_out_grad,
        cross_qkv_grad,
        cross_bias_grad,
        cross_out_grad,
        ff_in_grad,
        ff_bias_grad,
        ff_out_grad,
        gains_grad,
        shifts_grad,
    )


def solution(mesh):
    fast = mesh.shape["fsdp"] == 8 and mesh.shape["tensor"] == 4
    return jax.shard_map(
        functools.partial(shards, fast),
        mesh=mesh,
        in_specs=(
            P(("fsdp", "tensor"), None),
            P("fsdp", None, None),
            P(("fsdp", "tensor"), None),
            P(None, "fsdp", "tensor"),
            P(None, "tensor", "fsdp"),
            P("tensor", "fsdp"),
            P(None, "fsdp", "tensor"),
            P(None, "tensor", "fsdp"),
            P("tensor", "fsdp"),
            P("fsdp", "tensor"),
            P("tensor", "fsdp"),
            P("tensor", "fsdp"),
            P(None, "fsdp"),
            P(None, "fsdp"),
        ),
        out_specs=(
            P(("fsdp", "tensor"), None),
            P(("fsdp", "tensor"), None),
            P("fsdp", None, "tensor"),
            P(None, "fsdp", "tensor"),
            P(None, "tensor", "fsdp"),
            P("tensor", "fsdp"),
            P(None, "fsdp", "tensor"),
            P(None, "tensor", "fsdp"),
            P("tensor", "fsdp"),
            P("fsdp", "tensor"),
            P("tensor", "fsdp"),
            P("tensor", "fsdp"),
            P(None, ("fsdp", "tensor")),
            P(None, ("fsdp", "tensor")),
        ),
        check_vma=False,
    )
```

```python
import functools
import math

import jax
import jax.numpy as jnp
from jax import lax
from jax.experimental import pallas as pl
from jax.experimental.pallas import tpu as pltpu
from jax.sharding import PartitionSpec as P

D = 1024
HD = 64
f32 = jnp.float32
bf16 = jnp.bfloat16
NN = (((1,), (0,)), ((), ()))
NT = (((1,), (1,)), ((), ()))
TN = (((0,), (0,)), ((), ()))
MIB = 2**20


def dot(left, right, dims=NN):
    return lax.dot_general(left, right, dims, preferred_element_type=f32)


def struct(shape, dtype):
    return jax.ShapeDtypeStruct(shape, dtype)


class Line:
    def __init__(self, index):
        self.index = index
        self.kept = {}

    def wait(self, *values):
        self.index, _ = lax.optimization_barrier((self.index, values))

    def away(self, *values):
        for value in values:
            self.kept[id(value)] = value


KERNELS = {
    "untangle": (16, 0.3),
    "self_forward": (14, 0.3),
    "frames_in": (12, 0.3),
    "norm_two": (8, 4),
    "norm_three": (8, 4),
    "cross_forward": (20, 0.3),
    "feed": (22, 0.3),
    "feed_out": (12, 0.3),
    "ff_grad": (20, 0.3),
    "norm_three_back": (10, 4),
    "norm_two_back": (10, 4),
    "cross_back": (24, 0.3),
    "self_back": (16, 0.3),
    "cross_grad": (18, 0.3),
    "cross_grad_b": (18, 0.3),
    "self_grad": (10, 0.3),
    "self_grad_b": (12, 0.3),
    "frame_grad": (16, 0.3),
    "frame_sum": (20, 0.3),
    "halve": (12, 0.3),
    "input_grad": (8, 0.3),
    "ff_end": (8, 0.3),
    "cross_end": (8, 0.3),
    "self_end": (8, 0.3),
    "own": (8, 0.3),
    "output": (8, 0.3),
    "vectors": (8, 0.3),
    "frame_across": (12, 0.3),
    "small": (8, 0.3),
}


def call(body, name, outs, line, *args, far=(), scratch=()):
    grant, time = KERNELS[name]
    vm = pl.BlockSpec(memory_space=pltpu.VMEM)
    args = [
        pltpu.with_memory_space_constraint(a, pltpu.HBM) if id(a) in line.kept else a for a in args
    ]
    got = pl.pallas_call(
        body,
        name=name,
        out_shape=tuple(
            (pltpu.HBM if i in far else pltpu.VMEM)(out.shape, out.dtype)
            for i, out in enumerate(outs)
        ),
        in_specs=[pl.BlockSpec(memory_space=pltpu.SMEM)] + [vm] * len(args),
        out_specs=tuple(vm for _ in outs),
        scratch_shapes=scratch,
        compiler_params=pltpu.CompilerParams(vmem_limit_bytes=grant * MIB),
        cost_estimate=pl.CostEstimate(
            flops=int(time * 1.15e9), bytes_accessed=int(time * 3.69e6), transcendentals=0
        ),
    )(line.index, *args)
    line.away(*(got[i] for i in far))
    line.wait(got[-1])
    return got


def rows_at(half, count):
    return pl.ds(pl.multiple_of(half * count, 32), count)


def place(target, mine, other, half):
    count = mine.shape[0]
    target[rows_at(half, count), :] = mine[...]
    target[rows_at(1 - half, count), :] = other[...]


def pick(pair, seq, chip):
    near, far = pair
    return jnp.where(chip == seq, near[...].astype(f32), far[...].astype(f32)).astype(near.dtype)


def place_of(target, rows, seq, half, chip):
    count = rows[0].shape[0]
    target[rows_at(half, count), :] = pick(rows[:2], seq, chip)
    target[rows_at(1 - half, count), :] = pick(rows[2:], seq, chip)


def normalize(v):
    center = v - jnp.mean(v, axis=-1, keepdims=True)
    inverse = lax.rsqrt(jnp.mean(center * center, axis=-1, keepdims=True) + 1e-05)
    return center * inverse, inverse


def spots(pieces, rels, me):
    for piece, group in zip(pieces, rels):
        for spot, rel in enumerate(group):
            yield piece.at[spot], me ^ rel, pl.ds(pl.multiple_of((me ^ rel) * 128, 128), 128)


def head_masks(width):
    lane = lax.broadcasted_iota(jnp.int32, (1, width), 1) // HD
    return [lane == h for h in range(width // HD)]


def causal_mask(length):
    return lax.broadcasted_iota(jnp.int32, (length, length), 0) >= lax.broadcasted_iota(
        jnp.int32, (length, length), 1
    )


def attention(q, k, v, lse_ref, causal):
    total = jnp.zeros(q.shape, f32)
    q = (q.astype(f32) * HD**-0.5).astype(bf16)
    allowed = causal_mask(q.shape[0]) if causal else None
    for h, mask in enumerate(head_masks(q.shape[1])):
        scores = dot(jnp.where(mask, q, 0), k, NT)
        if causal:
            scores = jnp.where(allowed, scores, -1e30)
        highest = jnp.max(scores, axis=1, keepdims=True)
        weight = jnp.exp(scores - highest)
        norm = jnp.sum(weight, axis=1, keepdims=True)
        total += dot(weight.astype(bf16), jnp.where(mask, v, 0)) * (1.0 / norm)
        lse_ref[:, h : h + 1] = highest + jnp.log(norm)
    return total.astype(bf16)


def attention_back(q, k, v, lse_ref, upstream, causal):
    dq = jnp.zeros(q.shape, f32)
    dk = jnp.zeros(k.shape, f32)
    dv = jnp.zeros(k.shape, f32)
    q = (q.astype(f32) * HD**-0.5).astype(bf16)
    allowed = causal_mask(q.shape[0]) if causal else None
    for h, mask in enumerate(head_masks(q.shape[1])):
        query, above = jnp.where(mask, q, 0), jnp.where(mask, upstream, 0)
        scores = dot(query, k, NT)
        if causal:
            scores = jnp.where(allowed, scores, -1e30)
        prob = jnp.exp(scores - lse_ref[:, h : h + 1])
        dprob = dot(above, v, NT)
        delta = jnp.sum(prob * dprob, axis=1, keepdims=True)
        dscore = (prob * (dprob - delta)).astype(bf16)
        dv += dot(prob.astype(bf16), above, TN)
        dk += dot(dscore, query, TN)
        dq += dot(dscore, jnp.where(mask, k, 0))
    return (dq * HD**-0.5).astype(bf16), dk.astype(bf16), dv.astype(bf16)


def halves(rows_ref, weight, dims, keep, send, half):
    count = keep.shape[0]
    send[...] = dot(rows_ref[rows_at(1 - half, count), :], weight, dims).astype(bf16)
    keep[...] = dot(rows_ref[rows_at(half, count), :], weight, dims)


def join_out(wo, piece, at):
    wo[:128, at] = piece[128:256, :128]
    wo[128:, at] = piece[128:256, 128:]


def join_small(vec, bias, pieces, rels, me):
    lane = lax.broadcasted_iota(jnp.int32, (128, D), 1)
    spot_of = lax.broadcasted_iota(jnp.int32, (128, D), 0)
    total = jnp.zeros((32, D), f32)
    for piece, owner, at in spots(pieces, rels, me):
        vec[:, at] = piece[256:272, :128].astype(f32)
        moves = jnp.where(((lane & 63) == owner * 8 + spot_of) & (spot_of < 8), 1.0, 0.0)
        total += dot(piece[256:288, 128:], moves.astype(bf16))
    row = lax.broadcasted_iota(jnp.int32, (32, D), 0)
    head = lax.broadcasted_iota(jnp.int32, (32, D), 1) >> 6
    total = jnp.where(head == jnp.where(row < 16, row & 3, row - 16), total, 0.0).astype(bf16)
    kind = lax.broadcasted_iota(jnp.int32, (8, 32), 0)
    row = lax.broadcasted_iota(jnp.int32, (8, 32), 1)
    moves = jnp.where(kind == jnp.where(row < 16, row >> 2, 4), 1.0, 0.0).astype(bf16)
    bias[...] = dot(moves, total)


def self_forward_body(rels, seq, index, x0, x1, x2, x3, *refs):
    if rels is None:
        vec, bias, w, wo, a_ref, qkv, o_ref, lse, keep, send, xs = refs
    else:
        pieces, (a_ref, qkv, o_ref, lse, keep, send, w, wo, vec, bias, xs) = refs[:6], refs[6:]
        me, wide = index[0], wo.shape[0]
        for piece, _, at in spots(pieces[:3], rels[0], me):
            w[at, :wide] = piece[:128, :]
            w[at, wide : 2 * wide] = piece[128:, :]
        for piece, _, at in spots(pieces[3:], rels[1], me):
            w[at, 2 * wide :] = piece[:128, :]
            join_out(wo, piece, at)
        join_small(vec, bias, pieces[3:], rels[1], me)
    half = index[1]
    width = wo.shape[0]
    place_of(xs, (x0, x1, x2, x3), seq, half, index[2])
    normal, _ = normalize(xs[...].astype(f32))
    a = (normal * vec[0:1, :] + vec[3:4, :]).astype(bf16)
    a_ref[...] = a
    qkv[:, :width] = (dot(a, w[:, :width]) + bias[0:1, :width]).astype(bf16)
    qkv[:, width : 2 * width] = dot(a, w[:, width : 2 * width]).astype(bf16)
    qkv[:, 2 * width :] = (dot(a, w[:, 2 * width :]) + bias[1:2, :width]).astype(bf16)
    o_ref[...] = attention(
        qkv[:, :width], qkv[:, width : 2 * width], qkv[:, 2 * width :], lse, True
    )
    halves(o_ref, wo[...], NN, keep, send, half)


def frames_body(rels, index, e, bias, *refs):
    if rels is None:
        w, k, v = refs
        width = k.shape[1]
    else:
        pieces, (k, v, w) = refs[:3], refs[3:]
        width = k.shape[1]
        for piece, _, at in spots(pieces, rels, index[0]):
            w[at, :width] = piece[:128, :]
            w[at, width:] = piece[128:, :]
    k[...] = dot(e[...], w[:, :width]).astype(bf16)
    v[...] = (dot(e[...], w[:, width:]) + bias[3:4, :width]).astype(bf16)


def cross_forward_body(rels, index, am, ao, bias, k, v, *refs):
    if rels is None:
        w, wo, a_ref, q_ref, o_ref, lse, keep, send = refs
    else:
        pieces, (a_ref, q_ref, o_ref, lse, keep, send, w, wo) = refs[:3], refs[3:]
        for piece, _, at in spots(pieces, rels, index[0]):
            w[at, :] = piece[:128, :]
            join_out(wo, piece, at)
    half = index[1]
    place(a_ref, am, ao, half)
    q_ref[...] = (dot(a_ref[...], w[...]) + bias[2:3, : w.shape[1]]).astype(bf16)
    o_ref[...] = attention(q_ref[...], k[...], v[...], lse, False)
    halves(o_ref, wo[...], NN, keep, send, half)


def norm_body(rows, seq, index, *refs):
    shift, gain, bias = rows
    if seq is None:
        base, keep, recv, far, vec, h_ref, a_ref = refs
        start = base[...]
    else:
        near, across, keep, recv, far, vec, h_ref, a_ref = refs
        start = pick((near, across), seq, index[2])
    h = (
        start.astype(f32)
        + keep[...]
        + recv[...].astype(f32)
        + far[...].astype(f32)
        + vec[shift : shift + 1, :]
    )
    h_ref[...] = h
    normal, _ = normalize(h)
    a_ref[...] = (normal * vec[gain : gain + 1, :] + vec[bias : bias + 1, :]).astype(bf16)


def norm_back_body(gain, index, base, keep, recv, far, h, vec, dh_ref, low_ref, sums):
    incoming = keep[...] + recv[...].astype(f32) + far[...].astype(f32)
    normal, inverse = normalize(h[...].astype(f32))
    sums[...] = jnp.zeros(sums.shape, f32)
    sums[0:1, :] = jnp.sum(incoming * normal, axis=0, keepdims=True)
    sums[1:2, :] = jnp.sum(incoming, axis=0, keepdims=True)
    scaled = incoming * vec[gain : gain + 1, :]
    centered = (
        scaled
        - jnp.mean(scaled, axis=-1, keepdims=True)
        - normal * jnp.mean(scaled * normal, axis=-1, keepdims=True)
    )
    count = keep.shape[0]
    above = (base[...] if base.shape[0] == count else base[rows_at(index[1], count), :]).astype(f32)
    dh = above + inverse * centered
    dh_ref[...] = dh
    low_ref[...] = dh.astype(bf16)
    sums[2:3, :] = jnp.sum(dh, axis=0, keepdims=True)
    sums[3:4, :] = jnp.sum(above, axis=0, keepdims=True)


def feed_body(rels, seq, index, am, ao, y0, y1, y2, y3, bias, *refs):
    if rels is None:
        w_in, w_out, a_ref, g_full, g_ref, du_ref, sums, keep, send = refs
    else:
        pieces, (a_ref, g_full, g_ref, du_ref, sums, keep, send, w_in, w_out) = refs[:6], refs[6:]
        for piece, _, at in spots(pieces[:3], rels[0], index[0]):
            for tile in range(w_in.shape[1] // 128):
                w_in[at, tile * 128 : tile * 128 + 128] = piece[tile]
        for piece, _, at in spots(pieces[3:], rels[1], index[0]):
            for tile in range(w_in.shape[1] // 128):
                w_out[tile * 128 : tile * 128 + 128, at] = piece[tile]
    half = index[1]
    place(a_ref, am, ao, half)
    place_of(g_full, (y0, y1, y2, y3), seq, half, index[2])
    hidden = w_in.shape[1]
    step = min(512, hidden)
    for at in range(0, hidden, step):
        to = at + step
        u = dot(a_ref[...], w_in[:, at:to]) + bias[4:5, at:to]
        dg = dot(g_full[...], w_out[at:to, :], NT)
        cdf = 0.5 * (1.0 + lax.erf(u * 0.7071067811865476))
        g_ref[:, at:to] = (u * cdf).astype(bf16)
        slope = cdf + u * (jnp.exp(-0.5 * u * u) * 0.3989422804014327)
        du = (dg * slope).astype(bf16)
        du_ref[:, at:to] = du
        sums[:, at:to] = jnp.sum(du.astype(f32), axis=0, keepdims=True)
    halves(du_ref, w_in[...], NT, keep, send, half)


def feed_out_body(index, g0, g1, w_out, keep0, keep1, send0, send1):
    half = index[1]
    halves(g0, w_out[...], NN, keep0, send0, half)
    halves(g1, w_out[...], NN, keep1, send1, half)


def cross_back_body(index, hm, ho, q, k, v, lse, w, wo, h_full, dq_ref, dkv, sums, keep, send):
    half = index[1]
    width = q.shape[1]
    place(h_full, hm, ho, half)
    upstream = dot(h_full[...], wo[...], NT).astype(bf16)
    dq, dk, dv = attention_back(q[...], k[...], v[...], lse, upstream, False)
    dq_ref[...] = dq
    dkv[:, :width] = dk
    dkv[:, width:] = dv
    sums[0:1, :] = jnp.sum(dq.astype(f32), axis=0, keepdims=True)
    sums[1:2, :] = jnp.sum(dv.astype(f32), axis=0, keepdims=True)
    halves(dq_ref, w[...], NT, keep, send, half)


def self_back_body(
    seq, index, hm, ho, qkv, lse, w, wo, x0, x1, x2, x3, h_full, dqkv, sums, vsums, keep, send
):
    half = index[1]
    width = wo.shape[0]
    place(h_full, hm, ho, half)
    upstream = dot(h_full[...], wo[...], NT).astype(bf16)
    dq, dk, dv = attention_back(
        qkv[:, :width], qkv[:, width : 2 * width], qkv[:, 2 * width :], lse, upstream, True
    )
    dqkv[:, :width] = dq
    dqkv[:, width : 2 * width] = dk
    dqkv[:, 2 * width :] = dv
    sums[0:1, :] = jnp.sum(dq.astype(f32), axis=0, keepdims=True)
    sums[1:2, :] = jnp.sum(dv.astype(f32), axis=0, keepdims=True)
    count = keep.shape[0]
    other = dot(dqkv[rows_at(1 - half, count), :], w[...], NT)
    send[...] = other.astype(bf16)
    mine = dot(dqkv[rows_at(half, count), :], w[...], NT)
    keep[...] = mine
    normal_m, _ = normalize(pick((x0, x1), seq, index[2]).astype(f32))
    normal_o, _ = normalize(pick((x2, x3), seq, index[2]).astype(f32))
    vsums[0:1, :] = jnp.sum(mine * normal_m, axis=0, keepdims=True) + jnp.sum(
        other * normal_o, axis=0, keepdims=True
    )
    vsums[1:2, :] = jnp.sum(mine, axis=0, keepdims=True) + jnp.sum(other, axis=0, keepdims=True)


def own_body(index, keep0, keep1, recv0, recv1, going, stay):
    own = index[2] == 0
    first = keep0[...] + recv0[...].astype(f32)
    second = keep1[...] + recv1[...].astype(f32)
    going[...] = jnp.where(own, second, first).astype(bf16)
    stay[...] = jnp.where(own, first, second)


def output_body(index, h0, h1, stay, far, vec, out):
    out[...] = (
        jnp.where(index[2] == 0, h0[...], h1[...])
        + stay[...]
        + far[...].astype(f32)
        + vec[8:9, :]
    )


def input_grad_body(index, base0, base1, stay, far, x, vec, out):
    incoming = stay[...] + far[...].astype(f32)
    normal, inverse = normalize(x[...].astype(f32))
    scaled = incoming * vec[0:1, :]
    centered = (
        scaled
        - jnp.mean(scaled, axis=-1, keepdims=True)
        - normal * jnp.mean(scaled * normal, axis=-1, keepdims=True)
    )
    out[...] = jnp.where(index[2] == 0, base0[...], base1[...]) + inverse * centered


def frame_grad_body(index, dkv0, dkv1, w, keep, across, send):
    half, chip = index[1], index[2]
    width = D // 4
    frames = dkv0.shape[0]
    for seq, dkv in enumerate((dkv0, dkv1)):
        for spot in range(2):
            chip_of = (chip + spot) % 2
            row = (seq * 2 + spot) * send.shape[0] // 4
            at = pl.ds(pl.multiple_of((chip_of * 2 + 1 - half) * width, width), width)
            send[row : row + frames, :] = dot(dkv[...], w[at, :], NT).astype(bf16)
            at = pl.ds(pl.multiple_of((chip_of * 2 + half) * width, width), width)
            row = seq * keep.shape[0] // 2
            (across if spot else keep)[row : row + frames, :] = dot(dkv[...], w[at, :], NT).astype(
                keep.dtype
            )


def frame_across_body(index, across, near, going):
    size = across.shape[0] // 2
    for seq in range(2):
        at, other = seq * size, (seq * 2 + 1) * size
        going[at : at + size, :] = (
            across[at : at + size, :].astype(f32) + near[other : other + size, :].astype(f32)
        ).astype(bf16)


def frame_sum_body(index, keep, near, far, out):
    size, width = keep.shape[0] // 2, keep.shape[1]
    tiles = width // 128
    frames = out.shape[0] // 2 // tiles
    for seq in range(2):
        at, other = seq * size, seq * 2 * size
        total = (
            keep[at : at + frames, :].astype(f32)
            + near[other : other + frames, :].astype(f32)
            + far[at : at + frames, :].astype(f32)
        )
        for tile in range(tiles):
            out[pl.ds(2 * tile + seq, frames, stride=2 * tiles), :] = total[:, tile * 128 : tile * 128 + 128]


def position_rel(order, position):
    return sum(bit for i, bit in enumerate(order) if position >> (len(order) - 1 - i) & 1)


def weight_grad_body(order, terms, rider, index, *refs):
    keep, send, scratch = refs[-3:]
    me, half = index[0], index[1]
    places = {position_rel(order, p): p for p in range(8)}
    for rel in (0, 2, 4, 6):
        at = pl.ds(pl.multiple_of(((me ^ rel) // 2) * 256, 256), 256)
        lane = 0
        for low, high, products in terms:
            to = lane + high - low
            total = None
            for left, right, side in products:
                left, right = refs[left], refs[right]
                if side is None:
                    rows = right[:, low:high]
                else:
                    rows = right[rows_at(half if side == 0 else 1 - half, left.shape[0]), low:high]
                part = dot(left[:, at], rows, TN)
                total = part if total is None else total + part
            scratch[0, :, lane:to] = total[:128]
            scratch[1, :, lane:to] = total[128:]
            lane = to
        for low in range(2):
            spot = places[rel + low]
            target = send if spot >= 4 else keep
            target[spot % 4, :128] = scratch[(me % 2) ^ low].astype(bf16)
            if rider is not None:
                target[spot % 4, 128:] = refs[rider][me ^ (rel + low)]


def halve_body(count, index, *refs):
    for i in range(count):
        keep, recv = refs[2 * i : 2 * i + 2]
        stay, go = refs[2 * count + 2 * i : 2 * count + 2 * i + 2]
        size = stay.shape[0]
        stay[...] = keep[:size].astype(f32) + recv[:size].astype(f32)
        go[...] = (keep[size:].astype(f32) + recv[size:].astype(f32)).astype(bf16)


def cross_end_body(index, keep0, recv0, keep1, recv1, qkv, out, self_out):
    width = qkv.shape[2]
    total = jnp.concatenate(
        [keep0[0] + recv0[0].astype(f32), keep1[0] + recv1[0].astype(f32)], axis=1
    )
    for i, lane in enumerate((2, 0, 1)):
        qkv[i] = total[:, lane * width : (lane + 1) * width]
    out[...] = total[:, 3 * width : 4 * width].T
    self_out[...] = total[:, 4 * width :].T


def self_end_body(index, keep0, recv0, keep1, recv1, vectors, qkv, self_bias, cross_bias, ff_bias):
    width = qkv.shape[2]
    second = keep1[0] + recv1[0].astype(f32)
    total = jnp.concatenate([keep0[0] + recv0[0].astype(f32), second[:128]], axis=1)
    for i in range(3):
        qkv[i] = total[:, i * width : (i + 1) * width]
    vectors[...] = second[128:144, :128]
    count = self_bias.shape[1]
    for i, target in enumerate((self_bias, cross_bias)):
        for j in range(2):
            row = 128 + (2 * i + j) * count
            target[j] = second[row : row + count, 128:136]
    ff_bias[...] = second[128 + 4 * count :, 128:136]


def small_body(index, vecs0, vecs1, two0, two1, three0, three1, self0, self1, cross0, cross1, ff0, ff1, out, rows):
    own = index[2] == 0
    two = jnp.where(own, two0[...], two1[...])
    three = jnp.where(own, three0[...], three1[...])
    vecs = vecs0[...] + vecs1[...]
    rows[...] = jnp.zeros(rows.shape, f32)
    for i, row in enumerate(
        (vecs[0:1], two[0:1], three[0:1], vecs[1:2], two[2:3], two[1:2], three[2:3], three[1:2], three[3:4])
    ):
        rows[i : i + 1, :] = row
    width = self0.shape[1]
    for i, (first, second) in enumerate(((self0, self1), (cross0, cross1))):
        total = first[...] + second[...]
        for j in range(2):
            at = (2 * i + j) * width
            rows[16:17, at : at + width] = total[j : j + 1]
    rows[17:18, :] = ff0[...] + ff1[...]
    row = lax.broadcasted_iota(jnp.int32, (32, D), 0)
    lane = lax.broadcasted_iota(jnp.int32, (32, D), 1)
    heads = jnp.where(row < 16, rows[16:17, :], rows[17:18, :])
    heads = jnp.where((lane >> 6) == (row & 15), heads, 0.0).astype(bf16)
    moves = jnp.where(
        (lax.broadcasted_iota(jnp.int32, (D, 64), 0) & 63) == lax.broadcasted_iota(jnp.int32, (D, 64), 1),
        1.0,
        0.0,
    ).astype(bf16)
    heads = dot(heads, moves).astype(bf16)
    spot = lax.broadcasted_iota(jnp.int32, (64, 128), 0)
    place = lax.broadcasted_iota(jnp.int32, (64, 128), 1)
    for owner in range(8):
        out[owner, :, :128] = rows[:32, owner * 128 : owner * 128 + 128].astype(bf16)
        moves = jnp.where((spot == owner * 8 + place) & (place < 8), 1.0, 0.0).astype(bf16)
        out[owner, :, 128:256] = dot(heads, moves).astype(bf16)
        out[owner, :, 256:] = jnp.zeros((32, out.shape[2] - 256), bf16)


def vectors_body(index, vectors, gains, shifts):
    part = jnp.zeros((16, 32), f32)
    for t in range(4):
        part = jnp.where(index[3] == t, vectors[:, 32 * t : 32 * t + 32], part)
    gains[...] = part[:3]
    shifts[...] = part[3:9]


def ff_grad_body(index, a0, a1, du0, du1, g0, g1, act0, act1, out):
    hidden = du0.shape[1]
    for at in range(0, D, 256):
        to = at + 256
        out[at:to, :hidden] = (
            dot(a0[:, at:to], du0[...], TN) + dot(a1[:, at:to], du1[...], TN)
        ).astype(bf16)
        out[at:to, hidden:] = (
            dot(g0[:, at:to], act0[...], TN) + dot(g1[:, at:to], act1[...], TN)
        ).astype(bf16)


def ff_end_body(index, total, grad_in, grad_out):
    hidden = grad_in.shape[1]
    grad_in[...] = total[:, :hidden].astype(f32)
    grad_out[...] = total[:, hidden:].astype(f32).T


def untangle_body(index, tangled, first, second):
    frames = first.shape[0]
    row = lax.broadcasted_iota(jnp.int32, (256, 256), 0)
    column = lax.broadcasted_iota(jnp.int32, (256, 256), 1)
    group = row // 16
    source = (row % 16) * 16 + 2 * (group % 8) + group // 8
    moves = jnp.where(source == column, 1.0, 0.0).astype(bf16)
    for frame in range(0, frames, 16):
        n = min(16, frames - frame)
        block = dot(moves[:, : 16 * n], tangled[16 * frame : 16 * (frame + n), :]).astype(bf16)
        for seq, target in enumerate((first, second)):
            for tile in range(8):
                at = (seq * 8 + tile) * 16
                target[frame : frame + n, tile * 128 : tile * 128 + 128] = block[at : at + n]


def permute_by(value, axis, bit):
    size = lax.axis_size(axis)
    return lax.ppermute(value, axis, [(i, i ^ bit) for i in range(size)])


class Gather:
    def __init__(self, line, shard, split, *after):
        self.line, self.split = line, split
        self.shard = self.pinned(shard, after)
        self.got = permute_by(self.shard, "fsdp", GATHER_A[0])

    @staticmethod
    def pinned(value, after):
        return lax.optimization_barrier((value, after))[0] if after else value

    def second(self, *after):
        got = self.pinned(self.got, after)
        cuts = slice(0, self.split), slice(self.split, None)
        self.near = [jnp.stack([self.shard[cut], got[cut]]) for cut in cuts]
        self.far = [
            permute_by(near, "fsdp", order[1]) for near, order in zip(self.near, (GATHER_A, GATHER_B))
        ]

    def third(self, *after):
        far = self.pinned(self.far, after)
        self.pieces = []
        for near, part, order in zip(self.near, far, (GATHER_A, GATHER_B)):
            self.pieces += [near, part, permute_by(jnp.concatenate([near, part]), "fsdp", order[2])]
        self.line.away(*self.pieces)


class Sum:
    def __init__(self, line, *parts):
        self.line = line
        self.keeps = [keep for keep, _, _ in parts]
        self.orders = [order for _, _, order in parts]
        self.number = 0
        self.send([send for _, send, _ in parts])

    def send(self, sends):
        self.recvs = [
            permute_by(send, "fsdp", order[self.number]) for send, order in zip(sends, self.orders)
        ]
        self.line.away(*self.recvs)
        self.number += 1

    def step(self):
        outs, args = [], []
        for keep, recv in zip(self.keeps, self.recvs):
            half = (keep.shape[0] // 2, *keep.shape[1:])
            outs += [struct(half, f32), struct(half, bf16)]
            args += [keep, recv]
        got = call(
            functools.partial(halve_body, len(self.keeps)), "halve", tuple(outs), self.line, *args,
        )
        self.keeps = got[::2]
        self.send(got[1::2])

    def end(self, body, name, outs):
        args = [a for pair in zip(self.keeps, self.recvs) for a in pair]
        return call(body, name, outs, self.line, *args, far=range(len(outs)))


def rels_of(order):
    b1, b2, b3 = order
    return ((0, b1), (b2, b2 ^ b1), (b3, b3 ^ b1, b3 ^ b2, b3 ^ b2 ^ b1))


GATHER_A, GATHER_B = (4, 2, 1), (4, 1, 2)
SUM_A, SUM_B = (1, 2, 4), (2, 1, 4)


def shards(
    fast,
    layer_input,
    encoder_states,
    out_grad,
    self_qkv,
    self_bias,
    self_out,
    cross_qkv,
    cross_bias,
    cross_out,
    ff_in,
    ff_bias,
    ff_out,
    norm_gains,
    shifts,
):
    tensor = lax.axis_size("tensor")
    fsdp_size = lax.axis_size("fsdp")
    t = lax.axis_index("tensor")
    me = lax.axis_index("fsdp")
    local_rows = layer_input.shape[0]
    seqs, frames, _ = encoder_states.shape
    length = local_rows * tensor // seqs
    count = length // 2
    width = self_qkv.shape[2]
    heads = width // HD
    hidden = ff_in.shape[1]
    step = tensor // 4
    half = (t // step) % 2
    chip = t // (tensor // 2)
    line = Line(jnp.stack([me, half, chip, t]).astype(jnp.int32))
    group = [[i for i in range(tensor) if (i // step) % 2 == side] for side in range(2)]

    def partner(value):
        return permute_by(value, "tensor", step)

    def rows_of_all(own):
        if fast:
            across = permute_by(own, "tensor", 2)
            return own, across, partner(own), partner(across)
        whole = lax.all_gather(own, "tensor", axis=0, tiled=True).reshape(seqs, 2, count, D)
        return tuple(
            lax.dynamic_index_in_dim(
                lax.dynamic_index_in_dim(whole, seq, 0, False), side, 0, False
            )
            for side in (half, 1 - half)
            for seq in (chip, 1 - chip)
        )

    class Exchange:
        def __init__(self, keep, send):
            self.keep, self.recv = keep, partner(send)

        def go(self):
            keep, recv = self.keep, self.recv
            if fast:
                going = (keep + recv.astype(f32)).astype(bf16)
                line.wait(going)
                self.terms = keep, recv, permute_by(going, "tensor", 2)
            else:
                total = lax.psum(keep + recv.astype(f32), "tensor", axis_index_groups=group)
                self.terms = total, jnp.zeros_like(recv), jnp.zeros_like(recv)
            return self.terms

    def own_of(first, second):
        return jnp.where(chip == 0, first, second)

    def own_rows(first, second):
        return lax.dynamic_slice_in_dim(
            own_of(first, second), (t % step) * local_rows, local_rows, 0
        )

    def own_sum(keep0, keep1, send0, send1):
        terms = [Exchange(k, s).go() for k, s in ((keep0, send0), (keep1, send1))]
        stay, near, far = (own_rows(a, b) for a, b in zip(*terms))
        return stay + near.astype(f32), far

    def own_terms(keep0, keep1, recv0, recv1):
        going, stay = call(
            own_body, "own", (struct(recv0.shape, bf16), struct(recv0.shape, f32)), line,
            keep0, keep1, recv0, recv1,
        )
        return stay, permute_by(going, "tensor", 2)

    rels_a, rels_b = rels_of(GATHER_A), rels_of(GATHER_B)
    packed_rows = jnp.concatenate([norm_gains, shifts], 0)
    packed_bias = jnp.concatenate(
        [self_bias.reshape(-1, HD // fsdp_size), cross_bias.reshape(-1, HD // fsdp_size), ff_bias],
        0,
    )
    if fast:
        extra = jnp.concatenate(
            [
                jnp.pad(packed_rows, ((0, 32 - packed_rows.shape[0]), (0, 0))),
                jnp.pad(packed_bias, ((0, 0), (0, 128 - packed_bias.shape[1]))),
            ],
            1,
        )

        def beside(out):
            return jnp.concatenate([out[:128], out[128:]], 1)

        packed = jnp.concatenate(
            [self_qkv.reshape(3 * 128, width), beside(self_out), extra], 0
        )
        self_w = Gather(line, packed, 256)
        (x_own, g_own), _ = lax.optimization_barrier(((layer_input, out_grad), self_w.got))
        packed = jnp.concatenate(
            [cross_qkv[1], cross_qkv[2], cross_qkv[0], beside(cross_out)], 0
        )
        tiles = hidden // 128
        packed_ff = jnp.concatenate(
            [
                ff_in.reshape(128, tiles, 128).transpose(1, 0, 2),
                ff_out.reshape(tiles, 128, 128),
            ],
            0,
        )
        self_w.second()
        x_rows = rows_of_all(x_own)
        cross_w = Gather(line, packed, 256, self_w.far)
        g_own, _ = lax.optimization_barrier((g_own, x_rows[2]))
        g_rows = rows_of_all(g_own)
        line.wait(self_w.far)
        tangled = encoder_states.reshape(2, frames, 8, 128).transpose(1, 2, 0, 3).reshape(-1, 128)
        line.away(tangled, *x_rows, *g_rows)
        e_seq = call(untangle_body, "untangle", (struct((frames, D), bf16),) * 2, line, tangled)
        self_w.third()
        cross_w.second(e_seq[0])
        ff_w = Gather(line, packed_ff, tiles, e_seq[0])
        line.wait(g_rows)
    else:
        x_rows = rows_of_all(layer_input)
        e_seq = [encoder_states[s] for s in range(2)]
        vec = lax.all_gather(packed_rows, "fsdp", axis=1, tiled=True).astype(f32)
        biases = lax.all_gather(packed_bias, "fsdp", axis=1, tiled=True).astype(f32)
        whole = lax.all_gather(self_qkv, "fsdp", axis=1, tiled=True)
        w_self = jnp.concatenate([whole[0], whole[1], whole[2]], 1)
        wo_self = lax.all_gather(self_out, "fsdp", axis=1, tiled=True)
        whole = lax.all_gather(cross_qkv, "fsdp", axis=1, tiled=True)
        w_cross, w_kv = whole[0], jnp.concatenate([whole[1], whole[2]], 1)
        wo_cross = lax.all_gather(cross_out, "fsdp", axis=1, tiled=True)
        w_in = lax.all_gather(ff_in, "fsdp", axis=0, tiled=True)
        w_out = lax.all_gather(ff_out, "fsdp", axis=1, tiled=True)
        bias = jnp.zeros((8, hidden), f32)
        bias = bias.at[:4, :width].set(biases[: 4 * heads].reshape(4, width))
        bias = bias.at[4].set(biases[4 * heads :].reshape(hidden))

    attn_flops = 8 * length * width * 1024
    row_pair = (struct((count, D), f32), struct((count, D), bf16))

    def self_forward(s):
        nonlocal w_self, wo_self, vec, bias
        outs = (
            struct((length, D), bf16),
            struct((length, 3 * width), bf16),
            struct((length, width), bf16),
            struct((length, heads), f32),
            *row_pair,
        )
        kwargs = dict(scratch=(pltpu.VMEM((length, D), bf16),),)
        if fast and s == 0:
            outs += (
                struct((D, 3 * width), bf16),
                struct((width, D), bf16),
                struct((16, D), f32),
                struct((8, D), f32),
            )
            *got, w_self, wo_self, vec, bias = call(
                functools.partial(self_forward_body, (rels_a, rels_b), s),
                "self_forward", outs, line, *x_rows, *self_w.pieces, **kwargs,
            )
        else:
            got = call(
                functools.partial(self_forward_body, None, s),
                "self_forward", outs, line, *x_rows, vec, bias, w_self, wo_self, **kwargs,
            )
        a1[s], qkv1[s], o1[s], lse1[s], *res = got
        sum1[s] = Exchange(*res)

    def frames_in(s):
        nonlocal w_kv
        outs = (struct((frames, width), bf16),) * 2
        flops = 4 * frames * D * width
        if fast and s == 0:
            k2[s], v2[s], w_kv = call(
                functools.partial(frames_body, rels_a),
                "frames_in", outs + (struct((D, 2 * width), bf16),), line, e_seq[s], bias,
                *cross_w.pieces[:3],
            )
        else:
            k2[s], v2[s] = call(
                functools.partial(frames_body, None),
                "frames_in", outs, line, e_seq[s], bias, w_kv,
            )

    def norm_of(rows, seq, base, terms, name):
        return call(
            functools.partial(norm_body, rows, seq),
            name, (struct((count, D), f32), struct((count, D), bf16)), line, *base, *terms, vec,
        )

    def norm_two(s):
        h1[s], mine = norm_of((4, 1, 5), s, x_rows[:2], sum1[s].terms, "norm_two")
        a2_rows[s] = mine, partner(mine)

    def cross_forward(s):
        nonlocal w_cross, wo_cross
        outs = (
            struct((length, D), bf16),
            struct((length, width), bf16),
            struct((length, width), bf16),
            struct((length, heads), f32),
            *row_pair,
        )
        args = (*a2_rows[s], bias, k2[s], v2[s])
        if fast and s == 0:
            *got, w_cross, wo_cross = call(
                functools.partial(cross_forward_body, rels_b), "cross_forward",
                outs + (struct((D, width), bf16), struct((width, D), bf16)),
                line, *args, *cross_w.pieces[3:],
            )
        else:
            got = call(
                functools.partial(cross_forward_body, None), "cross_forward",
                outs, line, *args, w_cross, wo_cross,
            )
        a2[s], q2[s], o2[s], lse2[s], *res = got
        sum2[s] = Exchange(*res)

    def norm_three(s):
        h2[s], mine = norm_of((6, 2, 7), None, (h1[s],), sum2[s].terms, "norm_three")
        a3_rows[s] = mine, partner(mine)

    def feed(s):
        nonlocal w_in, w_out
        outs = (
            struct((length, D), bf16),
            struct((length, D), bf16),
            struct((length, hidden), bf16),
            struct((length, hidden), bf16),
            struct((1, hidden), f32),
            *row_pair,
        )
        args = (*a3_rows[s], *g_rows, bias)
        flops = 6 * length * D * hidden
        if fast and s == 0:
            *got, w_in, w_out = call(
                functools.partial(feed_body, (rels_a, rels_b), s),
                "feed", outs + (struct((D, hidden), bf16), struct((hidden, D), bf16)), line,
                *args, *ff_w.pieces,
            )
        else:
            got = call(
                functools.partial(feed_body, None, s),
                "feed", outs, line, *args, w_in, w_out,
            )
        a3[s], g_full[s], act[s], du[s], ff_sums[s], *res = got
        sum3[s] = Exchange(*res)

    def feed_out():
        return call(
            feed_out_body, "feed_out",
            (*[row_pair[0]] * 2, *[row_pair[1]] * 2),
            line, act[0], act[1], w_out,
        )

    def norm_back(gain, base, terms, h, name):
        return call(
            functools.partial(norm_back_body, gain),
            name,
            (struct((count, D), f32), struct((count, D), bf16), struct((8, D), f32)),
            line, base, *terms, h, vec,
        )

    def norm_three_back(s):
        dh2[s], low, sums3[s] = norm_back(2, g_full[s], sum3[s].terms, h2[s], "norm_three_back")
        h2_rows[s] = low, partner(low)

    def cross_back(s):
        outs = (
            struct((length, D), bf16),
            struct((length, width), bf16),
            struct((frames, 2 * width), bf16),
            struct((2, width), f32),
            *row_pair,
        )
        h2_full[s], dq2[s], dkv2[s], cross_sums[s], *res = call(
            cross_back_body, "cross_back", outs, line,
            *h2_rows[s], q2[s], k2[s], v2[s], lse2[s], w_cross, wo_cross,
        )
        sum4[s] = Exchange(*res)

    def norm_two_back(s):
        dh1[s], low, sums2[s] = norm_back(1, dh2[s], sum4[s].terms, h1[s], "norm_two_back")
        h1_rows[s] = low, partner(low)

    def self_back(s):
        outs = (
            struct((length, D), bf16),
            struct((length, 3 * width), bf16),
            struct((2, width), f32),
            struct((2, D), f32),
            *row_pair,
        )
        h1_full[s], dqkv1[s], self_sums[s], vec_sums[s], *res5[s] = call(
            functools.partial(self_back_body, s), "self_back", outs, line,
            *h1_rows[s], qkv1[s], lse1[s], w_self, wo_self, *x_rows,
        )

    def weight_grad(terms, order, name, rider=None):
        operands, table, n = [], [], 0
        for lefts, rights, span in terms:
            low, high = span or (0, rights[0].shape[1])
            products = []
            for left, right in zip(lefts, rights):
                sides = [(left, None)] if not isinstance(left, tuple) else list(zip(left, (0, 1)))
                for part, side in sides:
                    products.append((len(operands), len(operands) + 1, side))
                    operands += [part, right]
            table.append((low, high, products))
            n += high - low
        part = struct((4, 128 + (0 if rider is None else rider.shape[1]), n), bf16)
        at = None
        if rider is not None:
            at = len(operands)
            operands.append(rider)
        got = call(
            functools.partial(weight_grad_body, order, table, at),
            name,
            (part, part),
            line,
            *operands,

            scratch=(pltpu.VMEM((2, 128, n), f32),),
        )
        return (*got, order)

    def plain_grad(lefts, rights):
        return sum(dot(a, b, TN) for a, b in zip(lefts, rights))

    def frame_grad():
        padded = -(-frames // 16) * 16
        keep, across, send = call(
            frame_grad_body, "frame_grad",
            (
                struct((2 * padded, D // 4), bf16),
                struct((2 * padded, D // 4), bf16),
                struct((4 * padded, D // 4), bf16),
            ),
            line, dkv2[0], dkv2[1], w_kv,
        )
        return keep, across, partner(send)

    def frame_go(keep, across, near):
        (going,) = call(
            frame_across_body, "frame_across", (struct(across.shape, bf16),), line, across, near
        )
        return keep, near, permute_by(going, "tensor", 2)

    (
        a1, qkv1, o1, lse1, sum1, h1, k2, v2, a2_rows, a2, q2, o2, lse2, sum2, h2, a3_rows, a3, g_full,
        act, du, ff_sums, sum3, dh2, sums3, h2_rows, h2_full, dq2, dkv2, cross_sums, sum4, dh1, sums2,
        h1_rows, h1_full, dqkv1, self_sums, vec_sums, res5,
    ) = ([None] * 2 for _ in range(38))
    rows_struct = (struct((local_rows, D), f32),)

    def output():
        pair = h2 if fast else [own_rows(*h2)] * 2
        return call(output_body, "output", rows_struct, line, *pair, *out_terms, vec, far=(0,))[0]

    def input_gradient():
        pair = dh1 if fast else [own_rows(*dh1)] * 2
        args = (*pair, *terms, layer_input, vec)
        return call(input_grad_body, "input_grad", rows_struct, line, *args, far=(0,))[0]

    if not fast:
        g_rows = rows_of_all(out_grad)
        for stage, sums in (
            (self_forward, sum1), (frames_in, None), (norm_two, None), (cross_forward, sum2), (norm_three, None),
            (feed, sum3), (norm_three_back, None), (cross_back, sum4), (norm_two_back, None), (self_back, None),
        ):
            for s in range(2):
                stage(s)
                if sums:
                    sums[s].go()
        out_terms = own_sum(*feed_out())
        terms = own_sum(res5[0][0], res5[1][0], res5[0][1], res5[1][1])
        layer_output, input_grad = output(), input_gradient()
    else:
        w_self = wo_self = w_kv = w_cross = wo_cross = w_in = w_out = vec = bias = None
        self_forward(0)
        self_forward(1)
        cross_w.third(a1[1])
        sum1[0].go()
        frames_in(0)
        sum1[1].go()
        ff_w.second(k2[0])
        norm_two(0)
        cross_forward(0)
        line.wait(ff_w.far)
        frames_in(1)
        norm_two(1)
        sum2[0].go()
        ff_w.third(o2[0])
        cross_forward(1)
        line.wait(ff_w.pieces)
        norm_three(0)
        sum2[1].go()
        feed(0)
        norm_three(1)
        sum3[0].go()
        feed(1)
        out_parts = feed_out()
        out_recv = partner(out_parts[2]), partner(out_parts[3])
        norm_three_back(0)
        sum3[1].go()
        (ff_parts,) = call(
            ff_grad_body, "ff_grad", (struct((D, 2 * hidden), bf16),), line,
            *a3, *du, *g_full, *act, far=(0,),
        )
        ff_total = lax.psum_scatter(ff_parts, "fsdp", scatter_dimension=0, tiled=True)
        out_terms = own_terms(*out_parts[:2], *out_recv)
        cross_back(0)
        norm_three_back(1)
        sum4[0].go()
        cross_back(1)
        norm_two_back(0)
        sum4[1].go()
        frame_terms = frame_grad()
        frame_terms = frame_go(*frame_terms)
        self_back(0)
        end0 = partner(res5[0][1])
        norm_two_back(1)
        line.wait(out_terms[1])
        layer_output = output()
        cross_sum = Sum(
            line,
            weight_grad([(e_seq, dkv2, None), (a2, dq2, (0, width // 2))], SUM_A, "cross_grad"),
            weight_grad(
                [
                    (a2, dq2, (width // 2, width)),
                    (h2_full, o2, None),
                    ((h1_full[0], h1_rows[1]), o1, None),
                ],
                SUM_B,
                "cross_grad_b",
            ),
        )
        self_back(1)
        end1 = partner(res5[1][1])
        split = 3 * width // 2
        self_parts = weight_grad([(a1, dqkv1, (0, split))], SUM_A, "self_grad")
        (small,) = call(
            small_body, "small", (struct((8, 32, split), bf16),), line,
            *vec_sums, *sums2, *sums3, *self_sums, *cross_sums, *ff_sums,
            scratch=(pltpu.VMEM((32, D), f32),),
        )
        self_sum = Sum(
            line,
            self_parts,
            weight_grad([(a1, dqkv1, (split, 3 * width))], SUM_B, "self_grad_b", small),
        )
        cross_sum.step()
        terms = own_terms(res5[0][0], res5[1][0], end0, end1)
        self_sum.step()
        cross_sum.step()
        input_grad = input_gradient()
        self_sum.step()
        tiles = D // 4 // 128
        (rows,) = call(
            frame_sum_body, "frame_sum", (struct((frames * 2 * tiles, 128), f32),), line, *frame_terms, far=(0,),
        )
        ff_in_grad, ff_out_grad = call(
            ff_end_body, "ff_end", (struct((128, hidden), f32), struct((hidden, 128), f32)), line,
            ff_total, far=(0, 1),
        )
        vectors, self_qkv_grad, self_bias_grad, cross_bias_grad, ff_bias_grad = self_sum.end(
            self_end_body,
            "self_end",
            (
                struct((16, 128), f32),
                struct((3, 128, width), f32),
                struct((2, heads, 8), f32),
                struct((2, heads, 8), f32),
                struct((hidden // HD, 8), f32),
            ),
        )
        vectors = vectors + permute_by(vectors, "tensor", 1)
        vectors = vectors + permute_by(vectors, "tensor", 2)

    if fast:
        cross_qkv_grad, cross_out_grad, self_out_grad = cross_sum.end(
            cross_end_body,
            "cross_end",
            (
                struct((3, 128, width), f32),
                struct((width, 128), f32),
                struct((width, 128), f32),
            ),
        )
        encoder_grad = (
            rows.reshape(frames, tiles, 2, 128).transpose(2, 0, 1, 3).reshape(2, frames, D // 4)
        )
        gains_grad, shifts_grad = call(
            vectors_body, "vectors", (struct((3, 32), f32), struct((6, 32), f32)), line, vectors,
            far=(0, 1),
        )
    else:
        part = jnp.stack([dot(dkv2[s], w_kv, NT) for s in range(2)])
        encoder_grad = lax.psum_scatter(part, "tensor", scatter_dimension=2, tiled=True)

        def scattered(part, dimension):
            return lax.psum_scatter(part, "fsdp", scatter_dimension=dimension, tiled=True)

        counts = (t % step) == 0

        def vector(sums, row):
            return jnp.where(counts, own_of(sums[0][row], sums[1][row]), 0.0)

        vectors = jnp.stack(
            [
                vec_sums[0][0] + vec_sums[1][0],
                vector(sums2, 0),
                vector(sums3, 0),
                vec_sums[0][1] + vec_sums[1][1],
                vector(sums2, 2),
                vector(sums2, 1),
                vector(sums3, 2),
                vector(sums3, 1),
                vector(sums3, 3),
            ]
        )
        bias_sums = jnp.concatenate(
            [
                self_sums[0] + self_sums[1],
                cross_sums[0] + cross_sums[1],
                (ff_sums[0] + ff_sums[1]).reshape(-1, width),
            ],
            0,
        ).reshape(-1, HD)
        vectors = scattered(vectors, 1)
        vectors = lax.psum_scatter(vectors, "tensor", scatter_dimension=1, tiled=True)
        bias_sums = scattered(bias_sums, 1)
        ff_in_grad = scattered(plain_grad(a3, du), 0)
        ff_out_grad = scattered(plain_grad(act, g_full), 1)
        cross_out_grad = scattered(plain_grad(o2, h2_full), 1)
        kv_grad = plain_grad(e_seq, dkv2)
        cross_qkv_grad = scattered(
            jnp.stack([plain_grad(a2, dq2), kv_grad[:, :width], kv_grad[:, width:]]), 1
        )
        self_out_grad = scattered(plain_grad(o1, h1_full), 1)
        qkv_grad = scattered(plain_grad(a1, dqkv1), 0)
        self_qkv_grad = jnp.stack([qkv_grad[:, i * width : (i + 1) * width] for i in range(3)])
        piece = HD // fsdp_size
        self_bias_grad = bias_sums[: 2 * heads].reshape(2, heads, piece)
        cross_bias_grad = bias_sums[2 * heads : 4 * heads].reshape(2, heads, piece)
        ff_bias_grad = bias_sums[4 * heads :]
        gains_grad, shifts_grad = vectors[:3], vectors[3:]
    return (
        layer_output,
        input_grad,
        encoder_grad,
        self_qkv_grad,
        self_bias_grad,
        self_out_grad,
        cross_qkv_grad,
        cross_bias_grad,
        cross_out_grad,
        ff_in_grad,
        ff_bias_grad,
        ff_out_grad,
        gains_grad,
        shifts_grad,
    )


def solution(mesh):
    fast = mesh.shape["fsdp"] == 8 and mesh.shape["tensor"] == 4
    return jax.shard_map(
        functools.partial(shards, fast),
        mesh=mesh,
        in_specs=(
            P(("fsdp", "tensor"), None),
            P("fsdp", None, None),
            P(("fsdp", "tensor"), None),
            P(None, "fsdp", "tensor"),
            P(None, "tensor", "fsdp"),
            P("tensor", "fsdp"),
            P(None, "fsdp", "tensor"),
            P(None, "tensor", "fsdp"),
            P("tensor", "fsdp"),
            P("fsdp", "tensor"),
            P("tensor", "fsdp"),
            P("tensor", "fsdp"),
            P(None, "fsdp"),
            P(None, "fsdp"),
        ),
        out_specs=(
            P(("fsdp", "tensor"), None),
            P(("fsdp", "tensor"), None),
            P("fsdp", None, "tensor"),
            P(None, "fsdp", "tensor"),
            P(None, "tensor", "fsdp"),
            P("tensor", "fsdp"),
            P(None, "fsdp", "tensor"),
            P(None, "tensor", "fsdp"),
            P("tensor", "fsdp"),
            P("fsdp", "tensor"),
            P("tensor", "fsdp"),
            P("tensor", "fsdp"),
            P(None, ("fsdp", "tensor")),
            P(None, ("fsdp", "tensor")),
        ),
        check_vma=False,
    )
```
